128 devices in a mesh: lat: 32 (over z, y_hi, x), lon: 4 (over y_lo, core).
Axes of the slice: x: 4, y: 4 (y_hi: 2, y_lo: 2; y = y_hi * 2 + y_lo), z: 4, core: 2. Of those that a mesh axis runs over, the one named last changes fastest.
Arguments:
- level_tokens: bfloat16 [256, 64, 13, 1024], P(('lat', 'lon')), may hold values from -24 to 24
- latent_query: bfloat16 [3, 1024], replicated, may hold values from -6 to 6
- key_weight: bfloat16 [1024, 1024], replicated, may hold values from -0.1875 to 0.1875
- value_weight: bfloat16 [1024, 1024], replicated, may hold values from -0.1875 to 0.1875
- resample_out: bfloat16 [1024, 1024], replicated, may hold values from -0.1875 to 0.1875
- norm_gain: float32 [2, 1024], replicated, may hold values from 0.5 to 1.5
- qkv_weight: bfloat16 [2, 1024, 3, 1024], P(None, 'lat', None, 'lon'), may hold values from -0.1875 to 0.1875
- out_weight: bfloat16 [2, 1024, 1024], P(None, 'lat', 'lon'), may hold values from -0.1875 to 0.1875
- window_label: int32 [256, 64], P('lat', 'lon'), may hold values from 0 to 3
- grad_latents: bfloat16 [256, 64, 3, 1024], P(('lat', 'lon')), may hold values from -6 to 6
Outputs:
- backbone_out: bfloat16 [256, 64, 3, 1024], P('lat', 'lon')
- grad_key_weight: float32 [1024, 1024], P(('lat', 'lon'))
- grad_value_weight: float32 [1024, 1024], P(('lat', 'lon'))
- grad_out_weight: float32 [1024, 1024], P(('lat', 'lon'))
The draws below stay inside these ranges and needn't reach their ends.
All inputs are finite; a program needn't handle non-finite values.
Results may differ from the reference program's by a relative error of at most 0.013.
Values may be sent and summed in bfloat16 or wider, within the bound.
A program may use at most 192 MiB of HBM per device.

```python
import jax
import jax.numpy as jnp
from jax import lax

D = 1024
HEADS = 16
LEV = 13
LATENT = 3
NLAT = 256
NLON = 64


def plant(entries, own_key, low, high):
    longest = entries.shape.index(max(entries.shape))
    spots = []
    for shift in (0, 1):
        where = [jax.random.randint(jax.random.fold_in(own_key, axis), (), 0, length) for axis, length in enumerate(entries.shape)]
        where[longest] = (where[longest] + shift) % entries.shape[longest]
        spots.append(tuple(where))
    return entries.at[spots[0]].set(low).at[spots[1]].set(high)


def spiked(result, rng, source, target, shards_of, factor):
    def block_of(dim):
        return (jnp.arange(result.shape[dim]) // (result.shape[dim] // shards_of)).reshape((-1,) + (1,) * (result.ndim - 1 - dim))

    one_side = jax.random.permutation(rng, shards_of)[block_of(target)]
    other_side = (block_of(target) + shards_of // 2) % shards_of
    return jnp.where((block_of(source) == one_side) | (block_of(source) == other_side), factor * result, result)


def shard_levels(own_key, dims, split, least, high):
    level, own = 1.0, jax.random.fold_in(own_key, 6)
    for position, blocks in split:
        steps = jnp.exp(jax.random.uniform(jax.random.fold_in(own, position), (blocks,), jnp.float32, least / len(split), high / len(split)))
        level = level * jnp.repeat(steps, dims[position] // blocks).reshape([-1 if axis == position else 1 for axis in range(len(dims))])
    return level


def bell_draw(own_key, shape, scale, reach, split=(), dtype=jnp.bfloat16):
    array = scale * jax.random.normal(own_key, shape, jnp.float32)
    if split:
        array = array * shard_levels(own_key, shape, split, -0.22, 0.18)
    return jnp.clip(array, -reach, reach).astype(dtype)


def noise_with(own_key, dims, scale, limit, cuts, heavy, held_as=jnp.bfloat16):
    drawn = scale * jax.random.normal(own_key, dims, jnp.float32)
    if cuts:
        drawn = drawn * shard_levels(own_key, dims, cuts, -0.22, 0.18)
    return jnp.clip(spiked(drawn, jax.random.fold_in(own_key, 3), *heavy), -limit, limit).astype(held_as)


def setup_inputs(seed: int = 0) -> dict:
    streams_of = jax.random.split(jax.random.key(seed), 11)
    level_tokens = noise_with(streams_of[0], (NLAT, NLON, LEV, D), 1.0, 24.0, ((0, 128),), (0, 3, 128, 5.5))
    latent_query = bell_draw(streams_of[1], (LATENT, D), 1.0, 6.0)
    key_weight = bell_draw(streams_of[2], (D, D), D ** -0.5, 0.1875)
    value_weight = bell_draw(streams_of[3], (D, D), D ** -0.5, 0.1875)
    resample_out = bell_draw(streams_of[4], (D, D), D ** -0.5, 0.1875)
    norm_gain = jnp.clip(1.0 + 0.1 * jax.random.normal(streams_of[5], (2, D), jnp.float32), 0.5, 1.5)
    qkv_weight = bell_draw(streams_of[6], (2, D, 3, D), D ** -0.5, 0.1875, ((1, 32), (3, 4)))
    out_weight = bell_draw(streams_of[7], (2, D, D), D ** -0.5, 0.1875, ((1, 32), (2, 4)))
    window_label = plant(jax.random.randint(streams_of[8], (NLAT, NLON), 0, 4), jax.random.fold_in(streams_of[8], 1), 0, 3).astype(jnp.int32)
    grad_latents = bell_draw(streams_of[9], (NLAT, NLON, LATENT, D), 1.0, 6.0, ((0, 128),))
    return dict(level_tokens=level_tokens, latent_query=latent_query, key_weight=key_weight, value_weight=value_weight, resample_out=resample_out, norm_gain=norm_gain, qkv_weight=qkv_weight, out_weight=out_weight, window_label=window_label, grad_latents=grad_latents)


def layer_norm(stream, norm_scale):
    values = stream.astype(jnp.float32)
    centre = lax.optimization_barrier(jnp.mean(values, axis=-1, keepdims=True))
    centred = values - centre
    spread = lax.optimization_barrier(jnp.mean(centred * centred, axis=-1, keepdims=True))
    return (centred * lax.rsqrt(spread + 1e-05) * norm_scale).astype(jnp.bfloat16)

def to_windows(stream):
    tile_rows, tile_cols, levels = (stream.shape[0], stream.shape[1], stream.shape[2])
    trailing = stream.shape[3:]
    window_grid = stream.reshape((tile_rows // 4, 4, tile_cols // 8, 8, levels) + trailing)
    window_grid = jnp.swapaxes(window_grid, 1, 2)
    return window_grid.reshape((tile_rows // 4 * (tile_cols // 8), 32 * levels) + trailing)

def from_windows(windowed, tile_rows, tile_cols):
    levels = windowed.shape[1] // 32
    trailing = windowed.shape[2:]
    window_grid = windowed.reshape((tile_rows // 4, tile_cols // 8, 4, 8, levels) + trailing)
    window_grid = jnp.swapaxes(window_grid, 1, 2)
    return window_grid.reshape((tile_rows, tile_cols, levels) + trailing)

def window_attend(projected, window_codes):
    head_size = projected.shape[-1]
    queries = projected[:, :, 0].astype(jnp.float32)
    key_part = projected[:, :, 1].astype(jnp.float32)
    value_part = projected[:, :, 2].astype(jnp.float32)
    logits = jnp.einsum('wqhe,wkhe->whqk', queries, key_part) * head_size ** (-0.5)
    allowed = window_codes[:, None, :, None] == window_codes[:, None, None, :]
    logits = jnp.where(allowed, logits, -1e+30)
    weights = jax.nn.softmax(logits, axis=-1).astype(jnp.bfloat16)
    attended = jnp.einsum('whqk,wkhe->wqhe', weights.astype(jnp.float32), value_part)
    return attended.astype(jnp.bfloat16).reshape(projected.shape[0], projected.shape[1], -1)

def sublayer(stream, token_codes, qkv_layer, out_layer, norm_scale):
    normed = to_windows(layer_norm(stream, norm_scale))
    window_codes = to_windows(token_codes)
    window_total = normed.shape[0]
    window_group = NLON // 8
    flat_weight = qkv_layer.reshape(D, 3 * D)

    def attend_block(operands):
        window_block, block_codes = operands
        projected = jnp.dot(window_block.reshape(-1, D), flat_weight, preferred_element_type=jnp.float32)
        projected = projected.astype(jnp.bfloat16).reshape(window_block.shape[0], window_block.shape[1], 3, HEADS, D // HEADS)
        attended = window_attend(projected, block_codes)
        update = jnp.dot(attended.reshape(-1, D), out_layer, preferred_element_type=jnp.float32)
        return update.reshape(window_block.shape[0], window_block.shape[1], D)
    update = lax.map(attend_block, (normed.reshape(window_total // window_group, window_group, normed.shape[1], D), window_codes.reshape(window_total // window_group, window_group, -1)))
    update = from_windows(update.reshape(window_total, -1, D), NLAT, NLON)
    return (stream.astype(jnp.float32) + update).astype(jnp.bfloat16)

def reference(level_tokens, latent_query, key_weight, value_weight, resample_out, norm_gain, qkv_weight, out_weight, window_label, grad_latents):
    head_size = D // HEADS
    score_scale = head_size ** (-0.5)
    query_heads = latent_query.astype(jnp.float32).reshape(LATENT, HEADS, head_size)

    def row_step(running, operands):
        row_tokens, grad_row = operands
        patch_count = row_tokens.shape[0]
        flat_tokens = row_tokens.reshape(-1, D)
        level_keys = jnp.dot(flat_tokens, key_weight, preferred_element_type=jnp.float32).astype(jnp.bfloat16)
        level_values = jnp.dot(flat_tokens, value_weight, preferred_element_type=jnp.float32).astype(jnp.bfloat16)
        key_heads = level_keys.reshape(patch_count, LEV, HEADS, head_size).astype(jnp.float32)
        value_heads = level_values.reshape(patch_count, LEV, HEADS, head_size).astype(jnp.float32)
        logits = jnp.einsum('qhe,plhe->phql', query_heads, key_heads) * score_scale
        level_probs = jax.nn.softmax(logits, axis=-1)
        level_weights = level_probs.astype(jnp.bfloat16)
        attended = jnp.einsum('phql,plhe->pqhe', level_weights.astype(jnp.float32), value_heads).astype(jnp.bfloat16)
        attended_flat = attended.reshape(-1, D)
        latents = jnp.dot(attended_flat, resample_out, preferred_element_type=jnp.float32).reshape(patch_count, LATENT, D)
        latents = (latents + latent_query.astype(jnp.float32)[None]).astype(jnp.bfloat16)
        grad_flat = grad_row.reshape(-1, D)
        grad_key, grad_value, grad_out = running
        grad_out = grad_out + jnp.dot(attended_flat.T, grad_flat, preferred_element_type=jnp.float32)
        d_attended = jnp.dot(grad_flat, resample_out.T, preferred_element_type=jnp.float32).astype(jnp.bfloat16)
        d_attended = d_attended.reshape(patch_count, LATENT, HEADS, head_size).astype(jnp.float32)
        d_weights = jnp.einsum('pqhe,plhe->phql', d_attended, value_heads)
        d_logits = level_probs * (d_weights - lax.optimization_barrier(jnp.sum(level_probs * d_weights, axis=-1, keepdims=True)))
        d_values = jnp.einsum('phql,pqhe->plhe', level_weights.astype(jnp.float32), d_attended).astype(jnp.bfloat16).reshape(-1, D)
        d_keys = (jnp.einsum('phql,qhe->plhe', d_logits, query_heads) * score_scale).astype(jnp.bfloat16).reshape(-1, D)
        grad_key = grad_key + jnp.dot(flat_tokens.T, d_keys, preferred_element_type=jnp.float32)
        grad_value = grad_value + jnp.dot(flat_tokens.T, d_values, preferred_element_type=jnp.float32)
        return ((grad_key, grad_value, grad_out), latents)
    empty_sum = jnp.zeros((D, D), jnp.float32)
    grads, latents = lax.scan(row_step, (empty_sum, empty_sum, empty_sum), (level_tokens, grad_latents))
    factor = (NLAT * NLON) ** (-0.5)
    plain = jnp.zeros((NLAT, NLON, LATENT), jnp.float32)
    middle = sublayer(latents, plain, qkv_weight[0], out_weight[0], norm_gain[0])
    rolled = jnp.roll(middle, (-2, -4), axis=(0, 1))
    wrapped = (jnp.arange(NLAT) >= NLAT - 2).astype(jnp.int32)
    token_codes = (window_label * 2 + wrapped[:, None]).astype(jnp.float32)
    token_codes = jnp.broadcast_to(token_codes[:, :, None], (NLAT, NLON, LATENT))
    backbone_out = sublayer(rolled, token_codes, qkv_weight[1], out_weight[1], norm_gain[1])
    return (backbone_out, grads[0] * factor, grads[1] * factor, grads[2] * factor)
```

```python
import functools

import jax
import jax.numpy as jnp
from jax import lax
from jax.experimental import pallas as pl
from jax.experimental.pallas import tpu as pltpu
from jax.sharding import PartitionSpec as P

MESH = pl.DeviceIdType.MESH
F32, BF16 = jnp.float32, jnp.bfloat16
D = 1024
HEADS = 16
LEV = 13
LATENT = 3
GROUPS = 8
MIB = 1024 * 1024
PACK = 512
ORDERS = (("x", "y", "z"), ("y", "z", "x"), ("z", "x", "y"))


def dot(a, b, dims=((1,), (0,))):
    return lax.dot_general(a, b, (dims, ((), ())), preferred_element_type=F32)


def my_place():
    lat, lon = lax.axis_index("lat"), lax.axis_index("lon")
    return {
        "z": lat // 8,
        "y": ((lat // 4) % 2) * 2 + lon // 2,
        "x": lat % 4,
        "core": lon % 2,
    }


def device_of(place):
    lat = place["z"] * 8 + (place["y"] // 2) * 4 + place["x"]
    return (lat, (place["y"] % 2) * 2 + place["core"])


def moved(place, dim, delta):
    size = 2 if dim == "core" else 4
    other = dict(place)
    other[dim] = (place[dim] + delta + size) % size
    return device_of(other)


def pick(dim, value):
    if dim == "y":
        if value is None:
            return {"yh": slice(None), "yl": slice(None)}
        return {"yh": pl.ds(value // 2, 1), "yl": pl.ds(value % 2, 1)}
    return {dim: slice(None) if value is None else pl.ds(value, 1)}


def greet(place):
    barrier = pltpu.get_barrier_semaphore()
    others = [moved(place, dim, step) for dim in "xyz" for step in (1, -1)] + [moved(place, "core", 1)]
    for other in others:
        pl.semaphore_signal(barrier, inc=1, device_id=other, device_id_type=MESH)
    pl.semaphore_wait(barrier, len(others))


class Gather:
    def __init__(self, place, w, send, recv, block, order):
        self.place, self.w, self.send, self.recv = place, w, send, recv
        self.block, self.order = block, order

    def region(self, phase, value, half=None, core=None):
        index = {}
        for position, dim in enumerate(self.order):
            if position < phase:
                index.update(pick(dim, None))
            elif position == phase:
                index.update(pick(dim, value))
            else:
                index.update(pick(dim, self.place[dim]))
        rows = slice(None) if half is None else pl.ds(16 * half, 16)
        core = self.place["core"] if core is None else core
        return self.w.at[self.block, index["yl"], core, index["z"], index["yh"], index["x"], rows, :]

    def copy(self, k, ref, other):
        return pltpu.make_async_remote_copy(
            src_ref=ref,
            dst_ref=ref,
            send_sem=self.send.at[self.block, k],
            recv_sem=self.recv.at[self.block, k],
            device_id=other,
            device_id_type=MESH,
        )

    def ring(self, phase, k):
        dim = self.order[phase]
        me = self.place[dim]
        ahead, behind = moved(self.place, dim, 1), moved(self.place, dim, -1)
        if k == 0:
            return self.copy(4 * phase, self.region(phase, me), ahead)
        if k == 1:
            return self.copy(4 * phase + 1, self.region(phase, me), behind)
        if k == 2:
            return self.copy(4 * phase + 2, self.region(phase, (me + 3) % 4, 0), ahead)
        return self.copy(4 * phase + 3, self.region(phase, (me + 1) % 4, 1), behind)

    def arrival(self, phase, k):
        dim = self.order[phase]
        me = self.place[dim]
        other = moved(self.place, dim, -1 if k % 2 == 0 else 1)
        ref = (
            self.region(phase, (me + 3) % 4),
            self.region(phase, (me + 1) % 4),
            self.region(phase, (me + 2) % 4, 0),
            self.region(phase, (me + 2) % 4, 1),
        )[k]
        return self.copy(4 * phase + k, ref, other)

    def across(self, core):
        ref = self.w.at[self.block, :, core]
        return self.copy(12, ref, moved(self.place, "core", 1))

    def step(self, s):
        phase, part = divmod(s, 2)
        if part == 0:
            if phase > 0:
                self.arrival(phase - 1, 2).wait_recv()
                self.arrival(phase - 1, 3).wait_recv()
            if phase < 3:
                self.ring(phase, 0).start()
                self.ring(phase, 1).start()
            else:
                self.across(self.place["core"]).start()
        elif phase < 3:
            self.arrival(phase, 0).wait_recv()
            self.ring(phase, 2).start()
            self.arrival(phase, 1).wait_recv()
            self.ring(phase, 3).start()
        else:
            self.across(1 - self.place["core"]).wait_recv()

    def drain(self):
        for phase in range(3):
            for k in range(4):
                self.ring(phase, k).wait_send()
        self.across(self.place["core"]).wait_send()


GATHER_STEPS = 8


def gather_kernel(shard, w, send, recv, own):
    place = my_place()
    lat_y = place["y"]
    copy = pltpu.make_async_copy(
        shard, w.at[:, lat_y % 2, place["core"], place["z"], lat_y // 2, place["x"]], own
    )
    copy.start()
    greet(place)
    copy.wait()
    parts = [Gather(place, w, send, recv, b, ORDERS[b % 3]) for b in range(8)]
    for s in range(GATHER_STEPS):
        for part in parts:
            part.step(s)
    for part in parts:
        part.drain()


def gather(shard):
    return pl.pallas_call(
        gather_kernel,
        out_shape=jax.ShapeDtypeStruct((8, 2, 2, 4, 2, 4, 32, 256), BF16),
        in_specs=[pl.BlockSpec(memory_space=pl.ANY)],
        out_specs=pl.BlockSpec(memory_space=pl.ANY),
        scratch_shapes=[
            pltpu.SemaphoreType.DMA((8, 13)),
            pltpu.SemaphoreType.DMA((8, 13)),
            pltpu.SemaphoreType.DMA,
        ],
        compiler_params=pltpu.CompilerParams(collective_id=0, has_side_effects=True),
    )(shard)


def landing_shape(order, phase, columns):
    sizes = {"z": 4, "yh": 2, "x": 4, "yl": 2}
    for dim in order[: phase + 1]:
        for name in ("yh", "yl") if dim == "y" else (dim,):
            sizes[name] = 1
    return (sizes["z"], sizes["yh"], sizes["x"], sizes["yl"], 16, columns)


class Reduce:
    def __init__(self, place, p, landing, send, recv, order):
        self.place, self.p, self.landing = place, p, landing
        self.send, self.recv, self.order = send, recv, order

    def region(self, phase, value, part):
        index = {}
        for position, dim in enumerate(self.order):
            if position < phase:
                index.update(pick(dim, self.place[dim]))
            elif position == phase:
                index.update(pick(dim, value))
            else:
                index.update(pick(dim, None))
        columns = {None: slice(None), 0: pl.ds(0, 256), 1: pl.ds(256, self.p.shape[-1] - 256)}[part]
        return (self.place["core"], index["z"], index["yh"], index["x"], index["yl"], slice(None), columns)

    def copy(self, k, src, dst, other):
        return pltpu.make_async_remote_copy(
            src_ref=src,
            dst_ref=dst,
            send_sem=self.send.at[k],
            recv_sem=self.recv.at[k],
            device_id=other,
            device_id_type=MESH,
        )

    def across(self):
        return self.copy(12, self.p.at[1 - self.place["core"]], self.landing[12], moved(self.place, "core", 1))

    def ring(self, phase, k):
        dim = self.order[phase]
        me = self.place[dim]
        target = ((me + 2) % 4, (me + 2) % 4, (me + 1) % 4, (me + 3) % 4)[k]
        part = (0, 1, None, None)[k]
        other = moved(self.place, dim, 1 if k % 2 == 0 else -1)
        return self.copy(4 * phase + k, self.p.at[self.region(phase, target, part)], self.landing[4 * phase + k], other)

    def add(self, region, *landed):
        total = self.p[region].astype(F32)
        for ref in landed:
            total = total + ref[...].astype(F32)
        self.p[region] = total.astype(BF16)

    def step(self, s):
        if s == 0:
            self.across().start()
            return
        phase, part = divmod(s - 1, 2)
        land = self.landing
        if part == 0:
            if phase == 0:
                self.across().wait_recv()
                core = self.place["core"]
                for z in range(4):
                    self.p[core, z] = (self.p[core, z].astype(F32) + land[12][z].astype(F32)).astype(BF16)
            else:
                self.ring(phase - 1, 2).wait_recv()
                self.ring(phase - 1, 3).wait_recv()
                me = self.place[self.order[phase - 1]]
                self.add(self.region(phase - 1, me, None), land[4 * phase - 2], land[4 * phase - 1])
            if phase < 3:
                self.ring(phase, 0).start()
                self.ring(phase, 1).start()
        else:
            me = self.place[self.order[phase]]
            self.ring(phase, 0).wait_recv()
            self.add(self.region(phase, (me + 1) % 4, 0), land[4 * phase])
            self.ring(phase, 2).start()
            self.ring(phase, 1).wait_recv()
            self.add(self.region(phase, (me + 3) % 4, 1), land[4 * phase + 1])
            self.ring(phase, 3).start()

    def drain(self):
        for phase in range(3):
            for k in range(4):
                self.ring(phase, k).wait_send()
        self.across().wait_send()

    def result(self):
        y = self.place["y"]
        return self.p[self.place["core"], self.place["z"], y // 2, self.place["x"], y % 2].astype(F32)


REDUCE_STEPS = 8


def landing_shapes(order, columns):
    shapes = []
    for phase in range(3):
        for part in (256, columns - 256, columns, columns):
            shapes.append(pltpu.VMEM(landing_shape(order, phase, part), BF16))
    shapes.append(pltpu.VMEM((4, 2, 4, 2, 16, columns), BF16))
    return shapes


def unpacked(rows):
    return jnp.concatenate([rows[:8, :PACK], rows[8:, :PACK]], axis=1)


def spread_queries(lq):
    row = lax.broadcasted_iota(jnp.int32, (128, D), 0)
    head = lax.broadcasted_iota(jnp.int32, (128, D), 1) // 64
    total = jnp.zeros((128, D), F32)
    for q in range(LATENT):
        total = total + jnp.where(row == q * HEADS + head, lq[q : q + 1, :].astype(F32), 0.0)
    return total.astype(BF16)


def finish_gradients(factor, value_rows, out_rows, lq, grad_key, grad_value, grad_out):
    grad_value[...] = unpacked(value_rows) * factor
    grad_out[...] = unpacked(out_rows) * factor
    small = value_rows[:8, PACK:] * (factor * 0.125)
    high = small.astype(BF16)
    low = (small - high.astype(F32)).astype(BF16)
    queries = spread_queries(lq)
    grad_key[...] = dot(high, queries) + dot(low, queries)


def reduce_kernel(factor, pv_in, po_in, lq, grad_key, grad_value, grad_out, pv, po, send, recv, own, *landing):
    place = my_place()
    copies = [
        pltpu.make_async_copy(pv_in, pv, own.at[0]),
        pltpu.make_async_copy(po_in, po, own.at[1]),
    ]
    for copy in copies:
        copy.start()
    greet(place)
    for copy in copies:
        copy.wait()
    parts = [
        Reduce(place, pv, landing[:13], send.at[0], recv.at[0], ORDERS[0]),
        Reduce(place, po, landing[13:], send.at[1], recv.at[1], ORDERS[1]),
    ]
    for s in range(REDUCE_STEPS):
        for part in parts:
            part.step(s)
    for part in parts:
        part.drain()
    finish_gradients(factor, parts[0].result(), parts[1].result(), lq, grad_key, grad_value, grad_out)


def reduce_gradients(factor, pv, po, lq):
    vmem = pl.BlockSpec(memory_space=pltpu.VMEM)
    anywhere = pl.BlockSpec(memory_space=pl.ANY)
    return pl.pallas_call(
        functools.partial(reduce_kernel, factor),
        out_shape=[jax.ShapeDtypeStruct((8, D), F32)] * 3,
        in_specs=[anywhere, anywhere, vmem],
        out_specs=[vmem] * 3,
        scratch_shapes=[
            pltpu.VMEM(pv.shape, BF16),
            pltpu.VMEM(po.shape, BF16),
            pltpu.SemaphoreType.DMA((2, 13)),
            pltpu.SemaphoreType.DMA((2, 13)),
            pltpu.SemaphoreType.DMA((2,)),
        ]
        + landing_shapes(ORDERS[0], pv.shape[-1])
        + landing_shapes(ORDERS[1], po.shape[-1]),
        compiler_params=pltpu.CompilerParams(
            collective_id=1, has_side_effects=True, vmem_limit_bytes=48 * MIB
        ),
    )(pv, po, lq)


def resample_project(tok, kw, vw, lq, spread, values, logits):
    row = lax.broadcasted_iota(jnp.int32, (128, 768), 0)
    column = lax.broadcasted_iota(jnp.int32, (128, 768), 1)
    for cb in range(4):
        hit = row == (column // 256) * HEADS + cb * 4 + (column % 256) // 64
        spread[cb] = jnp.where(hit, 1.0, 0.0).astype(BF16)
    kq = dot(kw[...], spread_queries(lq), ((1,), (1,))) * 0.125
    high = kq.astype(BF16)
    low = (kq - high.astype(F32)).astype(BF16)

    def project(pair, _):
        rows = tok[pl.ds(pair * 2, 2)].reshape(416, D)
        for nb in range(4):
            part = dot(rows, vw[:, nb * 256 : (nb + 1) * 256]).astype(BF16)
            values[pl.ds(pair * 2, 2), :, nb * 256 : (nb + 1) * 256] = part.reshape(2, 208, 256)
        logits[pl.ds(pair * 2, 2)] = (dot(rows, high) + dot(rows, low)).reshape(2, 208, 128)
        return 0

    lax.fori_loop(0, GROUPS // 2, project, 0)


def resample_softmax(logits, weights):
    def group(g, _):
        x = logits[g].reshape(LEV, 16, 128)
        x = jnp.exp(x - jnp.max(x, axis=0, keepdims=True))
        x = x / jnp.sum(x, axis=0, keepdims=True)
        logits[g] = x.reshape(208, 128)
        weights[g] = x.astype(BF16).reshape(208, 128)
        return 0

    lax.fori_loop(0, GROUPS, group, 0)


def times_transposed(rows, ro, out):
    for nb in range(4):
        part = dot(rows[...].reshape(384, D), ro[nb * 256 : (nb + 1) * 256, :], ((1,), (1,)))
        out[:, :, nb * 256 : (nb + 1) * 256] = part.astype(BF16).reshape(GROUPS, 48, 256)


def resample_mix(values, weights, probs, spread, d_attended, attended, d_values, d_logits):
    def group(g, _):
        w = weights[g]
        d_weights = jnp.zeros((208, 128), F32)
        for cb in range(4):
            columns = slice(cb * 256, (cb + 1) * 256)
            wide = dot(w, spread[cb])
            v = values[g, :, columns].astype(F32).reshape(LEV, 16, 256)
            d_v = jnp.zeros((LEV, 16, 256), F32)
            products = []
            for q in range(LATENT):
                wq = wide[:, q * 256 : (q + 1) * 256].reshape(LEV, 16, 256)
                da = d_attended[g, q * 16 : (q + 1) * 16, columns].astype(F32)[None]
                attended[g, q * 16 : (q + 1) * 16, columns] = jnp.sum(wq * v, axis=0).astype(BF16)
                d_v = d_v + wq * da
                products.append((v * da).astype(BF16).reshape(208, 256))
            d_values[g, :, columns] = d_v.astype(BF16).reshape(208, 256)
            d_weights = d_weights + dot(jnp.concatenate(products, axis=1), spread[cb], ((1,), (1,)))
        p = probs[g].reshape(LEV, 16, 128)
        dw = d_weights.reshape(LEV, 16, 128)
        d_logits[g] = (p * (dw - jnp.sum(p * dw, axis=0, keepdims=True))).astype(BF16).reshape(208, 128)
        return 0

    lax.fori_loop(0, GROUPS, group, 0)


def resample_latents(attended, ro, lq, latents):
    rows = attended[...].reshape(384, D)
    for nb in range(4):
        columns = slice(nb * 256, (nb + 1) * 256)
        part = dot(rows, ro[:, columns]).reshape(GROUPS, LATENT, 16, 256)
        part = part + lq[:, columns].astype(F32)[None, :, None, :]
        latents[:, :, columns] = part.astype(BF16).reshape(GROUPS, 48, 256)


def pack_pair(left, right, p, z, columns):
    left = left.reshape(2, 4, 2, 2, 8, left.shape[-1])
    right = right.reshape(2, 4, 2, 2, 8, right.shape[-1])
    for core in range(2):
        both = jnp.concatenate([left[:, :, :, core], right[:, :, :, core]], axis=3)
        p[core, z, :, :, :, :, columns] = both.astype(BF16)


def resample_gradients(tok, grad, attended, d_values, d_logits, turned, pv, po):
    def block(z, _):
        columns = pl.ds(pl.multiple_of(z * 256, 256), 256)
        turned[...] = tok[:, :, columns].reshape(GROUPS * 208, 256).T
        for nb in range(2):
            halves = []
            for half in range(2):
                c = slice(half * PACK + nb * 256, half * PACK + (nb + 1) * 256)
                halves.append(dot(turned[...], d_values[:, :, c].reshape(GROUPS * 208, 256)))
            pack_pair(halves[0], halves[1], pv, z, slice(nb * 256, (nb + 1) * 256))
        small = dot(turned[...], d_logits[...].reshape(GROUPS * 208, 128))
        pack_pair(small, jnp.zeros_like(small), pv, z, slice(PACK, PACK + 128))
        turned[:, :384] = attended[:, :, columns].reshape(384, 256).T
        for nb in range(2):
            halves = []
            for half in range(2):
                c = slice(half * PACK + nb * 256, half * PACK + (nb + 1) * 256)
                halves.append(dot(turned[:, :384], grad[:, :, c].reshape(384, 256)))
            pack_pair(halves[0], halves[1], po, z, slice(nb * 256, (nb + 1) * 256))
        return 0

    lax.fori_loop(0, 4, block, 0)


RESAMPLE_SCRATCH = [
    pltpu.VMEM((4, 128, 768), BF16),
    pltpu.VMEM((GROUPS, 208, D), BF16),
    pltpu.VMEM((GROUPS, 208, 128), F32),
    pltpu.VMEM((GROUPS, 208, 128), BF16),
    pltpu.VMEM((GROUPS, 48, D), BF16),
    pltpu.VMEM((GROUPS, 48, D), BF16),
    pltpu.VMEM((GROUPS, 208, D), BF16),
    pltpu.VMEM((GROUPS, 208, 128), BF16),
    pltpu.VMEM((256, GROUPS * 208), BF16),
]


def resample_kernel(tok, grad, kw, vw, ro, lq, latents, pv, po, *scratch):
    spread, values, logits, weights, d_attended, attended, d_values, d_logits, turned = scratch
    resample_project(tok, kw, vw, lq, spread, values, logits)
    resample_softmax(logits, weights)
    times_transposed(grad, ro, d_attended)
    resample_mix(values, weights, logits, spread, d_attended, attended, d_values, d_logits)
    resample_latents(attended, ro, lq, latents)
    resample_gradients(tok, grad, attended, d_values, d_logits, turned, pv, po)


def resample(tok, grad, kw, vw, ro, lq):
    vmem = pl.BlockSpec(memory_space=pltpu.VMEM)
    return pl.pallas_call(
        resample_kernel,
        out_shape=[
            jax.ShapeDtypeStruct((GROUPS, 48, D), BF16),
            jax.ShapeDtypeStruct((2, 4, 2, 4, 2, 16, PACK + 128), BF16),
            jax.ShapeDtypeStruct((2, 4, 2, 4, 2, 16, PACK), BF16),
        ],
        in_specs=[vmem] * 6,
        out_specs=[vmem] * 3,
        scratch_shapes=RESAMPLE_SCRATCH,
        compiler_params=pltpu.CompilerParams(vmem_limit_bytes=56 * MIB),
    )(tok, grad, kw, vw, ro, lq)


def normalise(x, gain, normed):
    def window(w, _):
        rows = pl.ds(pl.multiple_of(w * 96, 96), 96)
        values = x[rows, :].astype(F32)
        centred = values - jnp.mean(values, axis=-1, keepdims=True)
        spread = jnp.mean(centred * centred, axis=-1, keepdims=True)
        normed[rows, :] = (centred * lax.rsqrt(spread + 1e-05) * gain).astype(BF16)
        return 0

    lax.fori_loop(0, 4, window, 0)


def attend_heads(j, layer, w, normed, bias, mixed):
    def part(block):
        return dot(normed[...], w[layer * 4 + block, j // 2, j % 2].reshape(D, 256))

    queries, keys, values = (part(0) * 0.125).astype(BF16), part(1).astype(BF16), part(2).astype(BF16)
    head = lax.broadcasted_iota(jnp.int32, (96, 256), 1) // 64
    columns = pl.ds(pl.multiple_of(j * 256, 256), 256)
    for win in range(4):
        rows = slice(win * 96, (win + 1) * 96)
        q, k, v = queries[rows], keys[rows], values[rows]
        stacked = jnp.concatenate([jnp.where(head == h, q, jnp.zeros_like(q)) for h in range(4)], axis=0)
        logits = dot(stacked, k, ((1,), (1,)))
        if bias is not None:
            logits = (logits.reshape(4, 96, 96) + bias[win][None]).reshape(384, 96)
        e = jnp.exp(logits - jnp.max(logits, axis=-1, keepdims=True))
        out = dot(e.astype(BF16), v) * (1.0 / jnp.sum(e, axis=-1, keepdims=True))
        total = jnp.zeros((96, 256), F32)
        for h in range(4):
            total = total + jnp.where(head == h, out[h * 96 : (h + 1) * 96], 0.0)
        mixed[rows, columns] = total.astype(BF16)


def sublayer_kernel(masked, *refs):
    if masked:
        x, gain, w, bias, out, normed, mixed = refs
    else:
        x, gain, w, out, normed, mixed = refs
        bias = None
    normalise(x, gain[...], normed)

    def heads(j, _):
        attend_heads(j, 0, w, normed, bias, mixed)
        return 0

    lax.fori_loop(0, 4, heads, 0)
    for j in range(4):
        columns = slice(j * 256, (j + 1) * 256)
        update = dot(mixed[...], w[3, j // 2, j % 2].reshape(D, 256))
        out[:, columns] = (x[:, columns].astype(F32) + update).astype(BF16)


def sublayer(x, gain, w, layer, bias):
    vmem = pl.BlockSpec(memory_space=pltpu.VMEM)
    extra = [] if bias is None else [bias]
    return pl.pallas_call(
        functools.partial(sublayer_kernel, bias is not None),
        grid=(1,),
        out_shape=jax.ShapeDtypeStruct((384, D), BF16),
        in_specs=[vmem, vmem, pl.BlockSpec((4,) + w.shape[1:], lambda i: (layer,) + (0,) * 7)] + [vmem] * len(extra),
        out_specs=vmem,
        scratch_shapes=[pltpu.VMEM((384, D), BF16), pltpu.VMEM((384, D), BF16)],
        compiler_params=pltpu.CompilerParams(vmem_limit_bytes=56 * MIB),
    )(x, gain, w, *extra)


def from_behind(block, axis, distance):
    count = lax.axis_size(axis)
    return lax.ppermute(block, axis, [((i - distance) % count, i) for i in range(count)])


def local(
    level_tokens,
    latent_query,
    key_weight,
    value_weight,
    resample_out,
    norm_gain,
    qkv_weight,
    out_weight,
    window_label,
    grad_latents,
):
    tok = level_tokens.reshape(2, GROUPS, 2, 4, LEV, D).transpose(1, 4, 2, 0, 3, 5).reshape(GROUPS, 208, D)
    grad = grad_latents.reshape(2, GROUPS, 2, 4, LATENT, D).transpose(1, 4, 2, 0, 3, 5).reshape(GROUPS, 48, D)
    shard = jnp.concatenate([qkv_weight.transpose(0, 2, 1, 3), out_weight[:, None]], axis=1).reshape(8, 32, 256)
    w = gather(shard)
    latents, pv, po = resample(tok, grad, key_weight, value_weight, resample_out, latent_query)
    factor = (2 * 64 * lax.axis_size("lat") * lax.axis_size("lon")) ** (-0.5)
    grad_key, grad_value, grad_out = reduce_gradients(factor, pv, po, latent_query)

    tiles = lax.all_to_all(latents.reshape(4, 2, 48, D), "lon", split_axis=0, concat_axis=0, tiled=True)
    x = tiles.reshape(2, 2, 2, 48, D).swapaxes(1, 2).reshape(384, D)
    middle = sublayer(x, norm_gain[0:1], w, 0, None)
    cells = middle.reshape(2, 2, 2, LATENT, 2, 8, D).transpose(0, 2, 1, 4, 3, 5, 6).reshape(4, 4, LATENT, 8, D)
    cells = jnp.concatenate([cells[1:], from_behind(cells[:1], "lat", -1)], axis=0)
    cells = jnp.concatenate([cells[:, 1:], from_behind(cells[:, :1], "lon", -1)], axis=1)
    rolled = cells.reshape(2, 2, 2, 2, LATENT, 8, D).transpose(0, 2, 1, 4, 3, 5, 6).reshape(384, D)

    row = lax.axis_index("lat") * 8 + jnp.arange(8, dtype=jnp.int32)
    codes = window_label * 2 + (row >= 8 * lax.axis_size("lat") - 2).astype(jnp.int32)[:, None]
    codes = codes.reshape(2, 2, 2, 2, 2, 4).transpose(0, 3, 1, 4, 2, 5)
    codes = jnp.broadcast_to(codes[:, :, :, None], (2, 2, 2, LATENT, 2, 2, 4)).reshape(4, 96)
    bias = jnp.where(codes[:, :, None] == codes[:, None, :], 0.0, -1e30).astype(F32)
    out = sublayer(rolled, norm_gain[1:2], w, 1, bias)
    out = out.reshape(2, 2, 2, LATENT, 2, 2, 4, D).transpose(0, 2, 5, 1, 4, 6, 3, 7).reshape(8, 16, LATENT, D)
    return (out, grad_key, grad_value, grad_out)


def solution(mesh):
    in_specs = (
        P(("lat", "lon"), None, None, None),
        P(),
        P(),
        P(),
        P(),
        P(),
        P(None, "lat", None, "lon"),
        P(None, "lat", "lon"),
        P("lat", "lon"),
        P(("lat", "lon"), None, None, None),
    )
    out_specs = (
        P("lat", "lon", None, None),
        P(("lat", "lon"), None),
        P(("lat", "lon"), None),
        P(("lat", "lon"), None),
    )
    return jax.shard_map(local, mesh=mesh, in_specs=in_specs, out_specs=out_specs, check_vma=False)
```

```python
import functools

import jax
import jax.numpy as jnp
from jax import lax
from jax.experimental import pallas as pl
from jax.experimental.pallas import tpu as pltpu
from jax.sharding import PartitionSpec as P

MESH = pl.DeviceIdType.MESH
F32, BF16 = jnp.float32, jnp.bfloat16
D = 1024
HEADS = 16
LEV = 13
LATENT = 3
GROUPS = 8
MIB = 1024 * 1024


def dot(a, b, dims=((1,), (0,))):
    return lax.dot_general(a, b, (dims, ((), ())), preferred_element_type=F32)


def my_place():
    lat, lon = lax.axis_index("lat"), lax.axis_index("lon")
    return {
        "z": lat // 8,
        "y": ((lat // 4) % 2) * 2 + lon // 2,
        "x": lat % 4,
        "core": lon % 2,
    }


def device_of(place):
    lat = place["z"] * 8 + (place["y"] // 2) * 4 + place["x"]
    return (lat, (place["y"] % 2) * 2 + place["core"])


def moved(place, dim, delta):
    size = 2 if dim == "core" else 4
    other = dict(place)
    other[dim] = (place[dim] + delta + size) % size
    return device_of(other)


def pick(dim, value):
    if dim == "y":
        if value is None:
            return {"yh": slice(None), "yl": slice(None)}
        return {"yh": pl.ds(value // 2, 1), "yl": pl.ds(value % 2, 1)}
    return {dim: slice(None) if value is None else pl.ds(value, 1)}


def greet(place):
    barrier = pltpu.get_barrier_semaphore()
    others = [moved(place, dim, step) for dim in "xyz" for step in (1, -1)] + [moved(place, "core", 1)]
    lat, lon = device_of(place)
    others += [(lat, (lon + k) % 4) for k in range(1, 4)]
    others += [((lat + step) % 32, (lon + turn) % 4) for step, turn in ((1, 0), (31, 0), (1, 1), (31, 3))]
    for other in others:
        pl.semaphore_signal(barrier, inc=1, device_id=other, device_id_type=MESH)
    pl.semaphore_wait(barrier, len(others))


PARTS = (
    ((0, 3, ("x", "y", "z")), (3, 3, ("y", "z", "x")), (6, 2, ("z", "x", "y"))),
    ((8, 3, ("z", "x", "y")), (11, 3, ("x", "y", "z")), (14, 2, ("y", "z", "x"))),
)


class Gather:
    def __init__(self, place, w, send, recv, number, part):
        self.place, self.w, self.send, self.recv, self.number = place, w, send, recv, number
        first, count, self.order = part
        self.tiles = pl.ds(first, count)

    def region(self, phase, value, half=None):
        index = {}
        for position, dim in enumerate(self.order):
            if position < phase:
                index.update(pick(dim, None))
            elif position == phase:
                index.update(pick(dim, value))
            else:
                index.update(pick(dim, self.place[dim]))
        rows = slice(None) if half is None else pl.ds(16 * half, 16)
        core = self.place["core"]
        return self.w.at[self.tiles, index["yl"], core, index["z"], index["yh"], index["x"], rows, :]

    def copy(self, k, ref, other):
        return pltpu.make_async_remote_copy(
            src_ref=ref,
            dst_ref=ref,
            send_sem=self.send.at[self.number, k],
            recv_sem=self.recv.at[self.number, k],
            device_id=other,
            device_id_type=MESH,
        )

    def ring(self, phase, k):
        dim = self.order[phase]
        me = self.place[dim]
        other = moved(self.place, dim, 1 if k % 2 == 0 else -1)
        if k < 2:
            return self.copy(4 * phase + k, self.region(phase, me), other)
        return self.copy(4 * phase + k, self.region(phase, (me + 7 - 2 * k) % 4, k - 2), other)

    def arrival(self, phase, k):
        dim = self.order[phase]
        me = self.place[dim]
        other = moved(self.place, dim, -1 if k % 2 == 0 else 1)
        if k < 2:
            return self.copy(4 * phase + k, self.region(phase, (me + 3 + 2 * k) % 4), other)
        return self.copy(4 * phase + k, self.region(phase, (me + 2) % 4, k - 2), other)

    def across(self, core):
        return self.copy(12, self.w.at[self.tiles, :, core], moved(self.place, "core", 1))

    def step(self, s):
        phase, part = divmod(s, 2)
        if part == 0:
            if phase > 0:
                self.arrival(phase - 1, 2).wait_recv()
                self.arrival(phase - 1, 3).wait_recv()
            if phase < 3:
                self.ring(phase, 0).start()
                self.ring(phase, 1).start()
            else:
                self.across(self.place["core"]).start()
        elif phase < 3:
            self.arrival(phase, 0).wait_recv()
            self.ring(phase, 2).start()
            self.arrival(phase, 1).wait_recv()
            self.ring(phase, 3).start()
        else:
            self.across(1 - self.place["core"]).wait_recv()

    def drain(self):
        for phase in range(3):
            for k in range(4):
                self.ring(phase, k).wait_send()
        self.across(self.place["core"]).wait_send()


def landing_shape(order, phase, columns):
    sizes = {"z": 4, "yh": 2, "x": 4, "yl": 2}
    for dim in order[: phase + 1]:
        for name in ("yh", "yl") if dim == "y" else (dim,):
            sizes[name] = 1
    return (sizes["z"], sizes["yh"], sizes["x"], sizes["yl"], 16, columns)


HALF = {256: 128, 384: 128, 512: 256}


class Reduce:
    def __init__(self, place, p, landing, send, recv, order):
        self.place, self.p, self.landing = place, p, landing
        self.send, self.recv, self.order = send, recv, order

    def region(self, phase, value, part):
        index = {}
        for position, dim in enumerate(self.order):
            if position < phase:
                index.update(pick(dim, self.place[dim]))
            elif position == phase:
                index.update(pick(dim, value))
            else:
                index.update(pick(dim, None))
        width = self.p.shape[-1]
        cut = HALF[width]
        columns = {None: slice(None), 0: pl.ds(0, cut), 1: pl.ds(cut, width - cut)}[part]
        return (self.place["core"], index["z"], index["yh"], index["x"], index["yl"], slice(None), columns)

    def copy(self, k, src, dst, other):
        return pltpu.make_async_remote_copy(
            src_ref=src,
            dst_ref=dst,
            send_sem=self.send.at[k],
            recv_sem=self.recv.at[k],
            device_id=other,
            device_id_type=MESH,
        )

    def across(self):
        return self.copy(12, self.p.at[1 - self.place["core"]], self.landing[12], moved(self.place, "core", 1))

    def ring(self, phase, k):
        dim = self.order[phase]
        me = self.place[dim]
        target = ((me + 2) % 4, (me + 2) % 4, (me + 1) % 4, (me + 3) % 4)[k]
        part = (0, 1, None, None)[k]
        other = moved(self.place, dim, 1 if k % 2 == 0 else -1)
        return self.copy(4 * phase + k, self.p.at[self.region(phase, target, part)], self.landing[4 * phase + k], other)

    def add(self, region, *landed):
        total = self.p[region].astype(F32)
        for ref in landed:
            total = total + ref[...].astype(F32)
        self.p[region] = total.astype(BF16)

    def step(self, s):
        if s == 0:
            self.across().start()
            return
        phase, part = divmod(s - 1, 2)
        land = self.landing
        if part == 0:
            if phase == 0:
                self.across().wait_recv()
                core = self.place["core"]
                for z in range(4):
                    self.p[core, z] = (self.p[core, z].astype(F32) + land[12][z].astype(F32)).astype(BF16)
            else:
                self.ring(phase - 1, 2).wait_recv()
                self.ring(phase - 1, 3).wait_recv()
                me = self.place[self.order[phase - 1]]
                self.add(self.region(phase - 1, me, None), land[4 * phase - 2], land[4 * phase - 1])
            if phase < 3:
                self.ring(phase, 0).start()
                self.ring(phase, 1).start()
        else:
            me = self.place[self.order[phase]]
            self.ring(phase, 0).wait_recv()
            self.add(self.region(phase, (me + 1) % 4, 0), land[4 * phase])
            self.ring(phase, 2).start()
            self.ring(phase, 1).wait_recv()
            self.add(self.region(phase, (me + 3) % 4, 1), land[4 * phase + 1])
            self.ring(phase, 3).start()

    def drain(self):
        for phase in range(3):
            for k in range(4):
                self.ring(phase, k).wait_send()
        self.across().wait_send()

    def result(self):
        y = self.place["y"]
        return self.p[self.place["core"], self.place["z"], y // 2, self.place["x"], y % 2].astype(F32)


def landing_shapes(order, columns):
    shapes = []
    for phase in range(3):
        for part in (HALF[columns], columns - HALF[columns], columns, columns):
            shapes.append(pltpu.VMEM(landing_shape(order, phase, part), BF16))
    shapes.append(pltpu.VMEM((4, 2, 4, 2, 16, columns), BF16))
    return shapes


def spread_queries(lq):
    row = lax.broadcasted_iota(jnp.int32, (128, D), 0)
    head = lax.broadcasted_iota(jnp.int32, (128, D), 1) // 64
    total = jnp.zeros((128, D), F32)
    for q in range(LATENT):
        total = total + jnp.where(row == q * HEADS + head, lq[q : q + 1, :].astype(F32), 0.0)
    return total.astype(BF16)


def finish_gradients(factor, sums, lq, grad_key, grad_value, grad_out):
    first, second, third = sums
    grad_value[:, 0:256] = first[:8, :256] * factor
    grad_value[:, 256:512] = second[:8] * factor
    grad_value[:, 512:768] = first[8:, :256] * factor
    grad_value[:, 768:1024] = second[8:] * factor
    grad_out[:, 0:512] = third[:8] * factor
    grad_out[:, 512:1024] = third[8:] * factor
    small = first[:8, 256:] * (factor * 0.125)
    high = small.astype(BF16)
    low = (small - high.astype(F32)).astype(BF16)
    queries = spread_queries(lq)
    grad_key[...] = dot(high, queries) + dot(low, queries)


def looped(count, body, hooks):
    def step(i, _):
        body(i)
        for at, hook in hooks.items():
            pl.when(i == at)(hook)
        return 0

    lax.fori_loop(0, count, step, 0)


def group_at(g):
    return g // 4, pl.ds(pl.multiple_of((g % 4) * 16, 16), 16)


def spread_heads(spread):
    row = lax.broadcasted_iota(jnp.int32, (128, 768), 0)
    column = lax.broadcasted_iota(jnp.int32, (128, 768), 1)
    for cb in range(4):
        hit = row == (column // 256) * HEADS + cb * 4 + (column % 256) // 64
        spread[cb] = jnp.where(hit, 1.0, 0.0).astype(BF16)


def key_queries(kw, lq, kq):
    queries = spread_queries(lq)

    def rows(i, _):
        at = pl.ds(pl.multiple_of(i * 256, 256), 256)
        total = dot(kw[at, :], queries, ((1,), (1,))) * 0.125
        high = total.astype(BF16)
        kq[0, at, :] = high
        kq[1, at, :] = (total - high.astype(F32)).astype(BF16)
        return 0

    lax.fori_loop(0, 4, rows, 0)


def resample_project(tok, vw, kq, values, logits, hooks):
    def project(r):
        rows = tok[r].reshape(LEV * 64, D)
        for nb in range(4):
            columns = slice(nb * 256, (nb + 1) * 256)
            values[r, :, :, columns] = dot(rows, vw[:, columns]).astype(BF16).reshape(LEV, 64, 256)
        logits[r] = (dot(rows, kq[0]) + dot(rows, kq[1])).reshape(LEV, 64, 128)

    looped(2, project, hooks)


def resample_softmax(logits, weights):
    def group(g, _):
        r, c = group_at(g)
        x = logits[r, :, c]
        x = jnp.exp(x - jnp.max(x, axis=0, keepdims=True))
        x = x / jnp.sum(x, axis=0, keepdims=True)
        logits[r, :, c] = x
        weights[r, :, c] = x.astype(BF16)
        return 0

    lax.fori_loop(0, GROUPS, group, 0)


def resample_cotangents(grad, ro, d_attended):
    rows = grad[...].reshape(384, D)
    for nb in range(4):
        columns = slice(nb * 256, (nb + 1) * 256)
        part = dot(rows, ro[columns, :], ((1,), (1,)))
        d_attended[:, :, :, columns] = part.astype(BF16).reshape(2, LATENT, 64, 256)


def resample_mix(values, weights, probs, spread, d_attended, attended, d_logits, hooks):
    def group(g):
        r, c = group_at(g)
        w = weights[r, :, c].reshape(208, 128)
        d_weights = jnp.zeros((208, 128), F32)
        for cb in range(4):
            columns = slice(cb * 256, (cb + 1) * 256)
            wide = dot(w, spread[cb])
            v = values[r, :, c, columns].astype(F32)
            d_v = jnp.zeros((LEV, 16, 256), F32)
            products = []
            for q in range(LATENT):
                wq = wide[:, q * 256 : (q + 1) * 256].reshape(LEV, 16, 256)
                da = d_attended[r, q, c, columns].astype(F32)[None]
                attended[r, q, c, columns] = jnp.sum(wq * v, axis=0).astype(BF16)
                d_v = d_v + wq * da
                products.append((v * da).astype(BF16).reshape(208, 256))
            values[r, :, c, columns] = d_v.astype(BF16)
            d_weights = d_weights + dot(jnp.concatenate(products, axis=1), spread[cb], ((1,), (1,)))
        p = probs[r, :, c]
        dw = d_weights.reshape(LEV, 16, 128)
        d_logits[r, :, c] = (p * (dw - jnp.sum(p * dw, axis=0, keepdims=True))).astype(BF16)

    looped(GROUPS, group, hooks)


def resample_latents(attended, ro, lq, latents):
    rows = attended[...].reshape(384, D)
    for nb in range(4):
        columns = slice(nb * 256, (nb + 1) * 256)
        part = dot(rows, ro[:, columns]).reshape(2, LATENT, 64, 256)
        part = part + lq[:, columns].astype(F32)[None, :, None, :]
        latents[:, :, :, columns] = part.astype(BF16)


def pack_pair(left, right, p, z, columns):
    left = left.reshape(2, 4, 2, 2, 8, left.shape[-1])
    right = right.reshape(2, 4, 2, 2, 8, right.shape[-1])
    for core in range(2):
        both = jnp.concatenate([left[:, :, :, core], right[:, :, :, core]], axis=3)
        p[core, z, :, :, :, :, columns] = both.astype(BF16)


def resample_gradients(tok, grad, attended, d_values, d_logits, turned, packed, hooks):
    first, second, third = packed

    def block(z):
        columns = pl.ds(pl.multiple_of(z * 256, 256), 256)
        turned[...] = tok[:, :, :, columns].reshape(GROUPS * 208, 256).T
        for nb in range(2):
            halves = []
            for half in range(2):
                c = slice(half * 512 + nb * 256, half * 512 + (nb + 1) * 256)
                halves.append(dot(turned[...], d_values[:, :, :, c].reshape(GROUPS * 208, 256)))
            pack_pair(halves[0], halves[1], (first, second)[nb], z, slice(0, 256))
        small = dot(turned[...], d_logits[...].reshape(GROUPS * 208, 128))
        pack_pair(small, jnp.zeros_like(small), first, z, slice(256, 384))
        turned[:, :384] = attended[:, :, :, columns].reshape(384, 256).T
        for nb in range(2):
            halves = []
            for half in range(2):
                c = slice(half * 512 + nb * 256, half * 512 + (nb + 1) * 256)
                halves.append(dot(turned[:, :384], grad[:, :, :, c].reshape(384, 256)))
            pack_pair(halves[0], halves[1], third, z, slice(nb * 256, (nb + 1) * 256))

    looped(4, block, hooks)


def normalise(window, gain, normed):
    for win in range(4):
        values = window(win)
        centred = values - jnp.mean(values, axis=-1, keepdims=True)
        spread = jnp.mean(centred * centred, axis=-1, keepdims=True)
        normed[win * 96 : (win + 1) * 96, :] = (centred * lax.rsqrt(spread + 1e-05) * gain).astype(BF16)


def weight_block(w, layer, block, j):
    tile = layer * 8 + block
    return jnp.concatenate([w[tile + 4 * i, j // 2, j % 2].reshape(D, 128) for i in range(2)], axis=1)


def attend_heads(j, layer, w, normed, bias, mixed):
    queries, keys, values = (dot(normed[...], weight_block(w, layer, block, j)) for block in range(3))
    queries, keys, values = (queries * 0.125).astype(BF16), keys.astype(BF16), values.astype(BF16)
    head = lax.broadcasted_iota(jnp.int32, (96, 256), 1) // 64
    columns = pl.ds(pl.multiple_of(j * 256, 256), 256)
    for win in range(4):
        rows = slice(win * 96, (win + 1) * 96)
        q, k, v = queries[rows], keys[rows], values[rows]
        stacked = jnp.concatenate([jnp.where(head == h, q, jnp.zeros_like(q)) for h in range(4)], axis=0)
        logits = dot(stacked, k, ((1,), (1,)))
        if bias is not None:
            logits = (logits.reshape(4, 96, 96) + bias[win][None]).reshape(384, 96)
        e = jnp.exp(logits - jnp.max(logits, axis=-1, keepdims=True))
        out = dot(e.astype(BF16), v) * (1.0 / jnp.sum(e, axis=-1, keepdims=True))
        total = jnp.zeros((96, 256), F32)
        for h in range(4):
            total = total + jnp.where(head == h, out[h * 96 : (h + 1) * 96], 0.0)
        mixed[rows, columns] = total.astype(BF16)


def output_update(w, layer, j, mixed):
    return dot(mixed[...], weight_block(w, layer, 3, j)).reshape(2, 2, 4, LATENT, 8, 256)


def tile_rows(x, wr, columns=slice(None)):
    return x[4 * wr : 4 * wr + 4, :, :, columns].astype(F32)


def first_sublayer(x, gain, w, normed, mixed, middle, hooks):
    def window(win):
        wr, wc = divmod(win, 2)
        return tile_rows(x, wr)[:, :, 8 * wc : 8 * wc + 8].reshape(96, D)

    normalise(window, gain, normed)
    looped(4, lambda j: attend_heads(j, 0, w, normed, None, mixed), hooks)
    for j in range(4):
        columns = slice(j * 256, (j + 1) * 256)
        update = output_update(w, 0, j, mixed)
        for wr in range(2):
            both = jnp.concatenate([update[wr, 0], update[wr, 1]], axis=2)
            middle[4 * wr : 4 * wr + 4, :, 0:16, columns] = tile_rows(x, wr, columns) + both


def second_sublayer(middle, gain, w, normed, mixed, bias, out, hooks):
    def window(win):
        wr, wc = divmod(win, 2)
        return middle[4 * wr + 2 : 4 * wr + 6, :, 8 * wc + 4 : 8 * wc + 12, :].reshape(96, D)

    normalise(window, gain, normed)
    looped(4, lambda j: attend_heads(j, 1, w, normed, bias, mixed), hooks)
    for j in range(4):
        columns = slice(j * 256, (j + 1) * 256)
        update = output_update(w, 1, j, mixed)
        for wr in range(2):
            halves = []
            for wc in range(2):
                own = middle[4 * wr + 2 : 4 * wr + 6, :, 8 * wc + 4 : 8 * wc + 12, columns]
                halves.append(own + update[wr, wc])
            both = jnp.concatenate(halves, axis=2).astype(BF16)
            out[4 * wr : 4 * wr + 4, :, :, columns] = both


class Edges:
    def __init__(self, place, middle, rows_out, columns_out, rows_in, columns_in, corner_in, send, recv):
        lat, lon = device_of(place)
        above, beside = (lat + 31) % 32, (lon + 3) % 4
        self.middle, self.rows_out, self.columns_out = middle, rows_out, columns_out
        self.rows_in, self.columns_in, self.corner_in = rows_in, columns_in, corner_in
        plan = (
            (rows_out, rows_in, (above, lon)),
            (columns_out, columns_in, (lat, beside)),
            (columns_out.at[pl.ds(0, 32)], corner_in, (above, beside)),
        )
        self.copies = [
            pltpu.make_async_remote_copy(
                src_ref=src,
                dst_ref=dst,
                send_sem=send.at[k],
                recv_sem=recv.at[k],
                device_id=other,
                device_id_type=MESH,
            )
            for k, (src, dst, other) in enumerate(plan)
        ]

    def start(self):
        middle = self.middle
        for r in range(2):
            self.rows_out[r] = middle[r, :, 0:16].reshape(48, D).astype(BF16)
        for part in range(6):
            cells = [divmod(part * 4 + i, LATENT) for i in range(4)]
            rows = jnp.concatenate([middle[r, q, 0:4] for r, q in cells], axis=0)
            self.columns_out[part * 16 : (part + 1) * 16] = rows.astype(BF16)
        for copy in self.copies:
            copy.start()

    def finish(self):
        middle = self.middle
        for copy in self.copies:
            copy.wait_recv()
        for r in range(2):
            middle[8 + r, :, 0:16] = self.rows_in[r].astype(F32).reshape(LATENT, 16, D)
        for part in range(6):
            rows = self.columns_in[part * 16 : (part + 1) * 16].astype(F32)
            for i in range(4):
                r, q = divmod(part * 4 + i, LATENT)
                middle[r, q, 16:20] = rows[i * 4 : (i + 1) * 4]
        for part in range(2):
            rows = self.corner_in[part * 16 : (part + 1) * 16].astype(F32)
            for i in range(4):
                r, q = divmod(part * 4 + i, LATENT)
                if r < 2:
                    middle[8 + r, q, 16:20] = rows[i * 4 : (i + 1) * 4]

    def drain(self):
        for copy in self.copies:
            copy.wait_send()


class Tiles:
    def __init__(self, place, latents, x, send, recv, own):
        lat, lon = device_of(place)

        def at(column):
            return pl.ds(pl.multiple_of(column * 16, 16), 16)

        self.own = pltpu.make_async_copy(latents.at[:, :, at(lon)], x.at[pl.ds(2 * lon, 2)], own)
        self.out, self.arriving = [], []
        for k in range(1, 4):
            there, source = (lon + k) % 4, (lon + 4 - k) % 4
            for copies, column, row, other in (
                (self.out, there, lon, there),
                (self.arriving, source, source, source),
            ):
                copies.append(
                    pltpu.make_async_remote_copy(
                        src_ref=latents.at[:, :, at(column)],
                        dst_ref=x.at[pl.ds(2 * row, 2)],
                        send_sem=send.at[k - 1],
                        recv_sem=recv.at[k - 1],
                        device_id=(lat, other),
                        device_id_type=MESH,
                    )
                )

    def start(self):
        for copy in self.out:
            copy.start()
        self.own.start()

    def finish(self):
        self.own.wait()
        for copy in self.arriving:
            copy.wait_recv()

    def drain(self):
        for copy in self.out:
            copy.wait_send()


WIDTHS = (384, 256, 512)
REDUCE_ORDERS = (("x", "y", "z"), ("y", "z", "x"), ("z", "x", "y"))


def kernel(factor, tokens, grads, kw_far, vw_far, ro_far, lq, gains, qkv, ow, bias, *refs):
    out, grad_key, grad_value, grad_out = refs[:4]
    w, latents, x, rows_out, columns_out, rows_in, columns_in, corner_in = refs[4:12]
    packed, landing = refs[12:15], refs[15:54]
    g_send, g_recv, r_send, r_recv, t_send, t_recv, e_send, e_recv, near = refs[54:]
    place = my_place()
    y = place["y"]
    own = []
    for layer in range(2):
        for half in range(2):
            columns = pl.ds(128 * half, 128)
            tile = layer * 8 + half * 4
            mine = (y % 2, place["core"], place["z"], y // 2, place["x"])
            own.append((qkv.at[layer, :, :, columns], w.at[(pl.ds(tile, 3),) + mine]))
            own.append((ow.at[layer, :, columns], w.at[(tile + 3,) + mine]))
    own = [pltpu.make_async_copy(src, dst, near.at[i]) for i, (src, dst) in enumerate(own)]
    for copy in own:
        copy.start()
    layers = [
        [Gather(place, w, g_send, g_recv, 3 * layer + i, part) for i, part in enumerate(PARTS[layer])]
        for layer in range(2)
    ]
    sums = [
        Reduce(place, packed[i], landing[13 * i : 13 * i + 13], r_send.at[i], r_recv.at[i], REDUCE_ORDERS[i])
        for i in range(3)
    ]
    tiles = Tiles(place, latents, x, t_send, t_recv, near.at[8])

    def gathered(layer, s):
        def hook():
            for part in layers[layer]:
                part.step(s)

        return hook

    def reduced(s):
        def hook():
            for part in sums:
                part.step(s)

        return hook

    def both(*hooks):
        def hook():
            for one in hooks:
                one()

        return hook

    def resampler(tok, grad, kw, vw, ro, kq, values, logits, weights, spread, d_att, att, d_logits, turned):
        pairs = ((kw_far, kw), (tokens, tok), (vw_far, vw), (grads, grad), (ro_far, ro))
        copies = [pltpu.make_async_copy(far, here, near.at[9 + i]) for i, (far, here) in enumerate(pairs)]
        for copy in copies:
            copy.start()
        greet(place)
        for copy in own:
            copy.wait()
        gathered(0, 0)()
        gathered(1, 0)()
        spread_heads(spread)
        copies[0].wait()
        key_queries(kw, lq, kq)
        gathered(0, 1)()
        gathered(1, 1)()
        copies[1].wait()
        copies[2].wait()
        gathered(0, 2)()
        hooks = {0: both(gathered(0, 3), gathered(1, 2)), 1: gathered(0, 4)}
        resample_project(tok, vw, kq, values, logits, hooks)
        resample_softmax(logits, weights)
        copies[3].wait()
        copies[4].wait()
        resample_cotangents(grad, ro, d_att)
        hooks = {0: gathered(1, 3), 4: both(gathered(0, 5), gathered(1, 4))}
        resample_mix(values, weights, logits, spread, d_att, att, d_logits, hooks)
        resample_latents(att, ro, lq, latents)
        tiles.start()
        hooks = {0: gathered(0, 6), 3: gathered(0, 7)}
        resample_gradients(tok, grad, att, values, d_logits, turned, packed, hooks)

    pl.run_scoped(
        resampler,
        pltpu.VMEM((2, LEV, 64, D), BF16),
        pltpu.VMEM((2, LATENT, 64, D), BF16),
        pltpu.VMEM((D, D), BF16),
        pltpu.VMEM((D, D), BF16),
        pltpu.VMEM((D, D), BF16),
        pltpu.VMEM((2, D, 128), BF16),
        pltpu.VMEM((2, LEV, 64, D), BF16),
        pltpu.VMEM((2, LEV, 64, 128), F32),
        pltpu.VMEM((2, LEV, 64, 128), BF16),
        pltpu.VMEM((4, 128, 768), BF16),
        pltpu.VMEM((2, LATENT, 64, D), BF16),
        pltpu.VMEM((2, LATENT, 64, D), BF16),
        pltpu.VMEM((2, LEV, 64, 128), BF16),
        pltpu.VMEM((256, GROUPS * 208), BF16),
    )
    reduced(0)()

    def backbone(middle, normed, mixed):
        edges = Edges(place, middle, rows_out, columns_out, rows_in, columns_in, corner_in, e_send, e_recv)
        tiles.finish()
        hooks = {0: reduced(1), 1: gathered(1, 5), 2: reduced(2), 3: gathered(1, 6)}
        first_sublayer(x, gains[0:1, :], w, normed, mixed, middle, hooks)
        edges.start()
        gathered(1, 7)()
        reduced(3)()
        edges.finish()
        hooks = {0: reduced(4), 1: reduced(5), 2: reduced(6), 3: reduced(7)}
        second_sublayer(middle, gains[1:2, :], w, normed, mixed, bias, out, hooks)
        edges.drain()

    pl.run_scoped(
        backbone,
        pltpu.VMEM((10, LATENT, 24, D), F32),
        pltpu.VMEM((384, D), BF16),
        pltpu.VMEM((384, D), BF16),
    )
    finish_gradients(factor, [part.result() for part in sums], lq, grad_key, grad_value, grad_out)
    tiles.drain()
    for part in layers[0] + layers[1] + sums:
        part.drain()


def whole(factor, tokens, grads, kw, vw, ro, lq, gains, qkv, ow, bias):
    vmem, far = pl.BlockSpec(memory_space=pltpu.VMEM), pl.BlockSpec(memory_space=pl.ANY)
    landings = []
    for order, width in zip(REDUCE_ORDERS, WIDTHS):
        landings += landing_shapes(order, width)
    dma = pltpu.SemaphoreType.DMA
    return pl.pallas_call(
        functools.partial(kernel, factor),
        out_shape=[jax.ShapeDtypeStruct((8, LATENT, 16, D), BF16)] + [jax.ShapeDtypeStruct((8, D), F32)] * 3,
        in_specs=[far] * 5 + [vmem, vmem, far, far, vmem],
        out_specs=[vmem] * 4,
        scratch_shapes=[
            pltpu.VMEM((16, 2, 2, 4, 2, 4, 32, 128), BF16),
            pltpu.VMEM((2, LATENT, 64, D), BF16),
            pltpu.VMEM((8, LATENT, 16, D), BF16),
            pltpu.VMEM((2, 48, D), BF16),
            pltpu.VMEM((96, D), BF16),
            pltpu.VMEM((2, 48, D), BF16),
            pltpu.VMEM((96, D), BF16),
            pltpu.VMEM((32, D), BF16),
        ]
        + [pltpu.VMEM((2, 4, 2, 4, 2, 16, width), BF16) for width in WIDTHS]
        + landings
        + [dma((6, 13)), dma((6, 13)), dma((3, 13)), dma((3, 13))]
        + [dma((3,)), dma((3,)), dma((3,)), dma((3,)), dma((14,))],
        compiler_params=pltpu.CompilerParams(collective_id=0, has_side_effects=True, vmem_limit_bytes=63 * MIB),
    )(tokens, grads, kw, vw, ro, lq, gains, qkv, ow, bias)


def hand_over_kernel(*refs):
    count = len(refs) // 2
    for i in range(count):
        refs[count + i][...] = refs[i][...]


def hand_over(results):
    return pl.pallas_call(
        hand_over_kernel,
        out_shape=[jax.ShapeDtypeStruct(r.shape, r.dtype) for r in results],
        in_specs=[pl.BlockSpec(memory_space=pltpu.VMEM)] * len(results),
        out_specs=[pl.BlockSpec(memory_space=pltpu.VMEM)] * len(results),
    )(*results)


def local(
    level_tokens,
    latent_query,
    key_weight,
    value_weight,
    resample_out,
    norm_gain,
    qkv_weight,
    out_weight,
    window_label,
    grad_latents,
):
    row = lax.axis_index("lat") * 8 + jnp.arange(8, dtype=jnp.int32)
    codes = window_label * 2 + (row >= 8 * lax.axis_size("lat") - 2).astype(jnp.int32)[:, None]
    codes = codes.reshape(2, 4, 2, 8).transpose(0, 2, 1, 3)
    codes = jnp.broadcast_to(codes[:, :, :, None], (2, 2, 4, LATENT, 8)).reshape(4, 96)
    bias = jnp.where(codes[:, :, None] == codes[:, None, :], 0.0, -1e30).astype(F32)
    factor = (2 * 64 * lax.axis_size("lat") * lax.axis_size("lon")) ** (-0.5)
    results = whole(
        factor,
        level_tokens.swapaxes(1, 2),
        grad_latents.swapaxes(1, 2),
        key_weight,
        value_weight,
        resample_out,
        latent_query,
        norm_gain,
        qkv_weight.swapaxes(1, 2),
        out_weight,
        bias,
    )
    out, grad_key, grad_value, grad_out = hand_over(results)
    return (out.swapaxes(1, 2), grad_key, grad_value, grad_out)


def solution(mesh):
    in_specs = (
        P(("lat", "lon"), None, None, None),
        P(),
        P(),
        P(),
        P(),
        P(),
        P(None, "lat", None, "lon"),
        P(None, "lat", "lon"),
        P("lat", "lon"),
        P(("lat", "lon"), None, None, None),
    )
    out_specs = (
        P("lat", "lon", None, None),
        P(("lat", "lon"), None),
        P(("lat", "lon"), None),
        P(("lat", "lon"), None),
    )
    return jax.shard_map(local, mesh=mesh, in_specs=in_specs, out_specs=out_specs, check_vma=False)
```

```python
import functools

import jax
import jax.numpy as jnp
from jax import lax
from jax.experimental import pallas as pl
from jax.experimental.pallas import tpu as pltpu
from jax.sharding import PartitionSpec as P

MESH = pl.DeviceIdType.MESH
F32, BF16 = jnp.float32, jnp.bfloat16
D = 1024
HEADS = 16
LEV = 13
LATENT = 3
GROUPS = 8
MIB = 1024 * 1024


def dot(a, b, dims=((1,), (0,))):
    return lax.dot_general(a, b, (dims, ((), ())), preferred_element_type=F32)


def my_place():
    lat, lon = lax.axis_index("lat"), lax.axis_index("lon")
    return {
        "z": lat // 8,
        "y": ((lat // 4) % 2) * 2 + lon // 2,
        "x": lat % 4,
        "core": lon % 2,
    }


def device_of(place):
    lat = place["z"] * 8 + (place["y"] // 2) * 4 + place["x"]
    return (lat, (place["y"] % 2) * 2 + place["core"])


def moved(place, dim, delta):
    size = 2 if dim == "core" else 4
    other = dict(place)
    other[dim] = (place[dim] + delta + size) % size
    return device_of(other)


def pick(dim, value):
    if dim == "y":
        if value is None:
            return {"yh": slice(None), "yl": slice(None)}
        return {"yh": pl.ds(value // 2, 1), "yl": pl.ds(value % 2, 1)}
    return {dim: slice(None) if value is None else pl.ds(value, 1)}


def greet(place):
    barrier = pltpu.get_barrier_semaphore()
    others = [moved(place, dim, step) for dim in "xyz" for step in (1, -1, 2)] + [moved(place, "core", 1)]
    lat, lon = device_of(place)
    others += [(lat, (lon + k) % 4) for k in range(1, 4)]
    others += [((lat + step) % 32, (lon + turn) % 4) for step, turn in ((1, 0), (31, 0), (1, 1), (31, 3))]
    for other in others:
        pl.semaphore_signal(barrier, inc=1, device_id=other, device_id_type=MESH)
    pl.semaphore_wait(barrier, len(others))


PARTS = (
    ((0, 3, ("x", "y", "z")), (3, 3, ("y", "z", "x")), (6, 2, ("z", "x", "y"))),
    ((8, 3, ("x", "y", "z")), (11, 3, ("y", "z", "x")), (14, 2, ("z", "x", "y"))),
)


class Gather:
    def __init__(self, place, w, send, recv, number, part):
        self.place, self.w, self.send, self.recv, self.number = place, w, send, recv, number
        first, count, self.order = part
        self.tiles = pl.ds(first, count)

    def region(self, phase, value, half=None, core=None):
        index = {}
        for position, dim in enumerate(self.order):
            if position < phase:
                index.update(pick(dim, None))
            elif position == phase:
                index.update(pick(dim, value))
            else:
                index.update(pick(dim, self.place[dim]))
        rows = slice(None) if half is None else pl.ds(16 * half, 16)
        core = self.place["core"] if core is None else core
        return self.w.at[self.tiles, index["yl"], core, index["z"], index["yh"], index["x"], rows, :]

    def copy(self, k, ref, other):
        return pltpu.make_async_remote_copy(
            src_ref=ref,
            dst_ref=ref,
            send_sem=self.send.at[self.number, k],
            recv_sem=self.recv.at[self.number, k],
            device_id=other,
            device_id_type=MESH,
        )

    def ring(self, phase, k):
        dim = self.order[phase]
        me = self.place[dim]
        if phase < 2:
            return self.copy(4 * phase + k, self.region(phase, me), moved(self.place, dim, (1, -1, 2)[k]))
        other = moved(self.place, dim, 1 if k % 2 == 0 else -1)
        if k < 2:
            return self.copy(4 * phase + k, self.region(phase, me), other)
        return self.copy(4 * phase + k, self.region(phase, (me + 7 - 2 * k) % 4, k - 2), other)

    def arrival(self, phase, k):
        dim = self.order[phase]
        me = self.place[dim]
        source = (me + (3, 1, 2, 2)[k]) % 4
        half = k - 2 if phase == 2 and k > 1 else None
        return self.copy(4 * phase + k, self.region(phase, source, half), moved(self.place, dim, 1))

    def across(self, k, core):
        ref = self.region(2, (self.place[self.order[2]] + (0, 3, 1, 2)[k]) % 4, None, core)
        return self.copy(12 + k, ref, moved(self.place, "core", 1))

    def step(self, s):
        core = self.place["core"]
        if s < 3:
            if s > 0:
                for k in range(3):
                    self.arrival(s - 1, k).wait_recv()
            for k in range(3 if s < 2 else 2):
                self.ring(s, k).start()
            if s == 2:
                self.across(0, core).start()
        elif s == 3:
            for k in range(2):
                self.arrival(2, k).wait_recv()
                self.ring(2, k + 2).start()
                self.across(k + 1, core).start()
        elif s == 4:
            for k in (2, 3):
                self.arrival(2, k).wait_recv()
            self.across(3, core).start()
        else:
            for k in range(4):
                self.across(k, 1 - core).wait_recv()

    def drain(self):
        for phase in range(3):
            for k in range(3 if phase < 2 else 4):
                self.ring(phase, k).wait_send()
        for k in range(4):
            self.across(k, self.place["core"]).wait_send()


def landing_shape(order, phase, columns):
    sizes = {"z": 4, "yh": 2, "x": 4, "yl": 2}
    for dim in order[: phase + 1]:
        for name in ("yh", "yl") if dim == "y" else (dim,):
            sizes[name] = 1
    return (sizes["z"], sizes["yh"], sizes["x"], sizes["yl"], 16, columns)


class Reduce:
    def __init__(self, place, p, landing, send, recv, order):
        self.place, self.p, self.landing = place, p, landing
        self.send, self.recv, self.order = send, recv, order

    def region(self, phase, value):
        index = {}
        for position, dim in enumerate(self.order):
            if position < phase:
                index.update(pick(dim, self.place[dim]))
            elif position == phase:
                index.update(pick(dim, value))
            else:
                index.update(pick(dim, None))
        return (self.place["core"], index["z"], index["yh"], index["x"], index["yl"])

    def copy(self, k, src, other):
        return pltpu.make_async_remote_copy(
            src_ref=src,
            dst_ref=self.landing[k],
            send_sem=self.send.at[k],
            recv_sem=self.recv.at[k],
            device_id=other,
            device_id_type=MESH,
        )

    def across(self):
        return self.copy(9, self.p.at[1 - self.place["core"]], moved(self.place, "core", 1))

    def ring(self, phase, k):
        dim = self.order[phase]
        step = (1, -1, 2)[k]
        target = (self.place[dim] + step + 4) % 4
        return self.copy(3 * phase + k, self.p.at[self.region(phase, target)], moved(self.place, dim, step))

    def step(self, s):
        if s == 0:
            self.across().start()
        elif s == 1:
            self.across().wait_recv()
            core = self.place["core"]
            for z in range(4):
                total = self.p[core, z].astype(F32) + self.landing[9][z].astype(F32)
                self.p[core, z] = total.astype(BF16)
        else:
            for k in range(3):
                self.ring(s - 2, k).wait_recv()
            region = self.region(s - 2, self.place[self.order[s - 2]])
            total = self.p[region].astype(F32)
            for k in range(3):
                total = total + self.landing[3 * (s - 2) + k][...].astype(F32)
            self.p[region] = total.astype(BF16)
        if 0 < s < 4:
            for k in range(3):
                self.ring(s - 1, k).start()

    def drain(self):
        for phase in range(3):
            for k in range(3):
                self.ring(phase, k).wait_send()
        self.across().wait_send()

    def result(self):
        y = self.place["y"]
        return self.p[self.place["core"], self.place["z"], y // 2, self.place["x"], y % 2].astype(F32)


def landing_shapes(order, columns):
    shapes = [pltpu.VMEM(landing_shape(order, phase, columns), BF16) for phase in range(3) for _ in range(3)]
    return shapes + [pltpu.VMEM((4, 2, 4, 2, 16, columns), BF16)]


def spread_queries(lq):
    row = lax.broadcasted_iota(jnp.int32, (128, D), 0)
    head = lax.broadcasted_iota(jnp.int32, (128, D), 1) // 64
    total = jnp.zeros((128, D), F32)
    for q in range(LATENT):
        total = total + jnp.where(row == q * HEADS + head, lq[q : q + 1, :].astype(F32), 0.0)
    return total.astype(BF16)


def finish_gradients(factor, sums, lq, grad_key, grad_value, grad_out):
    first, second, third = sums
    grad_value[:, 0:256] = first[:8, :256] * factor
    grad_value[:, 256:512] = second[:8] * factor
    grad_value[:, 512:768] = first[8:, :256] * factor
    grad_value[:, 768:1024] = second[8:] * factor
    grad_out[:, 0:512] = third[:8] * factor
    grad_out[:, 512:1024] = third[8:] * factor
    small = first[:8, 256:] * (factor * 0.125)
    high = small.astype(BF16)
    low = (small - high.astype(F32)).astype(BF16)
    queries = spread_queries(lq)
    grad_key[...] = dot(high, queries) + dot(low, queries)


def looped(count, body, hooks):
    def step(i, _):
        body(i)
        for at, hook in hooks.items():
            pl.when(i == at)(hook)
        return 0

    lax.fori_loop(0, count, step, 0)


def group_at(g):
    return g // 4, pl.ds(pl.multiple_of((g % 4) * 16, 16), 16)


def spread_heads(spread):
    row = lax.broadcasted_iota(jnp.int32, (128, 768), 0)
    column = lax.broadcasted_iota(jnp.int32, (128, 768), 1)
    for cb in range(4):
        hit = row == (column // 256) * HEADS + cb * 4 + (column % 256) // 64
        spread[cb] = jnp.where(hit, 1.0, 0.0).astype(BF16)


def key_queries(kw, lq, kq):
    queries = spread_queries(lq)

    def rows(i, _):
        at = pl.ds(pl.multiple_of(i * 256, 256), 256)
        total = dot(kw[at, :], queries, ((1,), (1,))) * 0.125
        high = total.astype(BF16)
        kq[0, at, :] = high
        kq[1, at, :] = (total - high.astype(F32)).astype(BF16)
        return 0

    lax.fori_loop(0, 4, rows, 0)


def resample_project(tok, vw, kq, values, logits, hooks):
    def project(r):
        rows = tok[r].reshape(LEV * 64, D)
        for nb in range(4):
            columns = slice(nb * 256, (nb + 1) * 256)
            values[r, :, :, columns] = dot(rows, vw[:, columns]).astype(BF16).reshape(LEV, 64, 256)
        logits[r] = (dot(rows, kq[0]) + dot(rows, kq[1])).reshape(LEV, 64, 128)

    looped(2, project, hooks)


def resample_softmax(logits, weights):
    def group(g, _):
        r, c = group_at(g)
        x = logits[r, :, c]
        x = jnp.exp(x - jnp.max(x, axis=0, keepdims=True))
        x = x / jnp.sum(x, axis=0, keepdims=True)
        logits[r, :, c] = x
        weights[r, :, c] = x.astype(BF16)
        return 0

    lax.fori_loop(0, GROUPS, group, 0)


def resample_cotangents(grad, ro, d_attended):
    rows = grad[...].reshape(384, D)
    for nb in range(4):
        columns = slice(nb * 256, (nb + 1) * 256)
        part = dot(rows, ro[columns, :], ((1,), (1,)))
        d_attended[:, :, :, columns] = part.astype(BF16).reshape(2, LATENT, 64, 256)


def resample_mix(chip, values, weights, probs, spread, d_attended, attended, d_logits, hooks):
    def group(g):
        r, tile = g % 2, ((chip + 1 + g // 4) % 2) * 2 + (g // 2) % 2
        c = pl.ds(pl.multiple_of(tile * 16, 16), 16)
        w = weights[r, :, c].reshape(208, 128)
        d_weights = jnp.zeros((208, 128), F32)
        for cb in range(4):
            columns = slice(cb * 256, (cb + 1) * 256)
            wide = dot(w, spread[cb])
            v = values[r, :, c, columns].astype(F32)
            d_v = jnp.zeros((LEV, 16, 256), F32)
            products = []
            for q in range(LATENT):
                wq = wide[:, q * 256 : (q + 1) * 256].reshape(LEV, 16, 256)
                da = d_attended[r, q, c, columns].astype(F32)[None]
                attended[r, q, c, columns] = jnp.sum(wq * v, axis=0).astype(BF16)
                d_v = d_v + wq * da
                products.append((v * da).astype(BF16).reshape(208, 256))
            values[r, :, c, columns] = d_v.astype(BF16)
            d_weights = d_weights + dot(jnp.concatenate(products, axis=1), spread[cb], ((1,), (1,)))
        p = probs[r, :, c]
        dw = d_weights.reshape(LEV, 16, 128)
        d_logits[r, :, c] = (p * (dw - jnp.sum(p * dw, axis=0, keepdims=True))).astype(BF16)

    looped(GROUPS, group, hooks)


def resample_latents(chip, attended, ro, lq, latents):
    cells = pl.ds(pl.multiple_of(chip * 32, 32), 32)
    rows = attended[:, :, cells, :].reshape(192, D)
    for nb in range(4):
        columns = slice(nb * 256, (nb + 1) * 256)
        part = dot(rows, ro[:, columns]).reshape(2, LATENT, 32, 256)
        part = part + lq[:, columns].astype(F32)[None, :, None, :]
        latents[:, :, cells, columns] = part.astype(BF16)


def pack_pair(left, right, p, z, columns):
    left = left.reshape(2, 4, 2, 2, 8, left.shape[-1])
    right = right.reshape(2, 4, 2, 2, 8, right.shape[-1])
    for core in range(2):
        both = jnp.concatenate([left[:, :, :, core], right[:, :, :, core]], axis=3)
        p[core, z, :, :, :, :, columns] = both.astype(BF16)


def out_gradient(grad, attended, turned, packed):
    def block(z):
        columns = pl.ds(pl.multiple_of(z * 256, 256), 256)
        turned[:, :384] = attended[:, :, :, columns].reshape(384, 256).T
        for nb in range(2):
            halves = []
            for half in range(2):
                c = slice(half * 512 + nb * 256, half * 512 + (nb + 1) * 256)
                halves.append(dot(turned[:, :384], grad[:, :, :, c].reshape(384, 256)))
            pack_pair(halves[0], halves[1], packed, z, slice(nb * 256, (nb + 1) * 256))

    looped(4, block, {})


def token_gradients(tok, d_values, d_logits, turned, packed, hooks):
    def block(z):
        columns = pl.ds(pl.multiple_of(z * 256, 256), 256)
        turned[...] = tok[:, :, :, columns].reshape(GROUPS * 208, 256).T
        for nb in range(2):
            halves = []
            for half in range(2):
                c = slice(half * 512 + nb * 256, half * 512 + (nb + 1) * 256)
                halves.append(dot(turned[...], d_values[:, :, :, c].reshape(GROUPS * 208, 256)))
            pack_pair(halves[0], halves[1], packed[nb], z, slice(0, 256))
        small = dot(turned[...], d_logits[...].reshape(GROUPS * 208, 128))
        pack_pair(small, jnp.zeros_like(small), packed[0], z, slice(256, 384))

    looped(4, block, hooks)


def normalise(window, gain, normed):
    for win in range(4):
        values = window(win)
        centred = values - jnp.mean(values, axis=-1, keepdims=True)
        spread = jnp.mean(centred * centred, axis=-1, keepdims=True)
        normed[win * 96 : (win + 1) * 96, :] = (centred * lax.rsqrt(spread + 1e-05) * gain).astype(BF16)


def weight_block(w, layer, block, j):
    tile = layer * 8 + block
    return jnp.concatenate([w[tile + 4 * i, j // 2, j % 2].reshape(D, 128) for i in range(2)], axis=1)


def attend_heads(j, layer, w, normed, bias, mixed):
    queries, keys, values = (dot(normed[...], weight_block(w, layer, block, j)) for block in range(3))
    queries, keys, values = (queries * 0.125).astype(BF16), keys.astype(BF16), values.astype(BF16)
    left = lax.broadcasted_iota(jnp.int32, (96, 128), 1) < 64
    columns = pl.ds(pl.multiple_of(j * 256, 256), 256)
    none = jnp.zeros((96, 128), BF16)
    for win in range(4):
        rows = slice(win * 96, (win + 1) * 96)
        q, k, v = queries[rows], keys[rows], values[rows]
        stacked = []
        for h in range(4):
            half = q[:, 128 * (h // 2) : 128 * (h // 2 + 1)]
            half = jnp.where(left, half, none) if h % 2 == 0 else jnp.where(left, none, half)
            stacked.append(jnp.concatenate([half, none] if h < 2 else [none, half], axis=1))
        logits = dot(jnp.concatenate(stacked, axis=0), k, ((1,), (1,)))
        if bias is not None:
            logits = (logits.reshape(4, 96, 96) + bias[win][None]).reshape(384, 96)
        e = jnp.exp(logits - jnp.max(logits, axis=-1, keepdims=True))
        e = e * (1.0 / jnp.sum(e, axis=-1, keepdims=True))
        out = dot(e.astype(BF16), v)
        pairs = [
            jnp.where(left, out[0:96, :128], out[96:192, :128]),
            jnp.where(left, out[192:288, 128:], out[288:384, 128:]),
        ]
        mixed[rows, columns] = jnp.concatenate(pairs, axis=1).astype(BF16)


def label_mask(label, place, bias):
    lat = device_of(place)[0]
    row = lax.broadcasted_iota(jnp.int32, (8, 16), 0) + lat * 8
    codes = label[...].astype(F32) * 2.0 + jnp.where(row >= 8 * 32 - 2, 2.0, 1.0)
    token = lax.broadcasted_iota(jnp.int32, (96, 16), 0)
    column = lax.broadcasted_iota(jnp.int32, (96, 16), 1)
    ones = jnp.ones((96, 16), F32)
    for win in range(4):
        wr, wc = divmod(win, 2)
        own = jnp.zeros((96, 16), F32)
        for r in range(4):
            hit = (token // 24 == r) & (column == 8 * wc + token % 8)
            own = own + jnp.where(hit, codes[4 * wr + r : 4 * wr + r + 1, :], 0.0)
        one = dot(own, ones, ((1,), (1,)))
        other = dot(ones, own, ((1,), (1,)))
        bias[win] = jnp.where(one == other, 0.0, -1e30)


def output_update(w, layer, j, mixed):
    return dot(mixed[...], weight_block(w, layer, 3, j)).reshape(2, 2, 4, LATENT, 8, 256)


def tile_rows(x, wr, columns=slice(None)):
    return x[4 * wr : 4 * wr + 4, :, :, columns].astype(F32)


def first_sublayer(x, gain, w, normed, mixed, middle, hooks):
    def window(win):
        wr, wc = divmod(win, 2)
        return tile_rows(x, wr)[:, :, 8 * wc : 8 * wc + 8].reshape(96, D)

    normalise(window, gain, normed)
    looped(4, lambda j: attend_heads(j, 0, w, normed, None, mixed), hooks)
    for j in range(4):
        columns = slice(j * 256, (j + 1) * 256)
        update = output_update(w, 0, j, mixed)
        for wr in range(2):
            both = jnp.concatenate([update[wr, 0], update[wr, 1]], axis=2)
            middle[4 * wr : 4 * wr + 4, :, 0:16, columns] = tile_rows(x, wr, columns) + both


def second_sublayer(middle, gain, w, normed, mixed, bias, out, hooks):
    def window(win):
        wr, wc = divmod(win, 2)
        return middle[4 * wr + 2 : 4 * wr + 6, :, 8 * wc + 4 : 8 * wc + 12, :].reshape(96, D)

    normalise(window, gain, normed)
    looped(4, lambda j: attend_heads(j, 1, w, normed, bias, mixed), hooks)
    for j in range(4):
        columns = slice(j * 256, (j + 1) * 256)
        update = output_update(w, 1, j, mixed)
        for wr in range(2):
            halves = []
            for wc in range(2):
                own = middle[4 * wr + 2 : 4 * wr + 6, :, 8 * wc + 4 : 8 * wc + 12, columns]
                halves.append(own + update[wr, wc])
            both = jnp.concatenate(halves, axis=2).astype(BF16)
            out[4 * wr : 4 * wr + 4, :, :, columns] = both


class Edges:
    def __init__(self, place, middle, rows_out, columns_out, rows_in, columns_in, corner_in, send, recv):
        lat, lon = device_of(place)
        above, beside = (lat + 31) % 32, (lon + 3) % 4
        self.middle, self.rows_out, self.columns_out = middle, rows_out, columns_out
        self.rows_in, self.columns_in, self.corner_in = rows_in, columns_in, corner_in
        plan = (
            (rows_out, rows_in, (above, lon)),
            (columns_out, columns_in, (lat, beside)),
            (columns_out.at[pl.ds(0, 32)], corner_in, (above, beside)),
        )
        self.copies = [
            pltpu.make_async_remote_copy(
                src_ref=src,
                dst_ref=dst,
                send_sem=send.at[k],
                recv_sem=recv.at[k],
                device_id=other,
                device_id_type=MESH,
            )
            for k, (src, dst, other) in enumerate(plan)
        ]

    def start(self):
        middle = self.middle
        for r in range(2):
            self.rows_out[r] = middle[r, :, 0:16].reshape(48, D).astype(BF16)
        for part in range(6):
            cells = [divmod(part * 4 + i, LATENT) for i in range(4)]
            rows = jnp.concatenate([middle[r, q, 0:4] for r, q in cells], axis=0)
            self.columns_out[part * 16 : (part + 1) * 16] = rows.astype(BF16)
        for copy in self.copies:
            copy.start()

    def finish(self):
        middle = self.middle
        for copy in self.copies:
            copy.wait_recv()
        for r in range(2):
            middle[8 + r, :, 0:16] = self.rows_in[r].astype(F32).reshape(LATENT, 16, D)
        for part in range(6):
            rows = self.columns_in[part * 16 : (part + 1) * 16].astype(F32)
            for i in range(4):
                r, q = divmod(part * 4 + i, LATENT)
                middle[r, q, 16:20] = rows[i * 4 : (i + 1) * 4]
        for part in range(2):
            rows = self.corner_in[part * 16 : (part + 1) * 16].astype(F32)
            for i in range(4):
                r, q = divmod(part * 4 + i, LATENT)
                if r < 2:
                    middle[8 + r, q, 16:20] = rows[i * 4 : (i + 1) * 4]

    def drain(self):
        for copy in self.copies:
            copy.wait_send()


class Tiles:
    def __init__(self, place, latents, x, send, recv, own):
        lat, lon = device_of(place)

        def at(column):
            return pl.ds(pl.multiple_of(column * 16, 16), 16)

        self.own = pltpu.make_async_copy(latents.at[:, :, at(lon)], x.at[pl.ds(2 * lon, 2)], own)
        chip, core = lon // 2, lon % 2
        partners = ((1 - chip) * 2 + core, (1 - chip) * 2 + 1 - core, chip * 2 + 1 - core)
        self.out, self.arriving = [], []
        for k, other in enumerate(partners):
            for copies, row in ((self.out, lon), (self.arriving, other)):
                copies.append(
                    pltpu.make_async_remote_copy(
                        src_ref=latents.at[:, :, at(other)],
                        dst_ref=x.at[pl.ds(2 * row, 2)],
                        send_sem=send.at[k],
                        recv_sem=recv.at[k],
                        device_id=(lat, other),
                        device_id_type=MESH,
                    )
                )

    def start(self, here):
        if here:
            self.out[2].start()
            self.own.start()
        else:
            self.out[0].start()
            self.out[1].start()

    def finish(self):
        self.own.wait()
        for copy in self.arriving:
            copy.wait_recv()

    def drain(self):
        for copy in self.out:
            copy.wait_send()


WIDTHS = (384, 256, 512)
REDUCE_ORDERS = (("x", "y", "z"), ("y", "z", "x"), ("z", "x", "y"))


def kernel(factor, tokens, grads, kw_far, vw_far, ro_far, lq, gains, qkv, ow, label, *refs):
    out, grad_key, grad_value, grad_out = refs[:4]
    w, latents, x, rows_out, columns_out, rows_in, columns_in, corner_in = refs[4:12]
    packed, landing = refs[12:15], refs[15:45]
    g_send, g_recv, r_send, r_recv, t_send, t_recv, e_send, e_recv, near = refs[45:]
    place = my_place()
    y = place["y"]
    own = []
    for layer in range(2):
        for half in range(2):
            columns = pl.ds(128 * half, 128)
            tile = layer * 8 + half * 4
            mine = (y % 2, place["core"], place["z"], y // 2, place["x"])
            own.append((qkv.at[layer, :, :, columns], w.at[(pl.ds(tile, 3),) + mine]))
            own.append((ow.at[layer, :, columns], w.at[(tile + 3,) + mine]))
    own = [pltpu.make_async_copy(src, dst, near.at[i]) for i, (src, dst) in enumerate(own)]
    for copy in own:
        copy.start()
    layers = [
        [Gather(place, w, g_send, g_recv, 3 * layer + i, part) for i, part in enumerate(PARTS[layer])]
        for layer in range(2)
    ]
    sums = [
        Reduce(place, packed[i], landing[10 * i : 10 * i + 10], r_send.at[i], r_recv.at[i], REDUCE_ORDERS[i])
        for i in range(3)
    ]
    tiles = Tiles(place, latents, x, t_send, t_recv, near.at[8])

    def gathered(layer, s):
        def hook():
            for part in layers[layer]:
                part.step(s)

        return hook

    def reduced(s, *parts):
        def hook():
            for part in parts:
                sums[part].step(s)

        return hook

    def both(*hooks):
        def hook():
            for one in hooks:
                one()

        return hook

    def resampler(tok, grad, kw, vw, ro, kq, values, logits, weights, spread, d_att, att, d_logits, turned):
        pairs = ((kw_far, kw), (tokens, tok), (vw_far, vw), (grads, grad), (ro_far, ro))
        copies = [pltpu.make_async_copy(far, here, near.at[9 + i]) for i, (far, here) in enumerate(pairs)]
        for copy in copies:
            copy.start()
        greet(place)
        for copy in own:
            copy.wait()
        gathered(0, 0)()
        gathered(1, 0)()
        spread_heads(spread)
        copies[0].wait()
        key_queries(kw, lq, kq)
        gathered(0, 1)()
        copies[1].wait()
        copies[2].wait()
        resample_project(tok, vw, kq, values, logits, {1: gathered(0, 2)})
        resample_softmax(logits, weights)
        copies[3].wait()
        copies[4].wait()
        resample_cotangents(grad, ro, d_att)
        chip = y % 2

        def first_half():
            resample_latents(1 - chip, att, ro, lq, latents)
            tiles.start(False)

        hooks = {1: gathered(1, 1), 3: first_half, 7: gathered(0, 3)}
        resample_mix(chip, values, weights, logits, spread, d_att, att, d_logits, hooks)
        resample_latents(chip, att, ro, lq, latents)
        tiles.start(True)
        out_gradient(grad, att, turned, packed[2])
        gathered(1, 2)()
        reduced(0, 2)()
        token_gradients(tok, values, d_logits, turned, packed, {1: gathered(0, 4), 2: reduced(1, 2)})

    pl.run_scoped(
        resampler,
        pltpu.VMEM((2, LEV, 64, D), BF16),
        pltpu.VMEM((2, LATENT, 64, D), BF16),
        pltpu.VMEM((D, D), BF16),
        pltpu.VMEM((D, D), BF16),
        pltpu.VMEM((D, D), BF16),
        pltpu.VMEM((2, D, 128), BF16),
        pltpu.VMEM((2, LEV, 64, D), BF16),
        pltpu.VMEM((2, LEV, 64, 128), F32),
        pltpu.VMEM((2, LEV, 64, 128), BF16),
        pltpu.VMEM((4, 128, 768), BF16),
        pltpu.VMEM((2, LATENT, 64, D), BF16),
        pltpu.VMEM((2, LATENT, 64, D), BF16),
        pltpu.VMEM((2, LEV, 64, 128), BF16),
        pltpu.VMEM((256, GROUPS * 208), BF16),
    )
    reduced(0, 0, 1)()

    def backbone(middle, normed, mixed, bias):
        edges = Edges(place, middle, rows_out, columns_out, rows_in, columns_in, corner_in, e_send, e_recv)
        label_mask(label, place, bias)
        gathered(0, 5)()
        tiles.finish()
        first_sublayer(x, gains[0:1, :], w, normed, mixed, middle, {2: reduced(1, 0, 1), 3: gathered(1, 3)})
        edges.start()
        reduced(2, 2)()
        gathered(1, 4)()
        edges.finish()
        gathered(1, 5)()
        hooks = {0: reduced(2, 0, 1), 1: reduced(3, 2), 2: reduced(3, 0, 1), 3: reduced(4, 2)}
        second_sublayer(middle, gains[1:2, :], w, normed, mixed, bias, out, hooks)
        reduced(4, 0, 1)()
        edges.drain()

    pl.run_scoped(
        backbone,
        pltpu.VMEM((10, LATENT, 24, D), F32),
        pltpu.VMEM((384, D), BF16),
        pltpu.VMEM((384, D), BF16),
        pltpu.VMEM((4, 96, 96), F32),
    )
    finish_gradients(factor, [part.result() for part in sums], lq, grad_key, grad_value, grad_out)
    tiles.drain()
    for part in layers[0] + layers[1] + sums:
        part.drain()


def whole(factor, tokens, grads, kw, vw, ro, lq, gains, qkv, ow, label):
    vmem, far = pl.BlockSpec(memory_space=pltpu.VMEM), pl.BlockSpec(memory_space=pl.ANY)
    landings = []
    for order, width in zip(REDUCE_ORDERS, WIDTHS):
        landings += landing_shapes(order, width)
    dma = pltpu.SemaphoreType.DMA
    return pl.pallas_call(
        functools.partial(kernel, factor),
        out_shape=[jax.ShapeDtypeStruct((8, LATENT, 16, D), BF16)] + [jax.ShapeDtypeStruct((8, D), F32)] * 3,
        in_specs=[far] * 5 + [vmem, vmem, far, far, vmem],
        out_specs=[vmem] * 4,
        scratch_shapes=[
            pltpu.VMEM((16, 2, 2, 4, 2, 4, 32, 128), BF16),
            pltpu.VMEM((2, LATENT, 64, D), BF16),
            pltpu.VMEM((8, LATENT, 16, D), BF16),
            pltpu.VMEM((2, 48, D), BF16),
            pltpu.VMEM((96, D), BF16),
            pltpu.VMEM((2, 48, D), BF16),
            pltpu.VMEM((96, D), BF16),
            pltpu.VMEM((32, D), BF16),
        ]
        + [pltpu.VMEM((2, 4, 2, 4, 2, 16, width), BF16) for width in WIDTHS]
        + landings
        + [dma((6, 16)), dma((6, 16)), dma((3, 10)), dma((3, 10))]
        + [dma((3,)), dma((3,)), dma((3,)), dma((3,)), dma((14,))],
        compiler_params=pltpu.CompilerParams(collective_id=0, has_side_effects=True, vmem_limit_bytes=63 * MIB),
    )(tokens, grads, kw, vw, ro, lq, gains, qkv, ow, label)


def hand_over_kernel(*refs):
    count = len(refs) // 2
    for i in range(count):
        refs[count + i][...] = refs[i][...]


def hand_over(results):
    return pl.pallas_call(
        hand_over_kernel,
        out_shape=[jax.ShapeDtypeStruct(r.shape, r.dtype) for r in results],
        in_specs=[pl.BlockSpec(memory_space=pltpu.VMEM)] * len(results),
        out_specs=[pl.BlockSpec(memory_space=pltpu.VMEM)] * len(results),
    )(*results)


def local(
    level_tokens,
    latent_query,
    key_weight,
    value_weight,
    resample_out,
    norm_gain,
    qkv_weight,
    out_weight,
    window_label,
    grad_latents,
):
    factor = (2 * 64 * lax.axis_size("lat") * lax.axis_size("lon")) ** (-0.5)
    results = whole(
        factor,
        level_tokens.swapaxes(1, 2),
        grad_latents.swapaxes(1, 2),
        key_weight,
        value_weight,
        resample_out,
        latent_query,
        norm_gain,
        qkv_weight.swapaxes(1, 2),
        out_weight,
        window_label,
    )
    out, grad_key, grad_value, grad_out = hand_over(results)
    return (out.swapaxes(1, 2), grad_key, grad_value, grad_out)


def solution(mesh):
    in_specs = (
        P(("lat", "lon"), None, None, None),
        P(),
        P(),
        P(),
        P(),
        P(),
        P(None, "lat", None, "lon"),
        P(None, "lat", "lon"),
        P("lat", "lon"),
        P(("lat", "lon"), None, None, None),
    )
    out_specs = (
        P("lat", "lon", None, None),
        P(("lat", "lon"), None),
        P(("lat", "lon"), None),
        P(("lat", "lon"), None),
    )
    return jax.shard_map(local, mesh=mesh, in_specs=in_specs, out_specs=out_specs, check_vma=False)
```

```python
import functools

import jax
import jax.numpy as jnp
from jax import lax
from jax.experimental import pallas as pl
from jax.experimental.pallas import tpu as pltpu
from jax.sharding import PartitionSpec as P

MESH = pl.DeviceIdType.MESH
F32, BF16 = jnp.float32, jnp.bfloat16
D = 1024
HEADS = 16
LEV = 13
LATENT = 3
GROUPS = 8
MIB = 1024 * 1024


def dot(a, b, dims=((1,), (0,))):
    return lax.dot_general(a, b, (dims, ((), ())), preferred_element_type=F32)


def my_place():
    lat, lon = lax.axis_index("lat"), lax.axis_index("lon")
    return {
        "z": lat // 8,
        "y": ((lat // 4) % 2) * 2 + lon // 2,
        "x": lat % 4,
        "core": lon % 2,
    }


def device_of(place):
    lat = place["z"] * 8 + (place["y"] // 2) * 4 + place["x"]
    return (lat, (place["y"] % 2) * 2 + place["core"])


def moved(place, dim, delta):
    size = 2 if dim == "core" else 4
    other = dict(place)
    other[dim] = (place[dim] + delta + size) % size
    return device_of(other)


def pick(dim, value):
    if dim == "y":
        if value is None:
            return {"yh": slice(None), "yl": slice(None)}
        return {"yh": pl.ds(value // 2, 1), "yl": pl.ds(value % 2, 1)}
    return {dim: slice(None) if value is None else pl.ds(value, 1)}


def greet(place):
    barrier = pltpu.get_barrier_semaphore()
    others = [moved(place, dim, step) for dim in "xyz" for step in (1, -1, 2)] + [moved(place, "core", 1)]
    lat, lon = device_of(place)
    others += [(lat, (lon + k) % 4) for k in range(1, 4)]
    others += [((lat + step) % 32, (lon + turn) % 4) for step, turn in ((1, 0), (31, 0), (1, 1), (31, 3))]
    for other in others:
        pl.semaphore_signal(barrier, inc=1, device_id=other, device_id_type=MESH)
    pl.semaphore_wait(barrier, len(others))


PARTS = (
    ((0, 3, ("x", "y", "z")), (3, 3, ("y", "z", "x")), (6, 2, ("z", "x", "y"))),
    ((8, 3, ("x", "y", "z")), (11, 3, ("y", "z", "x")), (14, 2, ("z", "x", "y"))),
)


class Gather:
    def __init__(self, place, w, send, recv, number, part):
        self.place, self.w, self.send, self.recv, self.number = place, w, send, recv, number
        first, count, self.order = part
        self.tiles = pl.ds(first, count)

    def region(self, phase, value, half=None, core=None):
        index = {}
        for position, dim in enumerate(self.order):
            if position < phase:
                index.update(pick(dim, None))
            elif position == phase:
                index.update(pick(dim, value))
            else:
                index.update(pick(dim, self.place[dim]))
        rows = slice(None) if half is None else pl.ds(16 * half, 16)
        core = self.place["core"] if core is None else core
        return self.w.at[self.tiles, index["yl"], core, index["z"], index["yh"], index["x"], rows, :]

    def copy(self, k, ref, other):
        return pltpu.make_async_remote_copy(
            src_ref=ref,
            dst_ref=ref,
            send_sem=self.send.at[self.number, k],
            recv_sem=self.recv.at[self.number, k],
            device_id=other,
            device_id_type=MESH,
        )

    def ring(self, phase, k):
        dim = self.order[phase]
        me = self.place[dim]
        if phase < 2:
            return self.copy(4 * phase + k, self.region(phase, me), moved(self.place, dim, (1, -1, 2)[k]))
        other = moved(self.place, dim, 1 if k % 2 == 0 else -1)
        if k < 2:
            return self.copy(4 * phase + k, self.region(phase, me), other)
        return self.copy(4 * phase + k, self.region(phase, (me + 7 - 2 * k) % 4, k - 2), other)

    def arrival(self, phase, k):
        dim = self.order[phase]
        me = self.place[dim]
        source = (me + (3, 1, 2, 2)[k]) % 4
        half = k - 2 if phase == 2 and k > 1 else None
        return self.copy(4 * phase + k, self.region(phase, source, half), moved(self.place, dim, 1))

    def across(self, k, core):
        ref = self.region(2, (self.place[self.order[2]] + (0, 3, 1, 2)[k]) % 4, None, core)
        return self.copy(12 + k, ref, moved(self.place, "core", 1))

    def step(self, s):
        core = self.place["core"]
        if s < 3:
            if s > 0:
                for k in range(3):
                    self.arrival(s - 1, k).wait_recv()
            for k in range(3 if s < 2 else 2):
                self.ring(s, k).start()
            if s == 2:
                self.across(0, core).start()
        elif s == 3:
            for k in range(2):
                self.arrival(2, k).wait_recv()
                self.ring(2, k + 2).start()
                self.across(k + 1, core).start()
        elif s == 4:
            for k in (2, 3):
                self.arrival(2, k).wait_recv()
            self.across(3, core).start()
        else:
            for k in range(4):
                self.across(k, 1 - core).wait_recv()

    def drain(self):
        for phase in range(3):
            for k in range(3 if phase < 2 else 4):
                self.ring(phase, k).wait_send()
        for k in range(4):
            self.across(k, self.place["core"]).wait_send()


def landing_shape(order, phase, columns):
    sizes = {"z": 4, "yh": 2, "x": 4, "yl": 2}
    for dim in order[: phase + 1]:
        for name in ("yh", "yl") if dim == "y" else (dim,):
            sizes[name] = 1
    return (sizes["z"], sizes["yh"], sizes["x"], sizes["yl"], 16, columns)


class Reduce:
    def __init__(self, place, p, landing, send, recv, order):
        self.place, self.p, self.landing = place, p, landing
        self.send, self.recv, self.order = send, recv, order

    def region(self, phase, value):
        index = {}
        for position, dim in enumerate(self.order):
            if position < phase:
                index.update(pick(dim, self.place[dim]))
            elif position == phase:
                index.update(pick(dim, value))
            else:
                index.update(pick(dim, None))
        return (self.place["core"], index["z"], index["yh"], index["x"], index["yl"])

    def copy(self, k, src, other):
        return pltpu.make_async_remote_copy(
            src_ref=src,
            dst_ref=self.landing[k],
            send_sem=self.send.at[k],
            recv_sem=self.recv.at[k],
            device_id=other,
            device_id_type=MESH,
        )

    def across(self):
        return self.copy(9, self.p.at[1 - self.place["core"]], moved(self.place, "core", 1))

    def ring(self, phase, k):
        dim = self.order[phase]
        step = (1, -1, 2)[k]
        target = (self.place[dim] + step + 4) % 4
        return self.copy(3 * phase + k, self.p.at[self.region(phase, target)], moved(self.place, dim, step))

    def step(self, s):
        if s == 0:
            self.across().start()
        elif s == 1:
            self.across().wait_recv()
            core = self.place["core"]
            for z in range(4):
                total = self.p[core, z].astype(F32) + self.landing[9][z].astype(F32)
                self.p[core, z] = total.astype(BF16)
        else:
            for k in range(3):
                self.ring(s - 2, k).wait_recv()
            region = self.region(s - 2, self.place[self.order[s - 2]])
            total = self.p[region].astype(F32)
            for k in range(3):
                total = total + self.landing[3 * (s - 2) + k][...].astype(F32)
            self.p[region] = total.astype(BF16)
        if 0 < s < 4:
            for k in range(3):
                self.ring(s - 1, k).start()

    def drain(self):
        for phase in range(3):
            for k in range(3):
                self.ring(phase, k).wait_send()
        self.across().wait_send()

    def result(self):
        y = self.place["y"]
        return self.p[self.place["core"], self.place["z"], y // 2, self.place["x"], y % 2].astype(F32)


def landing_shapes(order, columns):
    shapes = [pltpu.VMEM(landing_shape(order, phase, columns), BF16) for phase in range(3) for _ in range(3)]
    return shapes + [pltpu.VMEM((4, 2, 4, 2, 16, columns), BF16)]


def spread_queries(lq):
    row = lax.broadcasted_iota(jnp.int32, (128, D), 0)
    head = lax.broadcasted_iota(jnp.int32, (128, D), 1) // 64
    total = jnp.zeros((128, D), F32)
    for q in range(LATENT):
        total = total + jnp.where(row == q * HEADS + head, lq[q : q + 1, :].astype(F32), 0.0)
    return total.astype(BF16)


def finish_gradients(factor, sums, lq, grad_key, grad_value, grad_out):
    first, second, third = sums
    grad_value[:, 0:256] = first[:8, :256] * factor
    grad_value[:, 256:512] = second[:8] * factor
    grad_value[:, 512:768] = first[8:, :256] * factor
    grad_value[:, 768:1024] = second[8:] * factor
    grad_out[:, 0:512] = third[:8] * factor
    grad_out[:, 512:1024] = third[8:] * factor
    small = first[:8, 256:] * (factor * 0.125)
    high = small.astype(BF16)
    low = (small - high.astype(F32)).astype(BF16)
    queries = spread_queries(lq)
    grad_key[...] = dot(high, queries) + dot(low, queries)


def looped(count, body, hooks):
    def step(i, _):
        body(i)
        for at, hook in hooks.items():
            pl.when(i == at)(hook)
        return 0

    lax.fori_loop(0, count, step, 0)


def group_at(g):
    return g // 4, pl.ds(pl.multiple_of((g % 4) * 16, 16), 16)


def spread_heads(spread):
    row = lax.broadcasted_iota(jnp.int32, (128, 768), 0)
    column = lax.broadcasted_iota(jnp.int32, (128, 768), 1)
    for cb in range(4):
        hit = row == (column // 256) * HEADS + cb * 4 + (column % 256) // 64
        spread[cb] = jnp.where(hit, 1.0, 0.0).astype(BF16)


def key_queries(kw, lq, kq):
    queries = spread_queries(lq)

    def rows(i, _):
        at = pl.ds(pl.multiple_of(i * 256, 256), 256)
        total = dot(kw[at, :], queries, ((1,), (1,))) * 0.125
        high = total.astype(BF16)
        kq[0, at, :] = high
        kq[1, at, :] = (total - high.astype(F32)).astype(BF16)
        return 0

    lax.fori_loop(0, 4, rows, 0)


def resample_project(tok, vw, kq, values, logits, hooks):
    def project(r):
        rows = tok[r].reshape(LEV * 64, D)
        for nb in range(4):
            columns = slice(nb * 256, (nb + 1) * 256)
            values[r, :, :, columns] = dot(rows, vw[:, columns]).astype(BF16).reshape(LEV, 64, 256)
        logits[r] = (dot(rows, kq[0]) + dot(rows, kq[1])).reshape(LEV, 64, 128)

    looped(2, project, hooks)


def resample_softmax(logits, weights):
    def group(g, _):
        r, c = group_at(g)
        x = logits[r, :, c]
        x = jnp.exp(x - jnp.max(x, axis=0, keepdims=True))
        x = x / jnp.sum(x, axis=0, keepdims=True)
        logits[r, :, c] = x
        weights[r, :, c] = x.astype(BF16)
        return 0

    lax.fori_loop(0, GROUPS, group, 0)


def resample_cotangents(grad, ro, d_attended):
    rows = grad[...].reshape(384, D)
    for nb in range(4):
        columns = slice(nb * 256, (nb + 1) * 256)
        part = dot(rows, ro[columns, :], ((1,), (1,)))
        d_attended[:, :, :, columns] = part.astype(BF16).reshape(2, LATENT, 64, 256)


def resample_mix(chip, values, weights, probs, spread, d_attended, attended, d_logits, hooks):
    def group(g):
        r, tile = g % 2, ((chip + 1 + g // 4) % 2) * 2 + (g // 2) % 2
        c = pl.ds(pl.multiple_of(tile * 16, 16), 16)
        w = weights[r, :, c].reshape(208, 128)
        d_weights = jnp.zeros((208, 128), F32)
        for cb in range(4):
            columns = slice(cb * 256, (cb + 1) * 256)
            wide = dot(w, spread[cb])
            v = values[r, :, c, columns].astype(F32)
            d_v = jnp.zeros((LEV, 16, 256), F32)
            products = []
            for q in range(LATENT):
                wq = wide[:, q * 256 : (q + 1) * 256].reshape(LEV, 16, 256)
                da = d_attended[r, q, c, columns].astype(F32)[None]
                attended[r, q, c, columns] = jnp.sum(wq * v, axis=0).astype(BF16)
                d_v = d_v + wq * da
                products.append((v * da).astype(BF16).reshape(208, 256))
            values[r, :, c, columns] = d_v.astype(BF16)
            d_weights = d_weights + dot(jnp.concatenate(products, axis=1), spread[cb], ((1,), (1,)))
        p = probs[r, :, c]
        dw = d_weights.reshape(LEV, 16, 128)
        d_logits[r, :, c] = (p * (dw - jnp.sum(p * dw, axis=0, keepdims=True))).astype(BF16)

    looped(GROUPS, group, hooks)


def resample_latents(chip, attended, ro, lq, latents):
    cells = pl.ds(pl.multiple_of(chip * 32, 32), 32)
    rows = attended[:, :, cells, :].reshape(192, D)
    for nb in range(4):
        columns = slice(nb * 256, (nb + 1) * 256)
        part = dot(rows, ro[:, columns]).reshape(2, LATENT, 32, 256)
        part = part + lq[:, columns].astype(F32)[None, :, None, :]
        latents[:, :, cells, columns] = part.astype(BF16)


def pack_pair(left, right, p, z, columns):
    left = left.reshape(2, 4, 2, 2, 8, left.shape[-1])
    right = right.reshape(2, 4, 2, 2, 8, right.shape[-1])
    for core in range(2):
        both = jnp.concatenate([left[:, :, :, core], right[:, :, :, core]], axis=3)
        p[core, z, :, :, :, :, columns] = both.astype(BF16)


def out_gradient(grad, attended, turned, packed):
    def block(z):
        columns = pl.ds(pl.multiple_of(z * 256, 256), 256)
        turned[:, :384] = attended[:, :, :, columns].reshape(384, 256).T
        for nb in range(2):
            halves = []
            for half in range(2):
                c = slice(half * 512 + nb * 256, half * 512 + (nb + 1) * 256)
                halves.append(dot(turned[:, :384], grad[:, :, :, c].reshape(384, 256)))
            pack_pair(halves[0], halves[1], packed, z, slice(nb * 256, (nb + 1) * 256))

    looped(4, block, {})


def token_gradients(tok, d_values, d_logits, turned, packed, hooks):
    def block(z):
        columns = pl.ds(pl.multiple_of(z * 256, 256), 256)
        turned[...] = tok[:, :, :, columns].reshape(GROUPS * 208, 256).T
        for nb in range(2):
            halves = []
            for half in range(2):
                c = slice(half * 512 + nb * 256, half * 512 + (nb + 1) * 256)
                halves.append(dot(turned[...], d_values[:, :, :, c].reshape(GROUPS * 208, 256)))
            pack_pair(halves[0], halves[1], packed[nb], z, slice(0, 256))
        small = dot(turned[...], d_logits[...].reshape(GROUPS * 208, 128))
        pack_pair(small, jnp.zeros_like(small), packed[0], z, slice(256, 384))

    looped(4, block, hooks)


def normalise(window, gain, normed):
    for win in range(4):
        values = window(win)
        centred = values - jnp.mean(values, axis=-1, keepdims=True)
        spread = jnp.mean(centred * centred, axis=-1, keepdims=True)
        normed[win * 96 : (win + 1) * 96, :] = (centred * lax.rsqrt(spread + 1e-05) * gain).astype(BF16)


def weight_block(w, layer, block, j):
    tile = layer * 8 + block
    return jnp.concatenate([w[tile + 4 * i, j // 2, j % 2].reshape(D, 128) for i in range(2)], axis=1)


def attend_heads(j, layer, w, normed, bias, mixed):
    queries, keys, values = (dot(normed[...], weight_block(w, layer, block, j)) for block in range(3))
    queries, keys, values = (queries * 0.125).astype(BF16), keys.astype(BF16), values.astype(BF16)
    left = lax.broadcasted_iota(jnp.int32, (96, 128), 1) < 64
    columns = pl.ds(pl.multiple_of(j * 256, 256), 256)
    none = jnp.zeros((96, 128), BF16)
    for win in range(4):
        rows = slice(win * 96, (win + 1) * 96)
        q, k, v = queries[rows], keys[rows], values[rows]
        stacked = []
        for h in range(4):
            half = q[:, 128 * (h // 2) : 128 * (h // 2 + 1)]
            half = jnp.where(left, half, none) if h % 2 == 0 else jnp.where(left, none, half)
            stacked.append(jnp.concatenate([half, none] if h < 2 else [none, half], axis=1))
        logits = dot(jnp.concatenate(stacked, axis=0), k, ((1,), (1,)))
        if bias is not None:
            logits = (logits.reshape(4, 96, 96) + bias[win][None]).reshape(384, 96)
        e = jnp.exp(logits - jnp.max(logits, axis=-1, keepdims=True))
        e = e * (1.0 / jnp.sum(e, axis=-1, keepdims=True))
        out = dot(e.astype(BF16), v)
        pairs = [
            jnp.where(left, out[0:96, :128], out[96:192, :128]),
            jnp.where(left, out[192:288, 128:], out[288:384, 128:]),
        ]
        mixed[rows, columns] = jnp.concatenate(pairs, axis=1).astype(BF16)


def label_mask(label, place, bias):
    lat = device_of(place)[0]
    row = lax.broadcasted_iota(jnp.int32, (8, 16), 0) + lat * 8
    codes = label[...].astype(F32) * 2.0 + jnp.where(row >= 8 * 32 - 2, 2.0, 1.0)
    token = lax.broadcasted_iota(jnp.int32, (96, 16), 0)
    column = lax.broadcasted_iota(jnp.int32, (96, 16), 1)
    ones = jnp.ones((96, 16), F32)
    for win in range(4):
        wr, wc = divmod(win, 2)
        own = jnp.zeros((96, 16), F32)
        for r in range(4):
            hit = (token // 24 == r) & (column == 8 * wc + token % 8)
            own = own + jnp.where(hit, codes[4 * wr + r : 4 * wr + r + 1, :], 0.0)
        one = dot(own, ones, ((1,), (1,)))
        other = dot(ones, own, ((1,), (1,)))
        bias[win] = jnp.where(one == other, 0.0, -1e30)


def output_update(w, layer, j, mixed):
    return dot(mixed[...], weight_block(w, layer, 3, j)).reshape(2, 2, 4, LATENT, 8, 256)


def tile_rows(x, wr, columns=slice(None)):
    return x[4 * wr : 4 * wr + 4, :, :, columns].astype(F32)


def own_first(i, core):
    return (i % 2) * 2 + (core + i // 2) % 2


def first_sublayer(core, x, gain, w, normed, mixed, middle, ready, hooks):
    def window(win):
        wr, wc = divmod(win, 2)
        return tile_rows(x, wr)[:, :, 8 * wc : 8 * wc + 8].reshape(96, D)

    normalise(window, gain, normed)
    ready()
    looped(4, lambda i: attend_heads(own_first(i, core), 0, w, normed, None, mixed), hooks)
    for j in range(4):
        columns = slice(j * 256, (j + 1) * 256)
        update = output_update(w, 0, j, mixed)
        for wr in range(2):
            both = jnp.concatenate([update[wr, 0], update[wr, 1]], axis=2)
            middle[4 * wr : 4 * wr + 4, :, 0:16, columns] = tile_rows(x, wr, columns) + both


def second_sublayer(core, middle, gain, w, normed, mixed, bias, out, hooks):
    def window(win):
        wr, wc = divmod(win, 2)
        return middle[4 * wr + 2 : 4 * wr + 6, :, 8 * wc + 4 : 8 * wc + 12, :].reshape(96, D)

    normalise(window, gain, normed)
    looped(4, lambda i: attend_heads(own_first(i, core), 1, w, normed, bias, mixed), hooks)
    for j in range(4):
        columns = slice(j * 256, (j + 1) * 256)
        update = output_update(w, 1, j, mixed)
        for wr in range(2):
            halves = []
            for wc in range(2):
                own = middle[4 * wr + 2 : 4 * wr + 6, :, 8 * wc + 4 : 8 * wc + 12, columns]
                halves.append(own + update[wr, wc])
            both = jnp.concatenate(halves, axis=2).astype(BF16)
            out[4 * wr : 4 * wr + 4, :, :, columns] = both


class Edges:
    def __init__(self, place, middle, rows_out, columns_out, rows_in, columns_in, corner_in, send, recv):
        lat, lon = device_of(place)
        above, beside = (lat + 31) % 32, (lon + 3) % 4
        self.middle, self.rows_out, self.columns_out = middle, rows_out, columns_out
        self.rows_in, self.columns_in, self.corner_in = rows_in, columns_in, corner_in
        plan = (
            (rows_out, rows_in, (above, lon)),
            (columns_out, columns_in, (lat, beside)),
            (columns_out.at[pl.ds(0, 32)], corner_in, (above, beside)),
        )
        self.copies = [
            pltpu.make_async_remote_copy(
                src_ref=src,
                dst_ref=dst,
                send_sem=send.at[k],
                recv_sem=recv.at[k],
                device_id=other,
                device_id_type=MESH,
            )
            for k, (src, dst, other) in enumerate(plan)
        ]

    def start(self):
        middle = self.middle
        for r in range(2):
            self.rows_out[r] = middle[r, :, 0:16].reshape(48, D).astype(BF16)
        for part in range(6):
            cells = [divmod(part * 4 + i, LATENT) for i in range(4)]
            rows = jnp.concatenate([middle[r, q, 0:4] for r, q in cells], axis=0)
            self.columns_out[part * 16 : (part + 1) * 16] = rows.astype(BF16)
        for copy in self.copies:
            copy.start()

    def finish(self):
        middle = self.middle
        for copy in self.copies:
            copy.wait_recv()
        for r in range(2):
            middle[8 + r, :, 0:16] = self.rows_in[r].astype(F32).reshape(LATENT, 16, D)
        for part in range(6):
            rows = self.columns_in[part * 16 : (part + 1) * 16].astype(F32)
            for i in range(4):
                r, q = divmod(part * 4 + i, LATENT)
                middle[r, q, 16:20] = rows[i * 4 : (i + 1) * 4]
        for part in range(2):
            rows = self.corner_in[part * 16 : (part + 1) * 16].astype(F32)
            for i in range(4):
                r, q = divmod(part * 4 + i, LATENT)
                if r < 2:
                    middle[8 + r, q, 16:20] = rows[i * 4 : (i + 1) * 4]

    def drain(self):
        for copy in self.copies:
            copy.wait_send()


class Tiles:
    def __init__(self, place, latents, x, send, recv, own):
        lat, lon = device_of(place)

        def at(column):
            return pl.ds(pl.multiple_of(column * 16, 16), 16)

        self.own = pltpu.make_async_copy(latents.at[:, :, at(lon)], x.at[pl.ds(2 * lon, 2)], own)
        chip, core = lon // 2, lon % 2
        partners = ((1 - chip) * 2 + core, (1 - chip) * 2 + 1 - core, chip * 2 + 1 - core)
        self.out, self.arriving = [], []
        for k, other in enumerate(partners):
            for copies, row in ((self.out, lon), (self.arriving, other)):
                copies.append(
                    pltpu.make_async_remote_copy(
                        src_ref=latents.at[:, :, at(other)],
                        dst_ref=x.at[pl.ds(2 * row, 2)],
                        send_sem=send.at[k],
                        recv_sem=recv.at[k],
                        device_id=(lat, other),
                        device_id_type=MESH,
                    )
                )

    def start(self, here):
        if here:
            self.out[2].start()
            self.own.start()
        else:
            self.out[0].start()
            self.out[1].start()

    def finish(self):
        self.own.wait()
        for copy in self.arriving:
            copy.wait_recv()

    def drain(self):
        for copy in self.out:
            copy.wait_send()


WIDTHS = (384, 256, 512)
REDUCE_ORDERS = (("z", "x", "y"), ("x", "y", "z"), ("y", "z", "x"))


def kernel(factor, tokens, grads, kw_far, vw_far, ro_far, lq, gains, qkv, ow, label, *refs):
    out, grad_key, grad_value, grad_out = refs[:4]
    w, latents, x, rows_out, columns_out, rows_in, columns_in, corner_in = refs[4:12]
    packed, landing = refs[12:15], refs[15:45]
    g_send, g_recv, r_send, r_recv, t_send, t_recv, e_send, e_recv, near = refs[45:]
    place = my_place()
    y = place["y"]
    own = []
    for layer in range(2):
        for half in range(2):
            columns = pl.ds(128 * half, 128)
            tile = layer * 8 + half * 4
            mine = (y % 2, place["core"], place["z"], y // 2, place["x"])
            own.append((qkv.at[layer, :, :, columns], w.at[(pl.ds(tile, 3),) + mine]))
            own.append((ow.at[layer, :, columns], w.at[(tile + 3,) + mine]))
    own = [pltpu.make_async_copy(src, dst, near.at[i]) for i, (src, dst) in enumerate(own)]
    for copy in own:
        copy.start()
    layers = [
        [Gather(place, w, g_send, g_recv, 3 * layer + i, part) for i, part in enumerate(PARTS[layer])]
        for layer in range(2)
    ]
    sums = [
        Reduce(place, packed[i], landing[10 * i : 10 * i + 10], r_send.at[i], r_recv.at[i], REDUCE_ORDERS[i])
        for i in range(3)
    ]
    tiles = Tiles(place, latents, x, t_send, t_recv, near.at[8])

    def gathered(layer, s):
        def hook():
            for part in layers[layer]:
                part.step(s)

        return hook

    def reduced(s, *parts):
        def hook():
            for part in parts:
                sums[part].step(s)

        return hook

    def both(*hooks):
        def hook():
            for one in hooks:
                one()

        return hook

    def resampler(tok, grad, kw, vw, ro, kq, values, logits, weights, spread, d_att, att, d_logits, turned):
        pairs = ((kw_far, kw), (tokens, tok), (vw_far, vw), (grads, grad), (ro_far, ro))
        copies = [pltpu.make_async_copy(far, here, near.at[9 + i]) for i, (far, here) in enumerate(pairs)]
        for copy in copies:
            copy.start()
        greet(place)
        for copy in own:
            copy.wait()
        gathered(0, 0)()
        spread_heads(spread)
        gathered(1, 0)()
        copies[0].wait()
        key_queries(kw, lq, kq)
        gathered(0, 1)()
        copies[1].wait()
        copies[2].wait()
        resample_project(tok, vw, kq, values, logits, {0: gathered(1, 1)})
        resample_softmax(logits, weights)
        copies[3].wait()
        copies[4].wait()
        resample_cotangents(grad, ro, d_att)
        chip = y % 2

        def first_half():
            resample_latents(1 - chip, att, ro, lq, latents)
            tiles.start(False)

        hooks = {0: gathered(0, 2), 3: first_half, 6: both(gathered(0, 3), gathered(1, 2))}
        resample_mix(chip, values, weights, logits, spread, d_att, att, d_logits, hooks)
        resample_latents(chip, att, ro, lq, latents)
        tiles.start(True)
        out_gradient(grad, att, turned, packed[2])
        reduced(0, 2)()
        token_gradients(tok, values, d_logits, turned, packed, {})

    pl.run_scoped(
        resampler,
        pltpu.VMEM((2, LEV, 64, D), BF16),
        pltpu.VMEM((2, LATENT, 64, D), BF16),
        pltpu.VMEM((D, D), BF16),
        pltpu.VMEM((D, D), BF16),
        pltpu.VMEM((D, D), BF16),
        pltpu.VMEM((2, D, 128), BF16),
        pltpu.VMEM((2, LEV, 64, D), BF16),
        pltpu.VMEM((2, LEV, 64, 128), F32),
        pltpu.VMEM((2, LEV, 64, 128), BF16),
        pltpu.VMEM((4, 128, 768), BF16),
        pltpu.VMEM((2, LATENT, 64, D), BF16),
        pltpu.VMEM((2, LATENT, 64, D), BF16),
        pltpu.VMEM((2, LEV, 64, 128), BF16),
        pltpu.VMEM((256, GROUPS * 208), BF16),
    )
    reduced(0, 0, 1)()
    reduced(1, 2)()

    def backbone(middle, normed, mixed, bias):
        edges = Edges(place, middle, rows_out, columns_out, rows_in, columns_in, corner_in, e_send, e_recv)
        core = place["core"]
        label_mask(label, place, bias)
        reduced(1, 1)()
        tiles.finish()
        ready = both(gathered(0, 4), reduced(1, 0))
        hooks = {1: gathered(0, 5), 2: gathered(1, 3)}
        first_sublayer(core, x, gains[0:1, :], w, normed, mixed, middle, ready, hooks)
        edges.start()
        gathered(1, 4)()
        reduced(2, 0, 1)()
        edges.finish()
        reduced(2, 2)()
        hooks = {1: both(gathered(1, 5), reduced(3, 0, 1)), 2: reduced(3, 2)}
        second_sublayer(core, middle, gains[1:2, :], w, normed, mixed, bias, out, hooks)
        reduced(4, 0, 1, 2)()
        edges.drain()

    pl.run_scoped(
        backbone,
        pltpu.VMEM((10, LATENT, 24, D), F32),
        pltpu.VMEM((384, D), BF16),
        pltpu.VMEM((384, D), BF16),
        pltpu.VMEM((4, 96, 96), F32),
    )
    finish_gradients(factor, [part.result() for part in sums], lq, grad_key, grad_value, grad_out)
    tiles.drain()
    for part in layers[0] + layers[1] + sums:
        part.drain()


def whole(factor, tokens, grads, kw, vw, ro, lq, gains, qkv, ow, label):
    vmem, far = pl.BlockSpec(memory_space=pltpu.VMEM), pl.BlockSpec(memory_space=pl.ANY)
    landings = []
    for order, width in zip(REDUCE_ORDERS, WIDTHS):
        landings += landing_shapes(order, width)
    dma = pltpu.SemaphoreType.DMA
    return pl.pallas_call(
        functools.partial(kernel, factor),
        out_shape=[jax.ShapeDtypeStruct((8, LATENT, 16, D), BF16)] + [jax.ShapeDtypeStruct((8, D), F32)] * 3,
        in_specs=[far] * 5 + [vmem, vmem, far, far, vmem],
        out_specs=[vmem] * 4,
        scratch_shapes=[
            pltpu.VMEM((16, 2, 2, 4, 2, 4, 32, 128), BF16),
            pltpu.VMEM((2, LATENT, 64, D), BF16),
            pltpu.VMEM((8, LATENT, 16, D), BF16),
            pltpu.VMEM((2, 48, D), BF16),
            pltpu.VMEM((96, D), BF16),
            pltpu.VMEM((2, 48, D), BF16),
            pltpu.VMEM((96, D), BF16),
            pltpu.VMEM((32, D), BF16),
        ]
        + [pltpu.VMEM((2, 4, 2, 4, 2, 16, width), BF16) for width in WIDTHS]
        + landings
        + [dma((6, 16)), dma((6, 16)), dma((3, 10)), dma((3, 10))]
        + [dma((3,)), dma((3,)), dma((3,)), dma((3,)), dma((14,))],
        compiler_params=pltpu.CompilerParams(collective_id=0, has_side_effects=True, vmem_limit_bytes=63 * MIB),
    )(tokens, grads, kw, vw, ro, lq, gains, qkv, ow, label)


def hand_over_kernel(*refs):
    count = len(refs) // 2
    for i in range(count):
        refs[count + i][...] = refs[i][...]


def hand_over(results):
    return pl.pallas_call(
        hand_over_kernel,
        out_shape=[jax.ShapeDtypeStruct(r.shape, r.dtype) for r in results],
        in_specs=[pl.BlockSpec(memory_space=pltpu.VMEM)] * len(results),
        out_specs=[pl.BlockSpec(memory_space=pltpu.VMEM)] * len(results),
    )(*results)


def local(
    level_tokens,
    latent_query,
    key_weight,
    value_weight,
    resample_out,
    norm_gain,
    qkv_weight,
    out_weight,
    window_label,
    grad_latents,
):
    factor = (2 * 64 * lax.axis_size("lat") * lax.axis_size("lon")) ** (-0.5)
    results = whole(
        factor,
        level_tokens.swapaxes(1, 2),
        grad_latents.swapaxes(1, 2),
        key_weight,
        value_weight,
        resample_out,
        latent_query,
        norm_gain,
        qkv_weight.swapaxes(1, 2),
        out_weight,
        window_label,
    )
    out, grad_key, grad_value, grad_out = hand_over(results)
    return (out.swapaxes(1, 2), grad_key, grad_value, grad_out)


def solution(mesh):
    in_specs = (
        P(("lat", "lon"), None, None, None),
        P(),
        P(),
        P(),
        P(),
        P(),
        P(None, "lat", None, "lon"),
        P(None, "lat", "lon"),
        P("lat", "lon"),
        P(("lat", "lon"), None, None, None),
    )
    out_specs = (
        P("lat", "lon", None, None),
        P(("lat", "lon"), None),
        P(("lat", "lon"), None),
        P(("lat", "lon"), None),
    )
    return jax.shard_map(local, mesh=mesh, in_specs=in_specs, out_specs=out_specs, check_vma=False)
```

```python
import functools

import jax
import jax.numpy as jnp
from jax import lax
from jax.experimental import pallas as pl
from jax.experimental.pallas import tpu as pltpu
from jax.sharding import PartitionSpec as P

MESH = pl.DeviceIdType.MESH
F32, BF16 = jnp.float32, jnp.bfloat16
D = 1024
HEADS = 16
LEV = 13
LATENT = 3
GROUPS = 8
MIB = 1024 * 1024


def dot(a, b, dims=((1,), (0,))):
    return lax.dot_general(a, b, (dims, ((), ())), preferred_element_type=F32)


def my_place():
    lat, lon = lax.axis_index("lat"), lax.axis_index("lon")
    return {
        "z": lat // 8,
        "y": ((lat // 4) % 2) * 2 + lon // 2,
        "x": lat % 4,
        "core": lon % 2,
    }


def device_of(place):
    lat = place["z"] * 8 + (place["y"] // 2) * 4 + place["x"]
    return (lat, (place["y"] % 2) * 2 + place["core"])


def moved(place, dim, delta):
    size = 2 if dim == "core" else 4
    other = dict(place)
    other[dim] = (place[dim] + delta + size) % size
    return device_of(other)


def pick(dim, value):
    if dim == "y":
        if value is None:
            return {"yh": slice(None), "yl": slice(None)}
        return {"yh": pl.ds(value // 2, 1), "yl": pl.ds(value % 2, 1)}
    return {dim: slice(None) if value is None else pl.ds(value, 1)}


def greet(place):
    barrier = pltpu.get_barrier_semaphore()
    others = [moved(place, dim, step) for dim in "xyz" for step in (1, -1, 2)] + [moved(place, "core", 1)]
    lat, lon = device_of(place)
    others += [(lat, (lon + k) % 4) for k in range(1, 4)]
    others += [((lat + step) % 32, (lon + turn) % 4) for step, turn in ((1, 0), (31, 0), (1, 1), (31, 3))]
    for other in others:
        pl.semaphore_signal(barrier, inc=1, device_id=other, device_id_type=MESH)
    pl.semaphore_wait(barrier, len(others))


PARTS = (
    ((0, 2, ("x", "y", "z")), (2, 2, ("y", "z", "x")), (4, 2, ("z", "x", "y"))),
    ((6, 1, ("x", "y", "z")), (7, 1, ("y", "z", "x"))),
    ((8, 2, ("x", "y", "z")), (10, 2, ("y", "z", "x")), (12, 2, ("z", "x", "y"))),
    ((14, 1, ("y", "z", "x")), (15, 1, ("x", "y", "z"))),
)
Q0, O0, Q1, O1 = range(4)


class Gather:
    def __init__(self, place, w, send, recv, number, part):
        self.place, self.w, self.send, self.recv, self.number = place, w, send, recv, number
        first, count, self.order = part
        self.tiles = pl.ds(first, count)

    def region(self, phase, value, half=None, core=None):
        index = {}
        for position, dim in enumerate(self.order):
            if position < phase:
                index.update(pick(dim, None))
            elif position == phase:
                index.update(pick(dim, value))
            else:
                index.update(pick(dim, self.place[dim]))
        rows = slice(None) if half is None else pl.ds(16 * half, 16)
        core = self.place["core"] if core is None else core
        return self.w.at[self.tiles, index["yl"], core, index["z"], index["yh"], index["x"], rows, :]

    def copy(self, k, ref, other):
        return pltpu.make_async_remote_copy(
            src_ref=ref,
            dst_ref=ref,
            send_sem=self.send.at[self.number, k],
            recv_sem=self.recv.at[self.number, k],
            device_id=other,
            device_id_type=MESH,
        )

    def ring(self, phase, k):
        dim = self.order[phase]
        me = self.place[dim]
        if phase < 2:
            return self.copy(4 * phase + k, self.region(phase, me), moved(self.place, dim, (1, -1, 2)[k]))
        other = moved(self.place, dim, 1 if k % 2 == 0 else -1)
        if k < 2:
            return self.copy(4 * phase + k, self.region(phase, me), other)
        return self.copy(4 * phase + k, self.region(phase, (me + 7 - 2 * k) % 4, k - 2), other)

    def arrival(self, phase, k):
        dim = self.order[phase]
        me = self.place[dim]
        source = (me + (3, 1, 2, 2)[k]) % 4
        half = k - 2 if phase == 2 and k > 1 else None
        return self.copy(4 * phase + k, self.region(phase, source, half), moved(self.place, dim, 1))

    def across(self, k, core):
        ref = self.region(2, (self.place[self.order[2]] + (0, 3, 1, 2)[k]) % 4, None, core)
        return self.copy(12 + k, ref, moved(self.place, "core", 1))

    def step(self, s):
        core = self.place["core"]
        if s < 3:
            if s > 0:
                for k in range(3):
                    self.arrival(s - 1, k).wait_recv()
            for k in range(3 if s < 2 else 2):
                self.ring(s, k).start()
            if s == 2:
                self.across(0, core).start()
        elif s == 3:
            for k in range(2):
                self.arrival(2, k).wait_recv()
                self.ring(2, k + 2).start()
                self.across(k + 1, core).start()
        elif s == 4:
            for k in (2, 3):
                self.arrival(2, k).wait_recv()
            self.across(3, core).start()
        else:
            for k in range(4):
                self.across(k, 1 - core).wait_recv()

    def drain(self):
        for phase in range(3):
            for k in range(3 if phase < 2 else 4):
                self.ring(phase, k).wait_send()
        for k in range(4):
            self.across(k, self.place["core"]).wait_send()


def landing_shape(order, phase, columns):
    sizes = {"z": 4, "yh": 2, "x": 4, "yl": 2}
    for dim in order[: phase + 1]:
        for name in ("yh", "yl") if dim == "y" else (dim,):
            sizes[name] = 1
    return (sizes["z"], sizes["yh"], sizes["x"], sizes["yl"], 16, columns)


class Reduce:
    def __init__(self, place, p, landing, send, recv, order):
        self.place, self.p, self.landing = place, p, landing
        self.send, self.recv, self.order = send, recv, order

    def region(self, phase, value):
        index = {}
        for position, dim in enumerate(self.order):
            if position < phase:
                index.update(pick(dim, self.place[dim]))
            elif position == phase:
                index.update(pick(dim, value))
            else:
                index.update(pick(dim, None))
        return (self.place["core"], index["z"], index["yh"], index["x"], index["yl"])

    def copy(self, k, src, other):
        return pltpu.make_async_remote_copy(
            src_ref=src,
            dst_ref=self.landing[k],
            send_sem=self.send.at[k],
            recv_sem=self.recv.at[k],
            device_id=other,
            device_id_type=MESH,
        )

    def across(self):
        return self.copy(9, self.p.at[1 - self.place["core"]], moved(self.place, "core", 1))

    def ring(self, phase, k):
        dim = self.order[phase]
        step = (1, -1, 2)[k]
        target = (self.place[dim] + step + 4) % 4
        return self.copy(3 * phase + k, self.p.at[self.region(phase, target)], moved(self.place, dim, step))

    def step(self, s):
        if s == 0:
            self.across().start()
        elif s == 1:
            self.across().wait_recv()
            core = self.place["core"]
            for z in range(4):
                total = self.p[core, z].astype(F32) + self.landing[9][z].astype(F32)
                self.p[core, z] = total.astype(BF16)
        else:
            for k in range(3):
                self.ring(s - 2, k).wait_recv()
            region = self.region(s - 2, self.place[self.order[s - 2]])
            total = self.p[region].astype(F32)
            for k in range(3):
                total = total + self.landing[3 * (s - 2) + k][...].astype(F32)
            self.p[region] = total.astype(BF16)
        if 0 < s < 4:
            for k in range(3):
                self.ring(s - 1, k).start()

    def drain(self):
        for phase in range(3):
            for k in range(3):
                self.ring(phase, k).wait_send()
        self.across().wait_send()

    def result(self):
        y = self.place["y"]
        return self.p[self.place["core"], self.place["z"], y // 2, self.place["x"], y % 2].astype(F32)


def landing_shapes(order, columns):
    shapes = [pltpu.VMEM(landing_shape(order, phase, columns), BF16) for phase in range(3) for _ in range(3)]
    return shapes + [pltpu.VMEM((4, 2, 4, 2, 16, columns), BF16)]


def spread_queries(lq):
    row = lax.broadcasted_iota(jnp.int32, (128, D), 0)
    head = lax.broadcasted_iota(jnp.int32, (128, D), 1) // 64
    total = jnp.zeros((128, D), F32)
    for q in range(LATENT):
        total = total + jnp.where(row == q * HEADS + head, lq[q : q + 1, :].astype(F32), 0.0)
    return total.astype(BF16)


def finish_gradients(factor, sums, lq, grad_key, grad_value, grad_out):
    first, second, third = sums
    grad_value[:, 0:256] = first[:8, :256] * factor
    grad_value[:, 256:512] = second[:8] * factor
    grad_value[:, 512:768] = first[8:, :256] * factor
    grad_value[:, 768:1024] = second[8:] * factor
    grad_out[:, 0:512] = third[:8] * factor
    grad_out[:, 512:1024] = third[8:] * factor
    small = first[:8, 256:] * (factor * 0.125)
    high = small.astype(BF16)
    low = (small - high.astype(F32)).astype(BF16)
    queries = spread_queries(lq)
    grad_key[...] = dot(high, queries) + dot(low, queries)


def looped(count, body, hooks):
    def step(i, _):
        body(i)
        for at, hook in hooks.items():
            pl.when(i == at)(hook)
        return 0

    lax.fori_loop(0, count, step, 0)


def group_at(g):
    return g // 4, pl.ds(pl.multiple_of((g % 4) * 16, 16), 16)


def spread_heads(spread):
    row = lax.broadcasted_iota(jnp.int32, (128, 768), 0)
    column = lax.broadcasted_iota(jnp.int32, (128, 768), 1)
    for cb in range(4):
        hit = row == (column // 256) * HEADS + cb * 4 + (column % 256) // 64
        spread[cb] = jnp.where(hit, 1.0, 0.0).astype(BF16)


def key_queries(kw, lq, kq):
    queries = spread_queries(lq)

    def rows(i, _):
        at = pl.ds(pl.multiple_of(i * 256, 256), 256)
        total = dot(kw[at, :], queries, ((1,), (1,))) * 0.125
        high = total.astype(BF16)
        kq[0, at, :] = high
        kq[1, at, :] = (total - high.astype(F32)).astype(BF16)
        return 0

    lax.fori_loop(0, 4, rows, 0)


def resample_project(tok, vw, kq, values, logits, hooks):
    def project(r):
        rows = tok[r].reshape(LEV * 64, D)
        for nb in range(4):
            columns = slice(nb * 256, (nb + 1) * 256)
            values[r, :, :, columns] = dot(rows, vw[:, columns]).astype(BF16).reshape(LEV, 64, 256)
        logits[r] = (dot(rows, kq[0]) + dot(rows, kq[1])).reshape(LEV, 64, 128)

    looped(2, project, hooks)


def resample_softmax(logits, weights):
    def group(g, _):
        r, c = group_at(g)
        x = logits[r, :, c]
        x = jnp.exp(x - jnp.max(x, axis=0, keepdims=True))
        x = x / jnp.sum(x, axis=0, keepdims=True)
        logits[r, :, c] = x
        weights[r, :, c] = x.astype(BF16)
        return 0

    lax.fori_loop(0, GROUPS, group, 0)


def resample_cotangents(grad, ro, d_attended):
    rows = grad[...].reshape(384, D)
    for nb in range(4):
        columns = slice(nb * 256, (nb + 1) * 256)
        part = dot(rows, ro[columns, :], ((1,), (1,)))
        d_attended[:, :, :, columns] = part.astype(BF16).reshape(2, LATENT, 64, 256)


def resample_mix(chip, values, weights, probs, spread, d_attended, attended, d_logits, hooks):
    def group(g):
        r, tile = g % 2, ((chip + 1 + g // 4) % 2) * 2 + (g // 2) % 2
        c = pl.ds(pl.multiple_of(tile * 16, 16), 16)
        w = weights[r, :, c].reshape(208, 128)
        d_weights = jnp.zeros((208, 128), F32)
        for cb in range(4):
            columns = slice(cb * 256, (cb + 1) * 256)
            wide = dot(w, spread[cb])
            v = values[r, :, c, columns].astype(F32)
            d_v = jnp.zeros((LEV, 16, 256), F32)
            products = []
            for q in range(LATENT):
                wq = wide[:, q * 256 : (q + 1) * 256].reshape(LEV, 16, 256)
                da = d_attended[r, q, c, columns].astype(F32)[None]
                attended[r, q, c, columns] = jnp.sum(wq * v, axis=0).astype(BF16)
                d_v = d_v + wq * da
                products.append((v * da).astype(BF16).reshape(208, 256))
            values[r, :, c, columns] = d_v.astype(BF16)
            d_weights = d_weights + dot(jnp.concatenate(products, axis=1), spread[cb], ((1,), (1,)))
        p = probs[r, :, c]
        dw = d_weights.reshape(LEV, 16, 128)
        d_logits[r, :, c] = (p * (dw - jnp.sum(p * dw, axis=0, keepdims=True))).astype(BF16)

    looped(GROUPS, group, hooks)


def resample_latents(chip, attended, ro, lq, latents):
    cells = pl.ds(pl.multiple_of(chip * 32, 32), 32)
    rows = attended[:, :, cells, :].reshape(192, D)
    for nb in range(4):
        columns = slice(nb * 256, (nb + 1) * 256)
        part = dot(rows, ro[:, columns]).reshape(2, LATENT, 32, 256)
        part = part + lq[:, columns].astype(F32)[None, :, None, :]
        latents[:, :, cells, columns] = part.astype(BF16)


def pack_pair(left, right, p, z, columns):
    left = left.reshape(2, 4, 2, 2, 8, left.shape[-1])
    right = right.reshape(2, 4, 2, 2, 8, right.shape[-1])
    for core in range(2):
        both = jnp.concatenate([left[:, :, :, core], right[:, :, :, core]], axis=3)
        p[core, z, :, :, :, :, columns] = both.astype(BF16)


def out_gradient(grad, attended, turned, packed):
    def block(z):
        columns = pl.ds(pl.multiple_of(z * 256, 256), 256)
        turned[:, :384] = attended[:, :, :, columns].reshape(384, 256).T
        for nb in range(2):
            halves = []
            for half in range(2):
                c = slice(half * 512 + nb * 256, half * 512 + (nb + 1) * 256)
                halves.append(dot(turned[:, :384], grad[:, :, :, c].reshape(384, 256)))
            pack_pair(halves[0], halves[1], packed, z, slice(nb * 256, (nb + 1) * 256))

    looped(4, block, {})


def token_gradients(tok, d_values, d_logits, turned, packed, hooks):
    def block(z):
        columns = pl.ds(pl.multiple_of(z * 256, 256), 256)
        turned[...] = tok[:, :, :, columns].reshape(GROUPS * 208, 256).T
        for nb in range(2):
            halves = []
            for half in range(2):
                c = slice(half * 512 + nb * 256, half * 512 + (nb + 1) * 256)
                halves.append(dot(turned[...], d_values[:, :, :, c].reshape(GROUPS * 208, 256)))
            pack_pair(halves[0], halves[1], packed[nb], z, slice(0, 256))
        small = dot(turned[...], d_logits[...].reshape(GROUPS * 208, 128))
        pack_pair(small, jnp.zeros_like(small), packed[0], z, slice(256, 384))

    looped(4, block, hooks)


def normalise(window, gain, normed):
    for win in range(4):
        values = window(win)
        centred = values - jnp.mean(values, axis=-1, keepdims=True)
        spread = jnp.mean(centred * centred, axis=-1, keepdims=True)
        normed[win * 96 : (win + 1) * 96, :] = (centred * lax.rsqrt(spread + 1e-05) * gain).astype(BF16)


def weight_block(w, layer, block, j):
    tile = layer * 8 + block * 2
    return jnp.concatenate([w[tile + i, j // 2, j % 2].reshape(D, 128) for i in range(2)], axis=1)


def attend_heads(j, layer, w, normed, bias, mixed):
    queries, keys, values = (dot(normed[...], weight_block(w, layer, block, j)) for block in range(3))
    queries, keys, values = (queries * 0.125).astype(BF16), keys.astype(BF16), values.astype(BF16)
    left = lax.broadcasted_iota(jnp.int32, (96, 128), 1) < 64
    columns = pl.ds(pl.multiple_of(j * 256, 256), 256)
    none = jnp.zeros((96, 128), BF16)
    for win in range(4):
        rows = slice(win * 96, (win + 1) * 96)
        q, k, v = queries[rows], keys[rows], values[rows]
        stacked = []
        for h in range(4):
            half = q[:, 128 * (h // 2) : 128 * (h // 2 + 1)]
            half = jnp.where(left, half, none) if h % 2 == 0 else jnp.where(left, none, half)
            stacked.append(jnp.concatenate([half, none] if h < 2 else [none, half], axis=1))
        logits = dot(jnp.concatenate(stacked, axis=0), k, ((1,), (1,)))
        if bias is not None:
            logits = (logits.reshape(4, 96, 96) + bias[win][None]).reshape(384, 96)
        e = jnp.exp(logits - jnp.max(logits, axis=-1, keepdims=True))
        e = e * (1.0 / jnp.sum(e, axis=-1, keepdims=True))
        out = dot(e.astype(BF16), v)
        pairs = [
            jnp.where(left, out[0:96, :128], out[96:192, :128]),
            jnp.where(left, out[192:288, 128:], out[288:384, 128:]),
        ]
        mixed[rows, columns] = jnp.concatenate(pairs, axis=1).astype(BF16)


def label_mask(label, place, bias):
    lat = device_of(place)[0]
    row = lax.broadcasted_iota(jnp.int32, (8, 16), 0) + lat * 8
    codes = label[...].astype(F32) * 2.0 + jnp.where(row >= 8 * 32 - 2, 2.0, 1.0)
    token = lax.broadcasted_iota(jnp.int32, (96, 16), 0)
    column = lax.broadcasted_iota(jnp.int32, (96, 16), 1)
    ones = jnp.ones((96, 16), F32)
    for win in range(4):
        wr, wc = divmod(win, 2)
        own = jnp.zeros((96, 16), F32)
        for r in range(4):
            hit = (token // 24 == r) & (column == 8 * wc + token % 8)
            own = own + jnp.where(hit, codes[4 * wr + r : 4 * wr + r + 1, :], 0.0)
        one = dot(own, ones, ((1,), (1,)))
        other = dot(ones, own, ((1,), (1,)))
        bias[win] = jnp.where(one == other, 0.0, -1e30)


def output_update(w, layer, j, mixed):
    return dot(mixed[...], weight_block(w, layer, 3, j)).reshape(2, 2, 4, LATENT, 8, 256)


def tile_rows(x, wr, columns=slice(None)):
    return x[4 * wr : 4 * wr + 4, :, :, columns].astype(F32)


def own_first(i, core):
    return (i % 2) * 2 + (core + i // 2) % 2


def first_sublayer(core, x, gain, w, normed, mixed, middle, hooks):
    def window(win):
        wr, wc = divmod(win, 2)
        return tile_rows(x, wr)[:, :, 8 * wc : 8 * wc + 8].reshape(96, D)

    normalise(window, gain, normed)
    looped(4, lambda i: attend_heads(own_first(i, core), 0, w, normed, None, mixed), hooks)
    for j in range(4):
        columns = slice(j * 256, (j + 1) * 256)
        update = output_update(w, 0, j, mixed)
        for wr in range(2):
            both = jnp.concatenate([update[wr, 0], update[wr, 1]], axis=2)
            middle[4 * wr : 4 * wr + 4, :, 0:16, columns] = tile_rows(x, wr, columns) + both


def second_sublayer(core, middle, gain, w, normed, mixed, bias, out, ready, hooks):
    def window(win):
        wr, wc = divmod(win, 2)
        return middle[4 * wr + 2 : 4 * wr + 6, :, 8 * wc + 4 : 8 * wc + 12, :].reshape(96, D)

    normalise(window, gain, normed)
    ready()
    looped(4, lambda i: attend_heads(own_first(i, core), 1, w, normed, bias, mixed), hooks)
    for j in range(4):
        columns = slice(j * 256, (j + 1) * 256)
        update = output_update(w, 1, j, mixed)
        for wr in range(2):
            halves = []
            for wc in range(2):
                own = middle[4 * wr + 2 : 4 * wr + 6, :, 8 * wc + 4 : 8 * wc + 12, columns]
                halves.append(own + update[wr, wc])
            both = jnp.concatenate(halves, axis=2).astype(BF16)
            out[4 * wr : 4 * wr + 4, :, :, columns] = both


class Edges:
    def __init__(self, place, middle, rows_out, columns_out, rows_in, columns_in, corner_in, send, recv):
        lat, lon = device_of(place)
        above, beside = (lat + 31) % 32, (lon + 3) % 4
        self.middle, self.rows_out, self.columns_out = middle, rows_out, columns_out
        self.rows_in, self.columns_in, self.corner_in = rows_in, columns_in, corner_in
        plan = (
            (rows_out, rows_in, (above, lon)),
            (columns_out, columns_in, (lat, beside)),
            (columns_out.at[pl.ds(0, 32)], corner_in, (above, beside)),
        )
        self.copies = [
            pltpu.make_async_remote_copy(
                src_ref=src,
                dst_ref=dst,
                send_sem=send.at[k],
                recv_sem=recv.at[k],
                device_id=other,
                device_id_type=MESH,
            )
            for k, (src, dst, other) in enumerate(plan)
        ]

    def start(self):
        middle = self.middle
        for r in range(2):
            self.rows_out[r] = middle[r, :, 0:16].reshape(48, D).astype(BF16)
        for part in range(6):
            cells = [divmod(part * 4 + i, LATENT) for i in range(4)]
            rows = jnp.concatenate([middle[r, q, 0:4] for r, q in cells], axis=0)
            self.columns_out[part * 16 : (part + 1) * 16] = rows.astype(BF16)
        for copy in self.copies:
            copy.start()

    def finish(self):
        middle = self.middle
        for copy in self.copies:
            copy.wait_recv()
        for r in range(2):
            middle[8 + r, :, 0:16] = self.rows_in[r].astype(F32).reshape(LATENT, 16, D)
        for part in range(6):
            rows = self.columns_in[part * 16 : (part + 1) * 16].astype(F32)
            for i in range(4):
                r, q = divmod(part * 4 + i, LATENT)
                middle[r, q, 16:20] = rows[i * 4 : (i + 1) * 4]
        for part in range(2):
            rows = self.corner_in[part * 16 : (part + 1) * 16].astype(F32)
            for i in range(4):
                r, q = divmod(part * 4 + i, LATENT)
                if r < 2:
                    middle[8 + r, q, 16:20] = rows[i * 4 : (i + 1) * 4]

    def drain(self):
        for copy in self.copies:
            copy.wait_send()


class Tiles:
    def __init__(self, place, latents, x, send, recv, own):
        lat, lon = device_of(place)

        def at(column):
            return pl.ds(pl.multiple_of(column * 16, 16), 16)

        self.own = pltpu.make_async_copy(latents.at[:, :, at(lon)], x.at[pl.ds(2 * lon, 2)], own)
        chip, core = lon // 2, lon % 2
        partners = ((1 - chip) * 2 + core, (1 - chip) * 2 + 1 - core, chip * 2 + 1 - core)
        self.out, self.arriving = [], []
        for k, other in enumerate(partners):
            for copies, row in ((self.out, lon), (self.arriving, other)):
                copies.append(
                    pltpu.make_async_remote_copy(
                        src_ref=latents.at[:, :, at(other)],
                        dst_ref=x.at[pl.ds(2 * row, 2)],
                        send_sem=send.at[k],
                        recv_sem=recv.at[k],
                        device_id=(lat, other),
                        device_id_type=MESH,
                    )
                )

    def start(self, here):
        if here:
            self.out[2].start()
            self.own.start()
        else:
            self.out[0].start()
            self.out[1].start()

    def finish(self):
        self.own.wait()
        for copy in self.arriving:
            copy.wait_recv()

    def drain(self):
        for copy in self.out:
            copy.wait_send()


WIDTHS = (384, 256, 512)
REDUCE_ORDERS = (("z", "x", "y"), ("x", "y", "z"), ("y", "z", "x"))


def kernel(factor, tokens, grads, kw_far, vw_far, ro_far, lq, gains, qkv, ow, label, *refs):
    out, grad_key, grad_value, grad_out = refs[:4]
    w, latents, x, rows_out, columns_out, rows_in, columns_in, corner_in = refs[4:12]
    packed, landing = refs[12:15], refs[15:45]
    g_send, g_recv, r_send, r_recv, t_send, t_recv, e_send, e_recv, near = refs[45:]
    place = my_place()
    y = place["y"]
    own = []
    mine = (y % 2, place["core"], place["z"], y // 2, place["x"])
    for tile in range(16):
        layer, block, half = tile // 8, tile // 2 % 4, tile % 2
        columns = pl.ds(128 * half, 128)
        src = ow.at[layer, :, columns] if block == 3 else qkv.at[layer, block, :, columns]
        own.append((src, w.at[(tile,) + mine]))
    own = [pltpu.make_async_copy(src, dst, near.at[i]) for i, (src, dst) in enumerate(own)]
    for copy in own:
        copy.start()
    weights_in = []
    for group in PARTS:
        first = sum(len(g) for g in weights_in)
        weights_in.append([Gather(place, w, g_send, g_recv, first + i, part) for i, part in enumerate(group)])
    sums = [
        Reduce(place, packed[i], landing[10 * i : 10 * i + 10], r_send.at[i], r_recv.at[i], REDUCE_ORDERS[i])
        for i in range(3)
    ]
    tiles = Tiles(place, latents, x, t_send, t_recv, near.at[16])

    def gathered(group, s):
        def hook():
            for part in weights_in[group]:
                part.step(s)

        return hook

    def reduced(s, *parts):
        def hook():
            for part in parts:
                sums[part].step(s)

        return hook

    def both(*hooks):
        def hook():
            for one in hooks:
                one()

        return hook

    def resampler(tok, grad, kw, vw, ro, kq, values, logits, weights, spread, d_att, att, d_logits, turned):
        pairs = ((kw_far, kw), (tokens, tok), (vw_far, vw), (grads, grad), (ro_far, ro))
        copies = [pltpu.make_async_copy(far, here, near.at[17 + i]) for i, (far, here) in enumerate(pairs)]
        for copy in copies:
            copy.start()
        greet(place)
        for copy in own:
            copy.wait()
        gathered(Q0, 0)()
        spread_heads(spread)
        both(gathered(O0, 0), gathered(Q1, 0), gathered(O1, 0))()
        copies[0].wait()
        key_queries(kw, lq, kq)
        gathered(Q0, 1)()
        copies[1].wait()
        copies[2].wait()
        resample_project(tok, vw, kq, values, logits, {0: gathered(Q1, 1), 1: gathered(Q0, 2)})
        resample_softmax(logits, weights)
        copies[3].wait()
        copies[4].wait()
        resample_cotangents(grad, ro, d_att)
        chip = y % 2

        def first_half():
            resample_latents(1 - chip, att, ro, lq, latents)
            tiles.start(False)

        hooks = {1: gathered(O0, 1), 3: both(gathered(O0, 2), gathered(O1, 1), first_half), 7: gathered(Q0, 3)}
        resample_mix(chip, values, weights, logits, spread, d_att, att, d_logits, hooks)
        resample_latents(chip, att, ro, lq, latents)
        tiles.start(True)
        out_gradient(grad, att, turned, packed[2])
        gathered(O0, 3)()
        hooks = {0: gathered(O1, 2), 1: reduced(0, 2), 2: gathered(Q1, 2)}
        token_gradients(tok, values, d_logits, turned, packed, hooks)

    pl.run_scoped(
        resampler,
        pltpu.VMEM((2, LEV, 64, D), BF16),
        pltpu.VMEM((2, LATENT, 64, D), BF16),
        pltpu.VMEM((D, D), BF16),
        pltpu.VMEM((D, D), BF16),
        pltpu.VMEM((D, D), BF16),
        pltpu.VMEM((2, D, 128), BF16),
        pltpu.VMEM((2, LEV, 64, D), BF16),
        pltpu.VMEM((2, LEV, 64, 128), F32),
        pltpu.VMEM((2, LEV, 64, 128), BF16),
        pltpu.VMEM((4, 128, 768), BF16),
        pltpu.VMEM((2, LATENT, 64, D), BF16),
        pltpu.VMEM((2, LATENT, 64, D), BF16),
        pltpu.VMEM((2, LEV, 64, 128), BF16),
        pltpu.VMEM((256, GROUPS * 208), BF16),
    )
    reduced(0, 0, 1)()
    reduced(1, 2)()

    def backbone(middle, normed, mixed, bias):
        edges = Edges(place, middle, rows_out, columns_out, rows_in, columns_in, corner_in, e_send, e_recv)
        core = place["core"]
        label_mask(label, place, bias)
        both(gathered(Q0, 4), gathered(O1, 3), reduced(1, 0, 1))()
        tiles.finish()
        hooks = {1: both(gathered(Q0, 5), gathered(O0, 4)), 3: gathered(O0, 5)}
        first_sublayer(core, x, gains[0:1, :], w, normed, mixed, middle, hooks)
        gathered(Q1, 3)()
        edges.start()
        gathered(O1, 4)()
        reduced(2, 2)()
        edges.finish()
        reduced(2, 1)()
        ready = both(gathered(Q1, 4), reduced(2, 0))
        hooks = {1: both(gathered(Q1, 5), reduced(3, 2)), 2: reduced(3, 0, 1), 3: gathered(O1, 5)}
        second_sublayer(core, middle, gains[1:2, :], w, normed, mixed, bias, out, ready, hooks)
        reduced(4, 0, 1, 2)()
        edges.drain()

    pl.run_scoped(
        backbone,
        pltpu.VMEM((10, LATENT, 24, D), F32),
        pltpu.VMEM((384, D), BF16),
        pltpu.VMEM((384, D), BF16),
        pltpu.VMEM((4, 96, 96), F32),
    )
    finish_gradients(factor, [part.result() for part in sums], lq, grad_key, grad_value, grad_out)
    tiles.drain()
    for group in weights_in + [sums]:
        for part in group:
            part.drain()


def whole(factor, tokens, grads, kw, vw, ro, lq, gains, qkv, ow, label):
    vmem, far = pl.BlockSpec(memory_space=pltpu.VMEM), pl.BlockSpec(memory_space=pl.ANY)
    landings = []
    for order, width in zip(REDUCE_ORDERS, WIDTHS):
        landings += landing_shapes(order, width)
    dma = pltpu.SemaphoreType.DMA
    return pl.pallas_call(
        functools.partial(kernel, factor),
        out_shape=[jax.ShapeDtypeStruct((8, LATENT, 16, D), BF16)] + [jax.ShapeDtypeStruct((8, D), F32)] * 3,
        in_specs=[far] * 5 + [vmem, vmem, far, far, vmem],
        out_specs=[vmem] * 4,
        scratch_shapes=[
            pltpu.VMEM((16, 2, 2, 4, 2, 4, 32, 128), BF16),
            pltpu.VMEM((2, LATENT, 64, D), BF16),
            pltpu.VMEM((8, LATENT, 16, D), BF16),
            pltpu.VMEM((2, 48, D), BF16),
            pltpu.VMEM((96, D), BF16),
            pltpu.VMEM((2, 48, D), BF16),
            pltpu.VMEM((96, D), BF16),
            pltpu.VMEM((32, D), BF16),
        ]
        + [pltpu.VMEM((2, 4, 2, 4, 2, 16, width), BF16) for width in WIDTHS]
        + landings
        + [dma((10, 16)), dma((10, 16)), dma((3, 10)), dma((3, 10))]
        + [dma((3,)), dma((3,)), dma((3,)), dma((3,)), dma((22,))],
        compiler_params=pltpu.CompilerParams(collective_id=0, has_side_effects=True, vmem_limit_bytes=63 * MIB),
    )(tokens, grads, kw, vw, ro, lq, gains, qkv, ow, label)


def hand_over_kernel(tile, *refs):
    refs[3][...] = tile[...]

    @pl.when(pl.program_id(0) == 0)
    def _():
        for i in range(3):
            refs[4 + i][...] = refs[i][...]


def hand_over(results):
    specs = [pl.BlockSpec((2, LATENT, 16, D), lambda i: (i, 0, 0, 0))] + [pl.BlockSpec((8, D), lambda i: (0, 0))] * 3
    return pl.pallas_call(
        hand_over_kernel,
        grid=(4,),
        out_shape=[jax.ShapeDtypeStruct(r.shape, r.dtype) for r in results],
        in_specs=specs,
        out_specs=specs,
    )(*results)


def local(
    level_tokens,
    latent_query,
    key_weight,
    value_weight,
    resample_out,
    norm_gain,
    qkv_weight,
    out_weight,
    window_label,
    grad_latents,
):
    factor = (2 * 64 * lax.axis_size("lat") * lax.axis_size("lon")) ** (-0.5)
    results = whole(
        factor,
        level_tokens.swapaxes(1, 2),
        grad_latents.swapaxes(1, 2),
        key_weight,
        value_weight,
        resample_out,
        latent_query,
        norm_gain,
        qkv_weight.swapaxes(1, 2),
        out_weight,
        window_label,
    )
    out, grad_key, grad_value, grad_out = hand_over(results)
    return (out.swapaxes(1, 2), grad_key, grad_value, grad_out)


def solution(mesh):
    in_specs = (
        P(("lat", "lon"), None, None, None),
        P(),
        P(),
        P(),
        P(),
        P(),
        P(None, "lat", None, "lon"),
        P(None, "lat", "lon"),
        P("lat", "lon"),
        P(("lat", "lon"), None, None, None),
    )
    out_specs = (
        P("lat", "lon", None, None),
        P(("lat", "lon"), None),
        P(("lat", "lon"), None),
        P(("lat", "lon"), None),
    )
    return jax.shard_map(local, mesh=mesh, in_specs=in_specs, out_specs=out_specs, check_vma=False)
```

```python
import functools

import jax
import jax.numpy as jnp
from jax import lax
from jax.experimental import pallas as pl
from jax.experimental.pallas import tpu as pltpu
from jax.sharding import PartitionSpec as P

MESH = pl.DeviceIdType.MESH
F32, BF16 = jnp.float32, jnp.bfloat16
D = 1024
HEADS = 16
LEV = 13
LATENT = 3
GROUPS = 8
MIB = 1024 * 1024


def dot(a, b, dims=((1,), (0,))):
    return lax.dot_general(a, b, (dims, ((), ())), preferred_element_type=F32)


def my_place():
    lat, lon = lax.axis_index("lat"), lax.axis_index("lon")
    return {
        "z": lat // 8,
        "y": ((lat // 4) % 2) * 2 + lon // 2,
        "x": lat % 4,
        "core": lon % 2,
    }


def device_of(place):
    lat = place["z"] * 8 + (place["y"] // 2) * 4 + place["x"]
    return (lat, (place["y"] % 2) * 2 + place["core"])


def moved(place, dim, delta):
    size = 2 if dim == "core" else 4
    other = dict(place)
    other[dim] = (place[dim] + delta + size) % size
    return device_of(other)


def pick(dim, value):
    if dim == "y":
        if value is None:
            return {"yh": slice(None), "yl": slice(None)}
        return {"yh": pl.ds(value // 2, 1), "yl": pl.ds(value % 2, 1)}
    return {dim: slice(None) if value is None else pl.ds(value, 1)}


def greet(place):
    barrier = pltpu.get_barrier_semaphore()
    others = [moved(place, dim, step) for dim in "xyz" for step in (1, -1, 2)] + [moved(place, "core", 1)]
    lat, lon = device_of(place)
    others += [(lat, (lon + k) % 4) for k in range(1, 4)]
    others += [((lat + step) % 32, (lon + turn) % 4) for step, turn in ((1, 0), (31, 0), (1, 1), (31, 3))]
    for other in others:
        pl.semaphore_signal(barrier, inc=1, device_id=other, device_id_type=MESH)
    return lambda: pl.semaphore_wait(barrier, len(others))


PARTS = (
    ((0, 3, ("x", "y", "z")), (3, 3, ("y", "z", "x")), (6, 2, ("z", "x", "y"))),
    ((8, 3, ("x", "y", "z")), (11, 3, ("y", "z", "x")), (14, 2, ("z", "x", "y"))),
)


class Gather:
    def __init__(self, place, w, send, recv, number, part):
        self.place, self.w, self.send, self.recv, self.number = place, w, send, recv, number
        first, count, self.order = part
        self.tiles = pl.ds(first, count)

    def region(self, phase, value, half=None, core=None):
        index = {}
        for position, dim in enumerate(self.order):
            if position < phase:
                index.update(pick(dim, None))
            elif position == phase:
                index.update(pick(dim, value))
            else:
                index.update(pick(dim, self.place[dim]))
        rows = slice(None) if half is None else pl.ds(16 * half, 16)
        core = self.place["core"] if core is None else core
        return self.w.at[self.tiles, index["yl"], core, index["z"], index["yh"], index["x"], rows, :]

    def copy(self, k, ref, other):
        return pltpu.make_async_remote_copy(
            src_ref=ref,
            dst_ref=ref,
            send_sem=self.send.at[self.number, k],
            recv_sem=self.recv.at[self.number, k],
            device_id=other,
            device_id_type=MESH,
        )

    def ring(self, phase, k):
        dim = self.order[phase]
        me = self.place[dim]
        if phase < 2:
            return self.copy(4 * phase + k, self.region(phase, me), moved(self.place, dim, (1, -1, 2)[k]))
        other = moved(self.place, dim, 1 if k % 2 == 0 else -1)
        if k < 2:
            return self.copy(4 * phase + k, self.region(phase, me), other)
        return self.copy(4 * phase + k, self.region(phase, (me + 7 - 2 * k) % 4, k - 2), other)

    def arrival(self, phase, k):
        dim = self.order[phase]
        me = self.place[dim]
        source = (me + (3, 1, 2, 2)[k]) % 4
        half = k - 2 if phase == 2 and k > 1 else None
        return self.copy(4 * phase + k, self.region(phase, source, half), moved(self.place, dim, 1))

    def across(self, k, core):
        ref = self.region(2, (self.place[self.order[2]] + (0, 3, 1, 2)[k]) % 4, None, core)
        return self.copy(12 + k, ref, moved(self.place, "core", 1))

    def step(self, s):
        core = self.place["core"]
        if s < 3:
            if s > 0:
                for k in range(3):
                    self.arrival(s - 1, k).wait_recv()
            for k in range(3 if s < 2 else 2):
                self.ring(s, k).start()
            if s == 2:
                self.across(0, core).start()
        elif s == 3:
            for k in range(2):
                self.arrival(2, k).wait_recv()
                self.ring(2, k + 2).start()
                self.across(k + 1, core).start()
        elif s == 4:
            for k in (2, 3):
                self.arrival(2, k).wait_recv()
            self.across(3, core).start()
        else:
            for k in range(4):
                self.across(k, 1 - core).wait_recv()

    def drain(self):
        for phase in range(3):
            for k in range(3 if phase < 2 else 4):
                self.ring(phase, k).wait_send()
        for k in range(4):
            self.across(k, self.place["core"]).wait_send()


def landing_shape(order, phase, columns):
    sizes = {"z": 4, "yh": 2, "x": 4, "yl": 2}
    for dim in order[: phase + 1]:
        for name in ("yh", "yl") if dim == "y" else (dim,):
            sizes[name] = 1
    return (sizes["z"], sizes["yh"], sizes["x"], sizes["yl"], 16, columns)


class Reduce:
    def __init__(self, place, p, landing, send, recv, order):
        self.place, self.p, self.landing = place, p, landing
        self.send, self.recv, self.order = send, recv, order

    def region(self, phase, value):
        index = {}
        for position, dim in enumerate(self.order):
            if position < phase:
                index.update(pick(dim, self.place[dim]))
            elif position == phase:
                index.update(pick(dim, value))
            else:
                index.update(pick(dim, None))
        return (self.place["core"], index["z"], index["yh"], index["x"], index["yl"])

    def copy(self, k, src, other):
        return pltpu.make_async_remote_copy(
            src_ref=src,
            dst_ref=self.landing[k],
            send_sem=self.send.at[k],
            recv_sem=self.recv.at[k],
            device_id=other,
            device_id_type=MESH,
        )

    def across(self):
        return self.copy(9, self.p.at[1 - self.place["core"]], moved(self.place, "core", 1))

    def ring(self, phase, k):
        dim = self.order[phase]
        step = (1, -1, 2)[k]
        target = (self.place[dim] + step + 4) % 4
        return self.copy(3 * phase + k, self.p.at[self.region(phase, target)], moved(self.place, dim, step))

    def step(self, s):
        if s == 0:
            self.across().start()
        elif s == 1:
            self.across().wait_recv()
            core = self.place["core"]
            for z in range(4):
                total = self.p[core, z].astype(F32) + self.landing[9][z].astype(F32)
                self.p[core, z] = total.astype(BF16)
        else:
            for k in range(3):
                self.ring(s - 2, k).wait_recv()
            region = self.region(s - 2, self.place[self.order[s - 2]])
            total = self.p[region].astype(F32)
            for k in range(3):
                total = total + self.landing[3 * (s - 2) + k][...].astype(F32)
            self.p[region] = total.astype(BF16)
        if 0 < s < 4:
            for k in range(3):
                self.ring(s - 1, k).start()

    def drain(self):
        for phase in range(3):
            for k in range(3):
                self.ring(phase, k).wait_send()
        self.across().wait_send()

    def result(self):
        y = self.place["y"]
        return self.p[self.place["core"], self.place["z"], y // 2, self.place["x"], y % 2].astype(F32)


def landing_shapes(order, columns):
    shapes = [pltpu.VMEM(landing_shape(order, phase, columns), BF16) for phase in range(3) for _ in range(3)]
    return shapes + [pltpu.VMEM((4, 2, 4, 2, 16, columns), BF16)]


def spread_queries(lq):
    row = lax.broadcasted_iota(jnp.int32, (128, D), 0)
    head = lax.broadcasted_iota(jnp.int32, (128, D), 1) // 64
    total = jnp.zeros((128, D), F32)
    for q in range(LATENT):
        total = total + jnp.where(row == q * HEADS + head, lq[q : q + 1, :].astype(F32), 0.0)
    return total.astype(BF16)


def finish_gradients(factor, sums, lq, grad_key, grad_value, grad_out):
    first, second, third = sums
    grad_value[:, 0:256] = first[:8, :256] * factor
    grad_value[:, 256:512] = second[:8] * factor
    grad_value[:, 512:768] = first[8:, :256] * factor
    grad_value[:, 768:1024] = second[8:] * factor
    grad_out[:, 0:512] = third[:8] * factor
    grad_out[:, 512:1024] = third[8:] * factor
    small = first[:8, 256:] * (factor * 0.125)
    high = small.astype(BF16)
    low = (small - high.astype(F32)).astype(BF16)
    queries = spread_queries(lq)
    grad_key[...] = dot(high, queries) + dot(low, queries)


def looped(count, body, hooks):
    def step(i, _):
        body(i)
        for at, hook in hooks.items():
            pl.when(i == at)(hook)
        return 0

    lax.fori_loop(0, count, step, 0)


def group_at(g):
    return g // 4, pl.ds(pl.multiple_of((g % 4) * 16, 16), 16)


def spread_heads(spread):
    row = lax.broadcasted_iota(jnp.int32, (128, 768), 0)
    column = lax.broadcasted_iota(jnp.int32, (128, 768), 1)
    for cb in range(4):
        hit = row == (column // 256) * HEADS + cb * 4 + (column % 256) // 64
        spread[cb] = jnp.where(hit, 1.0, 0.0).astype(BF16)


def key_queries(kw, lq, kq):
    queries = spread_queries(lq)

    def rows(i, _):
        at = pl.ds(pl.multiple_of(i * 256, 256), 256)
        total = dot(kw[at, :], queries, ((1,), (1,))) * 0.125
        high = total.astype(BF16)
        kq[0, at, :] = high
        kq[1, at, :] = (total - high.astype(F32)).astype(BF16)
        return 0

    lax.fori_loop(0, 4, rows, 0)


def resample_project(tok, vw, kq, values, logits, hooks):
    def project(r):
        rows = tok[r].reshape(LEV * 64, D)
        for nb in range(4):
            columns = slice(nb * 256, (nb + 1) * 256)
            values[r, :, :, columns] = dot(rows, vw[:, columns]).astype(BF16).reshape(LEV, 64, 256)
        logits[r] = (dot(rows, kq[0]) + dot(rows, kq[1])).reshape(LEV, 64, 128)

    looped(2, project, hooks)


def resample_softmax(logits, weights):
    def group(g, _):
        r, c = group_at(g)
        x = logits[r, :, c]
        x = jnp.exp(x - jnp.max(x, axis=0, keepdims=True))
        x = x / jnp.sum(x, axis=0, keepdims=True)
        logits[r, :, c] = x
        weights[r, :, c] = x.astype(BF16)
        return 0

    lax.fori_loop(0, GROUPS, group, 0)


def resample_cotangents(grad, ro, d_attended):
    rows = grad[...].reshape(384, D)
    for nb in range(4):
        columns = slice(nb * 256, (nb + 1) * 256)
        part = dot(rows, ro[columns, :], ((1,), (1,)))
        d_attended[:, :, :, columns] = part.astype(BF16).reshape(2, LATENT, 64, 256)


def resample_mix(chip, values, weights, probs, spread, d_attended, attended, d_logits, hooks):
    def group(g):
        r, tile = g % 2, ((chip + 1 + g // 4) % 2) * 2 + (g // 2) % 2
        c = pl.ds(pl.multiple_of(tile * 16, 16), 16)
        w = weights[r, :, c].reshape(208, 128)
        d_weights = jnp.zeros((208, 128), F32)
        for cb in range(4):
            columns = slice(cb * 256, (cb + 1) * 256)
            wide = dot(w, spread[cb])
            v = values[r, :, c, columns].astype(F32)
            d_v = jnp.zeros((LEV, 16, 256), F32)
            products = []
            for q in range(LATENT):
                wq = wide[:, q * 256 : (q + 1) * 256].reshape(LEV, 16, 256)
                da = d_attended[r, q, c, columns].astype(F32)[None]
                attended[r, q, c, columns] = jnp.sum(wq * v, axis=0).astype(BF16)
                d_v = d_v + wq * da
                products.append((v * da).astype(BF16).reshape(208, 256))
            values[r, :, c, columns] = d_v.astype(BF16)
            d_weights = d_weights + dot(jnp.concatenate(products, axis=1), spread[cb], ((1,), (1,)))
        p = probs[r, :, c]
        dw = d_weights.reshape(LEV, 16, 128)
        d_logits[r, :, c] = (p * (dw - jnp.sum(p * dw, axis=0, keepdims=True))).astype(BF16)

    looped(GROUPS, group, hooks)


def resample_latents(chip, attended, ro, lq, latents):
    cells = pl.ds(pl.multiple_of(chip * 32, 32), 32)
    rows = attended[:, :, cells, :].reshape(192, D)
    for nb in range(4):
        columns = slice(nb * 256, (nb + 1) * 256)
        part = dot(rows, ro[:, columns]).reshape(2, LATENT, 32, 256)
        part = part + lq[:, columns].astype(F32)[None, :, None, :]
        latents[:, :, cells, columns] = part.astype(BF16)


def pack_pair(left, right, p, z, columns):
    left = left.reshape(2, 4, 2, 2, 8, left.shape[-1])
    right = right.reshape(2, 4, 2, 2, 8, right.shape[-1])
    for core in range(2):
        both = jnp.concatenate([left[:, :, :, core], right[:, :, :, core]], axis=3)
        p[core, z, :, :, :, :, columns] = both.astype(BF16)


def out_gradient(grad, attended, turned, packed):
    def block(z):
        columns = pl.ds(pl.multiple_of(z * 256, 256), 256)
        turned[:, :384] = attended[:, :, :, columns].reshape(384, 256).T
        for nb in range(2):
            halves = []
            for half in range(2):
                c = slice(half * 512 + nb * 256, half * 512 + (nb + 1) * 256)
                halves.append(dot(turned[:, :384], grad[:, :, :, c].reshape(384, 256)))
            pack_pair(halves[0], halves[1], packed, z, slice(nb * 256, (nb + 1) * 256))

    looped(4, block, {})


def token_gradients(tok, d_values, d_logits, turned, packed, hooks):
    def block(z):
        columns = pl.ds(pl.multiple_of(z * 256, 256), 256)
        turned[...] = tok[:, :, :, columns].reshape(GROUPS * 208, 256).T
        for nb in range(2):
            halves = []
            for half in range(2):
                c = slice(half * 512 + nb * 256, half * 512 + (nb + 1) * 256)
                halves.append(dot(turned[...], d_values[:, :, :, c].reshape(GROUPS * 208, 256)))
            pack_pair(halves[0], halves[1], packed[nb], z, slice(0, 256))
        small = dot(turned[...], d_logits[...].reshape(GROUPS * 208, 128))
        pack_pair(small, jnp.zeros_like(small), packed[0], z, slice(256, 384))

    looped(4, block, hooks)


def normalise(window, gain, normed):
    for win in range(4):
        values = window(win)
        centred = values - jnp.mean(values, axis=-1, keepdims=True)
        spread = jnp.mean(centred * centred, axis=-1, keepdims=True)
        normed[win * 96 : (win + 1) * 96, :] = (centred * lax.rsqrt(spread + 1e-05) * gain).astype(BF16)


def weight_block(w, layer, block, j):
    tile = layer * 8 + block
    return jnp.concatenate([w[tile + 4 * i, j // 2, j % 2].reshape(D, 128) for i in range(2)], axis=1)


def attend_heads(j, layer, w, normed, bias, mixed):
    queries, keys, values = (dot(normed[...], weight_block(w, layer, block, j)) for block in range(3))
    queries, keys, values = (queries * 0.125).astype(BF16), keys.astype(BF16), values.astype(BF16)
    left = lax.broadcasted_iota(jnp.int32, (96, 128), 1) < 64
    columns = pl.ds(pl.multiple_of(j * 256, 256), 256)
    none = jnp.zeros((96, 128), BF16)
    for win in range(4):
        rows = slice(win * 96, (win + 1) * 96)
        q, k, v = queries[rows], keys[rows], values[rows]
        stacked = []
        for h in range(4):
            half = q[:, 128 * (h // 2) : 128 * (h // 2 + 1)]
            half = jnp.where(left, half, none) if h % 2 == 0 else jnp.where(left, none, half)
            stacked.append(jnp.concatenate([half, none] if h < 2 else [none, half], axis=1))
        logits = dot(jnp.concatenate(stacked, axis=0), k, ((1,), (1,)))
        if bias is not None:
            logits = (logits.reshape(4, 96, 96) + bias[win][None]).reshape(384, 96)
        e = jnp.exp(logits - jnp.max(logits, axis=-1, keepdims=True))
        e = e * (1.0 / jnp.sum(e, axis=-1, keepdims=True))
        out = dot(e.astype(BF16), v)
        pairs = [
            jnp.where(left, out[0:96, :128], out[96:192, :128]),
            jnp.where(left, out[192:288, 128:], out[288:384, 128:]),
        ]
        mixed[rows, columns] = jnp.concatenate(pairs, axis=1).astype(BF16)


def label_mask(label, place, bias):
    lat = device_of(place)[0]
    row = lax.broadcasted_iota(jnp.int32, (8, 16), 0) + lat * 8
    codes = label[...].astype(F32) * 2.0 + jnp.where(row >= 8 * 32 - 2, 2.0, 1.0)
    token = lax.broadcasted_iota(jnp.int32, (96, 16), 0)
    column = lax.broadcasted_iota(jnp.int32, (96, 16), 1)
    ones = jnp.ones((96, 16), F32)
    for win in range(4):
        wr, wc = divmod(win, 2)
        own = jnp.zeros((96, 16), F32)
        for r in range(4):
            hit = (token // 24 == r) & (column == 8 * wc + token % 8)
            own = own + jnp.where(hit, codes[4 * wr + r : 4 * wr + r + 1, :], 0.0)
        one = dot(own, ones, ((1,), (1,)))
        other = dot(ones, own, ((1,), (1,)))
        bias[win] = jnp.where(one == other, 0.0, -1e30)


def output_update(w, layer, j, mixed):
    return dot(mixed[...], weight_block(w, layer, 3, j)).reshape(2, 2, 4, LATENT, 8, 256)


def tile_rows(x, wr, columns=slice(None)):
    return x[4 * wr : 4 * wr + 4, :, :, columns].astype(F32)


def own_first(i, core):
    return (i % 2) * 2 + (core + i // 2) % 2


def first_sublayer(core, x, gain, w, normed, mixed, middle, ready, hooks):
    def window(win):
        wr, wc = divmod(win, 2)
        return tile_rows(x, wr)[:, :, 8 * wc : 8 * wc + 8].reshape(96, D)

    normalise(window, gain, normed)
    ready()
    looped(4, lambda i: attend_heads(own_first(i, core), 0, w, normed, None, mixed), hooks)
    for j in range(4):
        columns = slice(j * 256, (j + 1) * 256)
        update = output_update(w, 0, j, mixed)
        for wr in range(2):
            both = jnp.concatenate([update[wr, 0], update[wr, 1]], axis=2)
            middle[4 * wr : 4 * wr + 4, :, 0:16, columns] = tile_rows(x, wr, columns) + both


def second_sublayer(core, middle, gain, w, normed, mixed, bias, out, hooks):
    def window(win):
        wr, wc = divmod(win, 2)
        return middle[4 * wr + 2 : 4 * wr + 6, :, 8 * wc + 4 : 8 * wc + 12, :].reshape(96, D)

    normalise(window, gain, normed)
    looped(4, lambda i: attend_heads(own_first(i, core), 1, w, normed, bias, mixed), hooks)
    for j in range(4):
        columns = slice(j * 256, (j + 1) * 256)
        update = output_update(w, 1, j, mixed)
        for wr in range(2):
            halves = []
            for wc in range(2):
                own = middle[4 * wr + 2 : 4 * wr + 6, :, 8 * wc + 4 : 8 * wc + 12, columns]
                halves.append(own + update[wr, wc])
            both = jnp.concatenate(halves, axis=2).astype(BF16)
            out[4 * wr : 4 * wr + 4, :, :, columns] = both


class Edges:
    def __init__(self, place, middle, rows_out, columns_out, rows_in, columns_in, corner_in, send, recv):
        lat, lon = device_of(place)
        above, beside = (lat + 31) % 32, (lon + 3) % 4
        self.middle, self.rows_out, self.columns_out = middle, rows_out, columns_out
        self.rows_in, self.columns_in, self.corner_in = rows_in, columns_in, corner_in
        plan = (
            (rows_out, rows_in, (above, lon)),
            (columns_out, columns_in, (lat, beside)),
            (columns_out.at[pl.ds(0, 32)], corner_in, (above, beside)),
        )
        self.copies = [
            pltpu.make_async_remote_copy(
                src_ref=src,
                dst_ref=dst,
                send_sem=send.at[k],
                recv_sem=recv.at[k],
                device_id=other,
                device_id_type=MESH,
            )
            for k, (src, dst, other) in enumerate(plan)
        ]

    def start(self):
        middle = self.middle
        for r in range(2):
            self.rows_out[r] = middle[r, :, 0:16].reshape(48, D).astype(BF16)
        for part in range(6):
            cells = [divmod(part * 4 + i, LATENT) for i in range(4)]
            rows = jnp.concatenate([middle[r, q, 0:4] for r, q in cells], axis=0)
            self.columns_out[part * 16 : (part + 1) * 16] = rows.astype(BF16)
        for copy in self.copies:
            copy.start()

    def finish(self):
        middle = self.middle
        for copy in self.copies:
            copy.wait_recv()
        for r in range(2):
            middle[8 + r, :, 0:16] = self.rows_in[r].astype(F32).reshape(LATENT, 16, D)
        for part in range(6):
            rows = self.columns_in[part * 16 : (part + 1) * 16].astype(F32)
            for i in range(4):
                r, q = divmod(part * 4 + i, LATENT)
                middle[r, q, 16:20] = rows[i * 4 : (i + 1) * 4]
        for part in range(2):
            rows = self.corner_in[part * 16 : (part + 1) * 16].astype(F32)
            for i in range(4):
                r, q = divmod(part * 4 + i, LATENT)
                if r < 2:
                    middle[8 + r, q, 16:20] = rows[i * 4 : (i + 1) * 4]

    def drain(self):
        for copy in self.copies:
            copy.wait_send()


class Tiles:
    def __init__(self, place, latents, x, send, recv, own):
        lat, lon = device_of(place)

        def at(column):
            return pl.ds(pl.multiple_of(column * 16, 16), 16)

        self.own = pltpu.make_async_copy(latents.at[:, :, at(lon)], x.at[pl.ds(2 * lon, 2)], own)
        chip, core = lon // 2, lon % 2
        partners = ((1 - chip) * 2 + core, (1 - chip) * 2 + 1 - core, chip * 2 + 1 - core)
        self.out, self.arriving = [], []
        for k, other in enumerate(partners):
            for copies, row in ((self.out, lon), (self.arriving, other)):
                copies.append(
                    pltpu.make_async_remote_copy(
                        src_ref=latents.at[:, :, at(other)],
                        dst_ref=x.at[pl.ds(2 * row, 2)],
                        send_sem=send.at[k],
                        recv_sem=recv.at[k],
                        device_id=(lat, other),
                        device_id_type=MESH,
                    )
                )

    def start(self, here):
        if here:
            self.out[2].start()
            self.own.start()
        else:
            self.out[0].start()
            self.out[1].start()

    def finish(self):
        self.own.wait()
        for copy in self.arriving:
            copy.wait_recv()

    def drain(self):
        for copy in self.out:
            copy.wait_send()


WIDTHS = (384, 256, 512)
REDUCE_ORDERS = (("z", "x", "y"), ("x", "y", "z"), ("y", "z", "x"))


def kernel(factor, tokens, grads, kw_far, vw_far, ro_far, lq, gains, qkv, ow, label, *refs):
    out_far, grad_key, grad_value, grad_out = refs[:4]
    w, latents, x, rows_out, columns_out, rows_in, columns_in, corner_in = refs[4:12]
    packed, landing = refs[12:15], refs[15:45]
    g_send, g_recv, r_send, r_recv, t_send, t_recv, e_send, e_recv, near, out = refs[45:]
    leave = pltpu.make_async_copy(out, out_far, near.at[14])
    place = my_place()
    all_greeted = greet(place)
    y = place["y"]
    own = []
    for layer in range(2):
        for half in range(2):
            columns = pl.ds(128 * half, 128)
            tile = layer * 8 + half * 4
            mine = (y % 2, place["core"], place["z"], y // 2, place["x"])
            own.append((qkv.at[layer, :, :, columns], w.at[(pl.ds(tile, 3),) + mine]))
            own.append((ow.at[layer, :, columns], w.at[(tile + 3,) + mine]))
    own = [pltpu.make_async_copy(src, dst, near.at[i]) for i, (src, dst) in enumerate(own)]
    for copy in own:
        copy.start()
    layers = [
        [Gather(place, w, g_send, g_recv, 3 * layer + i, part) for i, part in enumerate(PARTS[layer])]
        for layer in range(2)
    ]
    sums = [
        Reduce(place, packed[i], landing[10 * i : 10 * i + 10], r_send.at[i], r_recv.at[i], REDUCE_ORDERS[i])
        for i in range(3)
    ]
    tiles = Tiles(place, latents, x, t_send, t_recv, near.at[8])

    def gathered(layer, s):
        def hook():
            for part in layers[layer]:
                part.step(s)

        return hook

    def reduced(s, *parts):
        def hook():
            for part in parts:
                sums[part].step(s)

        return hook

    def both(*hooks):
        def hook():
            for one in hooks:
                one()

        return hook

    def resampler(tok, grad, kw, vw, ro, kq, values, logits, weights, spread, d_att, att, d_logits, turned):
        pairs = ((kw_far, kw), (tokens, tok), (vw_far, vw), (grads, grad), (ro_far, ro))
        copies = [pltpu.make_async_copy(far, here, near.at[9 + i]) for i, (far, here) in enumerate(pairs)]
        for copy in copies:
            copy.start()
        all_greeted()
        for copy in own:
            copy.wait()
        gathered(0, 0)()
        spread_heads(spread)
        gathered(1, 0)()
        copies[0].wait()
        key_queries(kw, lq, kq)
        gathered(0, 1)()
        copies[1].wait()
        copies[2].wait()
        resample_project(tok, vw, kq, values, logits, {0: gathered(1, 1)})
        resample_softmax(logits, weights)
        copies[3].wait()
        copies[4].wait()
        resample_cotangents(grad, ro, d_att)
        chip = y % 2

        def first_half():
            resample_latents(1 - chip, att, ro, lq, latents)
            tiles.start(False)

        hooks = {0: gathered(0, 2), 3: first_half, 6: both(gathered(0, 3), gathered(1, 2))}
        resample_mix(chip, values, weights, logits, spread, d_att, att, d_logits, hooks)
        resample_latents(chip, att, ro, lq, latents)
        tiles.start(True)
        out_gradient(grad, att, turned, packed[2])
        reduced(0, 2)()
        token_gradients(tok, values, d_logits, turned, packed, {})

    pl.run_scoped(
        resampler,
        pltpu.VMEM((2, LEV, 64, D), BF16),
        pltpu.VMEM((2, LATENT, 64, D), BF16),
        pltpu.VMEM((D, D), BF16),
        pltpu.VMEM((D, D), BF16),
        pltpu.VMEM((D, D), BF16),
        pltpu.VMEM((2, D, 128), BF16),
        pltpu.VMEM((2, LEV, 64, D), BF16),
        pltpu.VMEM((2, LEV, 64, 128), F32),
        pltpu.VMEM((2, LEV, 64, 128), BF16),
        pltpu.VMEM((4, 128, 768), BF16),
        pltpu.VMEM((2, LATENT, 64, D), BF16),
        pltpu.VMEM((2, LATENT, 64, D), BF16),
        pltpu.VMEM((2, LEV, 64, 128), BF16),
        pltpu.VMEM((256, GROUPS * 208), BF16),
    )
    reduced(0, 0, 1)()
    reduced(1, 2)()

    def backbone(middle, normed, mixed, bias):
        edges = Edges(place, middle, rows_out, columns_out, rows_in, columns_in, corner_in, e_send, e_recv)
        core = place["core"]
        label_mask(label, place, bias)
        reduced(1, 1)()
        tiles.finish()
        ready = both(gathered(0, 4), reduced(1, 0))
        hooks = {1: gathered(0, 5), 2: gathered(1, 3)}
        first_sublayer(core, x, gains[0:1, :], w, normed, mixed, middle, ready, hooks)
        edges.start()
        gathered(1, 4)()
        reduced(2, 0, 1)()
        edges.finish()
        reduced(2, 2)()
        hooks = {1: both(gathered(1, 5), reduced(3, 0, 1)), 2: reduced(3, 2)}
        second_sublayer(core, middle, gains[1:2, :], w, normed, mixed, bias, out, hooks)
        leave.start()
        reduced(4, 0, 1, 2)()
        edges.drain()

    pl.run_scoped(
        backbone,
        pltpu.VMEM((10, LATENT, 24, D), F32),
        pltpu.VMEM((384, D), BF16),
        pltpu.VMEM((384, D), BF16),
        pltpu.VMEM((4, 96, 96), F32),
    )
    finish_gradients(factor, [part.result() for part in sums], lq, grad_key, grad_value, grad_out)
    leave.wait()
    tiles.drain()
    for part in layers[0] + layers[1] + sums:
        part.drain()


def whole(factor, tokens, grads, kw, vw, ro, lq, gains, qkv, ow, label):
    vmem, far = pl.BlockSpec(memory_space=pltpu.VMEM), pl.BlockSpec(memory_space=pl.ANY)
    landings = []
    for order, width in zip(REDUCE_ORDERS, WIDTHS):
        landings += landing_shapes(order, width)
    dma = pltpu.SemaphoreType.DMA
    return pl.pallas_call(
        functools.partial(kernel, factor),
        out_shape=[jax.ShapeDtypeStruct((8, LATENT, 16, D), BF16)] + [jax.ShapeDtypeStruct((8, D), F32)] * 3,
        in_specs=[far] * 5 + [vmem, vmem, far, far, vmem],
        out_specs=[far] + [vmem] * 3,
        scratch_shapes=[
            pltpu.VMEM((16, 2, 2, 4, 2, 4, 32, 128), BF16),
            pltpu.VMEM((2, LATENT, 64, D), BF16),
            pltpu.VMEM((8, LATENT, 16, D), BF16),
            pltpu.VMEM((2, 48, D), BF16),
            pltpu.VMEM((96, D), BF16),
            pltpu.VMEM((2, 48, D), BF16),
            pltpu.VMEM((96, D), BF16),
            pltpu.VMEM((32, D), BF16),
        ]
        + [pltpu.VMEM((2, 4, 2, 4, 2, 16, width), BF16) for width in WIDTHS]
        + landings
        + [dma((6, 16)), dma((6, 16)), dma((3, 10)), dma((3, 10))]
        + [dma((3,)), dma((3,)), dma((3,)), dma((3,)), dma((15,)), pltpu.VMEM((8, LATENT, 16, D), BF16)],
        compiler_params=pltpu.CompilerParams(collective_id=0, has_side_effects=True, vmem_limit_bytes=63 * MIB),
    )(tokens, grads, kw, vw, ro, lq, gains, qkv, ow, label)


def hand_over_kernel(*refs):
    count = len(refs) // 2
    for i in range(count):
        refs[count + i][...] = refs[i][...]


def hand_over(results):
    return pl.pallas_call(
        hand_over_kernel,
        out_shape=[jax.ShapeDtypeStruct(r.shape, r.dtype) for r in results],
        in_specs=[pl.BlockSpec(memory_space=pltpu.VMEM)] * len(results),
        out_specs=[pl.BlockSpec(memory_space=pltpu.VMEM)] * len(results),
    )(*results)


def local(
    level_tokens,
    latent_query,
    key_weight,
    value_weight,
    resample_out,
    norm_gain,
    qkv_weight,
    out_weight,
    window_label,
    grad_latents,
):
    factor = (2 * 64 * lax.axis_size("lat") * lax.axis_size("lon")) ** (-0.5)
    results = whole(
        factor,
        level_tokens.swapaxes(1, 2),
        grad_latents.swapaxes(1, 2),
        key_weight,
        value_weight,
        resample_out,
        latent_query,
        norm_gain,
        qkv_weight.swapaxes(1, 2),
        out_weight,
        window_label,
    )
    out, grad_key, grad_value, grad_out = hand_over(results)
    return (out.swapaxes(1, 2), grad_key, grad_value, grad_out)


def solution(mesh):
    in_specs = (
        P(("lat", "lon"), None, None, None),
        P(),
        P(),
        P(),
        P(),
        P(),
        P(None, "lat", None, "lon"),
        P(None, "lat", "lon"),
        P("lat", "lon"),
        P(("lat", "lon"), None, None, None),
    )
    out_specs = (
        P("lat", "lon", None, None),
        P(("lat", "lon"), None),
        P(("lat", "lon"), None),
        P(("lat", "lon"), None),
    )
    return jax.shard_map(local, mesh=mesh, in_specs=in_specs, out_specs=out_specs, check_vma=False)
```

```python
import functools

import jax
import jax.numpy as jnp
from jax import lax
from jax.experimental import pallas as pl
from jax.experimental.pallas import tpu as pltpu
from jax.sharding import PartitionSpec as P

MESH = pl.DeviceIdType.MESH
F32, BF16 = jnp.float32, jnp.bfloat16
D = 1024
HEADS = 16
LEV = 13
LATENT = 3
GROUPS = 8
MIB = 1024 * 1024


def dot(a, b, dims=((1,), (0,))):
    return lax.dot_general(a, b, (dims, ((), ())), preferred_element_type=F32)


def my_place():
    lat, lon = lax.axis_index("lat"), lax.axis_index("lon")
    return {
        "z": lat // 8,
        "y": ((lat // 4) % 2) * 2 + lon // 2,
        "x": lat % 4,
        "core": lon % 2,
    }


def device_of(place):
    lat = place["z"] * 8 + (place["y"] // 2) * 4 + place["x"]
    return (lat, (place["y"] % 2) * 2 + place["core"])


def moved(place, dim, delta):
    size = 2 if dim == "core" else 4
    other = dict(place)
    other[dim] = (place[dim] + delta + size) % size
    return device_of(other)


def pick(dim, value):
    if dim == "y":
        if value is None:
            return {"yh": slice(None), "yl": slice(None)}
        return {"yh": pl.ds(value // 2, 1), "yl": pl.ds(value % 2, 1)}
    return {dim: slice(None) if value is None else pl.ds(value, 1)}


def greet(place):
    barrier = pltpu.get_barrier_semaphore()
    others = [moved(place, dim, step) for dim in "xyz" for step in (1, -1, 2)] + [moved(place, "core", 1)]
    lat, lon = device_of(place)
    others += [(lat, (lon + k) % 4) for k in range(1, 4)]
    others += [((lat + step) % 32, (lon + turn) % 4) for step, turn in ((1, 0), (31, 0), (1, 1), (31, 3))]
    for other in others:
        pl.semaphore_signal(barrier, inc=1, device_id=other, device_id_type=MESH)
    return lambda: pl.semaphore_wait(barrier, len(others))


PARTS = (
    ((0, 3, ("x", "y", "z")), (3, 3, ("y", "z", "x")), (6, 2, ("z", "x", "y"))),
    ((8, 3, ("x", "y", "z")), (11, 3, ("y", "z", "x")), (14, 2, ("z", "x", "y"))),
)


class Gather:
    def __init__(self, place, w, send, recv, number, part):
        self.place, self.w, self.send, self.recv, self.number = place, w, send, recv, number
        first, count, self.order = part
        self.tiles = pl.ds(first, count)

    def region(self, phase, value, half=None, core=None):
        index = {}
        for position, dim in enumerate(self.order):
            if position < phase:
                index.update(pick(dim, None))
            elif position == phase:
                index.update(pick(dim, value))
            else:
                index.update(pick(dim, self.place[dim]))
        rows = slice(None) if half is None else pl.ds(16 * half, 16)
        core = self.place["core"] if core is None else core
        return self.w.at[self.tiles, index["yl"], core, index["z"], index["yh"], index["x"], rows, :]

    def copy(self, k, ref, other):
        return pltpu.make_async_remote_copy(
            src_ref=ref,
            dst_ref=ref,
            send_sem=self.send.at[self.number, k],
            recv_sem=self.recv.at[self.number, k],
            device_id=other,
            device_id_type=MESH,
        )

    def ring(self, phase, k):
        dim = self.order[phase]
        me = self.place[dim]
        if phase < 2:
            return self.copy(4 * phase + k, self.region(phase, me), moved(self.place, dim, (1, -1, 2)[k]))
        other = moved(self.place, dim, 1 if k % 2 == 0 else -1)
        source = (me + (0, 0, 3, 1, 0, 0)[k]) % 4
        return self.copy(self.slot(k), self.region(2, source, (0, 1, 0, 1, 1, 0)[k]), other)

    def slot(self, k):
        return 8 + k if k < 4 else 12 + k

    def arrival(self, phase, k):
        dim = self.order[phase]
        me = self.place[dim]
        other = moved(self.place, dim, 1)
        source = (me + (3, 1, 2, 2, 3, 1)[k]) % 4
        if phase < 2:
            return self.copy(4 * phase + k, self.region(phase, source), other)
        return self.copy(self.slot(k), self.region(2, source, (0, 1, 0, 1, 1, 0)[k]), other)

    def across(self, k, core):
        ref = self.region(2, (self.place[self.order[2]] + (0, 3, 1, 2)[k]) % 4, None, core)
        return self.copy(12 + k, ref, moved(self.place, "core", 1))

    def step(self, s):
        core = self.place["core"]
        if s < 3:
            if s > 0:
                for k in range(3):
                    self.arrival(s - 1, k).wait_recv()
            for k in range(3) if s < 2 else (0, 1, 4, 5):
                self.ring(s, k).start()
            if s == 2:
                self.across(0, core).start()
        elif s == 3:
            for k in range(2):
                self.arrival(2, k).wait_recv()
                self.ring(2, k + 2).start()
        elif s == 4:
            for k in range(2):
                self.arrival(2, k + 4).wait_recv()
                self.across(k + 1, core).start()
        elif s == 5:
            for k in (2, 3):
                self.arrival(2, k).wait_recv()
            self.across(3, core).start()
        else:
            for k in range(4):
                self.across(k, 1 - core).wait_recv()

    def drain(self):
        for phase in range(3):
            for k in range(3 if phase < 2 else 6):
                self.ring(phase, k).wait_send()
        for k in range(4):
            self.across(k, self.place["core"]).wait_send()


def landing_shape(order, phase, columns):
    sizes = {"z": 4, "yh": 2, "x": 4, "yl": 2}
    for dim in order[: phase + 1]:
        for name in ("yh", "yl") if dim == "y" else (dim,):
            sizes[name] = 1
    return (sizes["z"], sizes["yh"], sizes["x"], sizes["yl"], 16, columns)


class Reduce:
    def __init__(self, place, p, landing, send, recv, order):
        self.place, self.p, self.landing = place, p, landing
        self.send, self.recv, self.order = send, recv, order

    def region(self, phase, value):
        index = {}
        for position, dim in enumerate(self.order):
            if position < phase:
                index.update(pick(dim, self.place[dim]))
            elif position == phase:
                index.update(pick(dim, value))
            else:
                index.update(pick(dim, None))
        return (self.place["core"], index["z"], index["yh"], index["x"], index["yl"])

    def copy(self, k, src, other):
        return pltpu.make_async_remote_copy(
            src_ref=src,
            dst_ref=self.landing[k],
            send_sem=self.send.at[k],
            recv_sem=self.recv.at[k],
            device_id=other,
            device_id_type=MESH,
        )

    def across(self):
        return self.copy(9, self.p.at[1 - self.place["core"]], moved(self.place, "core", 1))

    def ring(self, phase, k):
        dim = self.order[phase]
        step = (1, -1, 2)[k]
        target = (self.place[dim] + step + 4) % 4
        return self.copy(3 * phase + k, self.p.at[self.region(phase, target)], moved(self.place, dim, step))

    def step(self, s):
        if s == 0:
            self.across().start()
        elif s == 1:
            self.across().wait_recv()
            core = self.place["core"]
            for z in range(4):
                total = self.p[core, z].astype(F32) + self.landing[9][z].astype(F32)
                self.p[core, z] = total.astype(BF16)
        else:
            for k in range(3):
                self.ring(s - 2, k).wait_recv()
            region = self.region(s - 2, self.place[self.order[s - 2]])
            total = self.p[region].astype(F32)
            for k in range(3):
                total = total + self.landing[3 * (s - 2) + k][...].astype(F32)
            self.p[region] = total.astype(BF16)
        if 0 < s < 4:
            for k in range(3):
                self.ring(s - 1, k).start()

    def drain(self):
        for phase in range(3):
            for k in range(3):
                self.ring(phase, k).wait_send()
        self.across().wait_send()

    def result(self):
        y = self.place["y"]
        return self.p[self.place["core"], self.place["z"], y // 2, self.place["x"], y % 2].astype(F32)


def landing_shapes(order, columns):
    shapes = [pltpu.VMEM(landing_shape(order, phase, columns), BF16) for phase in range(3) for _ in range(3)]
    return shapes + [pltpu.VMEM((4, 2, 4, 2, 16, columns), BF16)]


def spread_queries(lq):
    row = lax.broadcasted_iota(jnp.int32, (128, D), 0)
    head = lax.broadcasted_iota(jnp.int32, (128, D), 1) // 64
    total = jnp.zeros((128, D), F32)
    for q in range(LATENT):
        total = total + jnp.where(row == q * HEADS + head, lq[q : q + 1, :].astype(F32), 0.0)
    return total.astype(BF16)


def finish_gradients(factor, sums, lq, grad_key, grad_value, grad_out):
    first, second, third = sums
    grad_value[:, 0:256] = first[:8, :256] * factor
    grad_value[:, 256:512] = second[:8] * factor
    grad_value[:, 512:768] = first[8:, :256] * factor
    grad_value[:, 768:1024] = second[8:] * factor
    grad_out[:, 0:512] = third[:8] * factor
    grad_out[:, 512:1024] = third[8:] * factor
    small = first[:8, 256:] * (factor * 0.125)
    high = small.astype(BF16)
    low = (small - high.astype(F32)).astype(BF16)
    queries = spread_queries(lq)
    grad_key[...] = dot(high, queries) + dot(low, queries)


def looped(count, body, hooks):
    def step(i, _):
        body(i)
        for at, hook in hooks.items():
            pl.when(i == at)(hook)
        return 0

    lax.fori_loop(0, count, step, 0)


def group_at(g):
    return g // 4, pl.ds(pl.multiple_of((g % 4) * 16, 16), 16)


def spread_heads(spread):
    row = lax.broadcasted_iota(jnp.int32, (128, 768), 0)
    column = lax.broadcasted_iota(jnp.int32, (128, 768), 1)
    for cb in range(4):
        hit = row == (column // 256) * HEADS + cb * 4 + (column % 256) // 64
        spread[cb] = jnp.where(hit, 1.0, 0.0).astype(BF16)


def key_queries(kw, lq, kq):
    queries = spread_queries(lq)

    def rows(i, _):
        at = pl.ds(pl.multiple_of(i * 256, 256), 256)
        total = dot(kw[at, :], queries, ((1,), (1,))) * 0.125
        high = total.astype(BF16)
        kq[0, at, :] = high
        kq[1, at, :] = (total - high.astype(F32)).astype(BF16)
        return 0

    lax.fori_loop(0, 4, rows, 0)


def resample_project(tok, vw, kq, values, logits, hooks):
    def project(r):
        rows = tok[r].reshape(LEV * 64, D)
        for nb in range(4):
            columns = slice(nb * 256, (nb + 1) * 256)
            values[r, :, :, columns] = dot(rows, vw[:, columns]).astype(BF16).reshape(LEV, 64, 256)
        logits[r] = (dot(rows, kq[0]) + dot(rows, kq[1])).reshape(LEV, 64, 128)

    looped(2, project, hooks)


def resample_softmax(logits, weights):
    def group(g, _):
        r, c = group_at(g)
        x = logits[r, :, c]
        x = jnp.exp(x - jnp.max(x, axis=0, keepdims=True))
        x = x / jnp.sum(x, axis=0, keepdims=True)
        logits[r, :, c] = x
        weights[r, :, c] = x.astype(BF16)
        return 0

    lax.fori_loop(0, GROUPS, group, 0)


def resample_cotangents(grad, ro, d_attended):
    rows = grad[...].reshape(384, D)
    for nb in range(4):
        columns = slice(nb * 256, (nb + 1) * 256)
        part = dot(rows, ro[columns, :], ((1,), (1,)))
        d_attended[:, :, :, columns] = part.astype(BF16).reshape(2, LATENT, 64, 256)


def resample_mix(chip, values, weights, probs, spread, d_attended, attended, d_logits, hooks):
    def group(g):
        r, tile = g % 2, ((chip + 1 + g // 4) % 2) * 2 + (g // 2) % 2
        c = pl.ds(pl.multiple_of(tile * 16, 16), 16)
        w = weights[r, :, c].reshape(208, 128)
        d_weights = jnp.zeros((208, 128), F32)
        for cb in range(4):
            columns = slice(cb * 256, (cb + 1) * 256)
            wide = dot(w, spread[cb])
            v = values[r, :, c, columns].astype(F32)
            d_v = jnp.zeros((LEV, 16, 256), F32)
            products = []
            for q in range(LATENT):
                wq = wide[:, q * 256 : (q + 1) * 256].reshape(LEV, 16, 256)
                da = d_attended[r, q, c, columns].astype(F32)[None]
                attended[r, q, c, columns] = jnp.sum(wq * v, axis=0).astype(BF16)
                d_v = d_v + wq * da
                products.append((v * da).astype(BF16).reshape(208, 256))
            values[r, :, c, columns] = d_v.astype(BF16)
            d_weights = d_weights + dot(jnp.concatenate(products, axis=1), spread[cb], ((1,), (1,)))
        p = probs[r, :, c]
        dw = d_weights.reshape(LEV, 16, 128)
        d_logits[r, :, c] = (p * (dw - jnp.sum(p * dw, axis=0, keepdims=True))).astype(BF16)

    looped(GROUPS, group, hooks)


def resample_latents(chip, attended, ro, lq, latents):
    cells = pl.ds(pl.multiple_of(chip * 32, 32), 32)
    rows = attended[:, :, cells, :].reshape(192, D)
    for nb in range(4):
        columns = slice(nb * 256, (nb + 1) * 256)
        part = dot(rows, ro[:, columns]).reshape(2, LATENT, 32, 256)
        part = part + lq[:, columns].astype(F32)[None, :, None, :]
        latents[:, :, cells, columns] = part.astype(BF16)


def pack_pair(left, right, p, z, columns):
    left = left.reshape(2, 4, 2, 2, 8, left.shape[-1])
    right = right.reshape(2, 4, 2, 2, 8, right.shape[-1])
    for core in range(2):
        both = jnp.concatenate([left[:, :, :, core], right[:, :, :, core]], axis=3)
        p[core, z, :, :, :, :, columns] = both.astype(BF16)


def out_gradient(grad, attended, turned, packed):
    def block(z):
        columns = pl.ds(pl.multiple_of(z * 256, 256), 256)
        turned[:, :384] = attended[:, :, :, columns].reshape(384, 256).T
        for nb in range(2):
            halves = []
            for half in range(2):
                c = slice(half * 512 + nb * 256, half * 512 + (nb + 1) * 256)
                halves.append(dot(turned[:, :384], grad[:, :, :, c].reshape(384, 256)))
            pack_pair(halves[0], halves[1], packed, z, slice(nb * 256, (nb + 1) * 256))

    looped(4, block, {})


def token_gradients(tok, d_values, d_logits, turned, packed, hooks):
    def block(z):
        columns = pl.ds(pl.multiple_of(z * 256, 256), 256)
        turned[...] = tok[:, :, :, columns].reshape(GROUPS * 208, 256).T
        for nb in range(2):
            halves = []
            for half in range(2):
                c = slice(half * 512 + nb * 256, half * 512 + (nb + 1) * 256)
                halves.append(dot(turned[...], d_values[:, :, :, c].reshape(GROUPS * 208, 256)))
            pack_pair(halves[0], halves[1], packed[nb], z, slice(0, 256))
        small = dot(turned[...], d_logits[...].reshape(GROUPS * 208, 128))
        pack_pair(small, jnp.zeros_like(small), packed[0], z, slice(256, 384))

    looped(4, block, hooks)


def normalise(window, gain, normed):
    for win in range(4):
        values = window(win)
        centred = values - jnp.mean(values, axis=-1, keepdims=True)
        spread = jnp.mean(centred * centred, axis=-1, keepdims=True)
        normed[win * 96 : (win + 1) * 96, :] = (centred * lax.rsqrt(spread + 1e-05) * gain).astype(BF16)


def weight_block(w, layer, block, j):
    tile = layer * 8 + block
    return jnp.concatenate([w[tile + 4 * i, j // 2, j % 2].reshape(D, 128) for i in range(2)], axis=1)


def attend_heads(j, layer, w, normed, bias, mixed):
    queries, keys, values = (dot(normed[...], weight_block(w, layer, block, j)) for block in range(3))
    queries, keys, values = (queries * 0.125).astype(BF16), keys.astype(BF16), values.astype(BF16)
    left = lax.broadcasted_iota(jnp.int32, (96, 128), 1) < 64
    columns = pl.ds(pl.multiple_of(j * 256, 256), 256)
    none = jnp.zeros((96, 128), BF16)
    for win in range(4):
        rows = slice(win * 96, (win + 1) * 96)
        q, k, v = queries[rows], keys[rows], values[rows]
        stacked = []
        for h in range(4):
            half = q[:, 128 * (h // 2) : 128 * (h // 2 + 1)]
            half = jnp.where(left, half, none) if h % 2 == 0 else jnp.where(left, none, half)
            stacked.append(jnp.concatenate([half, none] if h < 2 else [none, half], axis=1))
        logits = dot(jnp.concatenate(stacked, axis=0), k, ((1,), (1,)))
        if bias is not None:
            logits = (logits.reshape(4, 96, 96) + bias[win][None]).reshape(384, 96)
        e = jnp.exp(logits - jnp.max(logits, axis=-1, keepdims=True))
        e = e * (1.0 / jnp.sum(e, axis=-1, keepdims=True))
        out = dot(e.astype(BF16), v)
        pairs = [
            jnp.where(left, out[0:96, :128], out[96:192, :128]),
            jnp.where(left, out[192:288, 128:], out[288:384, 128:]),
        ]
        mixed[rows, columns] = jnp.concatenate(pairs, axis=1).astype(BF16)


def label_mask(label, place, bias):
    lat = device_of(place)[0]
    row = lax.broadcasted_iota(jnp.int32, (8, 16), 0) + lat * 8
    codes = label[...].astype(F32) * 2.0 + jnp.where(row >= 8 * 32 - 2, 2.0, 1.0)
    token = lax.broadcasted_iota(jnp.int32, (96, 16), 0)
    column = lax.broadcasted_iota(jnp.int32, (96, 16), 1)
    ones = jnp.ones((96, 16), F32)
    for win in range(4):
        wr, wc = divmod(win, 2)
        own = jnp.zeros((96, 16), F32)
        for r in range(4):
            hit = (token // 24 == r) & (column == 8 * wc + token % 8)
            own = own + jnp.where(hit, codes[4 * wr + r : 4 * wr + r + 1, :], 0.0)
        one = dot(own, ones, ((1,), (1,)))
        other = dot(ones, own, ((1,), (1,)))
        bias[win] = jnp.where(one == other, 0.0, -1e30)


def output_update(w, layer, j, mixed):
    return dot(mixed[...], weight_block(w, layer, 3, j)).reshape(2, 2, 4, LATENT, 8, 256)


def tile_rows(x, wr, columns=slice(None)):
    return x[4 * wr : 4 * wr + 4, :, :, columns].astype(F32)


def own_first(i, core):
    return (i % 2) * 2 + (core + i // 2) % 2


def first_sublayer(core, x, gain, w, normed, mixed, middle, ready, hooks):
    def window(win):
        wr, wc = divmod(win, 2)
        return tile_rows(x, wr)[:, :, 8 * wc : 8 * wc + 8].reshape(96, D)

    normalise(window, gain, normed)
    ready()
    looped(4, lambda i: attend_heads(own_first(i, core), 0, w, normed, None, mixed), hooks)
    for j in range(4):
        columns = slice(j * 256, (j + 1) * 256)
        update = output_update(w, 0, j, mixed)
        for wr in range(2):
            both = jnp.concatenate([update[wr, 0], update[wr, 1]], axis=2)
            middle[4 * wr : 4 * wr + 4, :, 0:16, columns] = tile_rows(x, wr, columns) + both


def second_sublayer(core, middle, gain, w, normed, mixed, bias, out, hooks):
    def window(win):
        wr, wc = divmod(win, 2)
        return middle[4 * wr + 2 : 4 * wr + 6, :, 8 * wc + 4 : 8 * wc + 12, :].reshape(96, D)

    normalise(window, gain, normed)
    looped(4, lambda i: attend_heads(own_first(i, core), 1, w, normed, bias, mixed), hooks)
    for j in range(4):
        columns = slice(j * 256, (j + 1) * 256)
        update = output_update(w, 1, j, mixed)
        for wr in range(2):
            halves = []
            for wc in range(2):
                own = middle[4 * wr + 2 : 4 * wr + 6, :, 8 * wc + 4 : 8 * wc + 12, columns]
                halves.append(own + update[wr, wc])
            both = jnp.concatenate(halves, axis=2).astype(BF16)
            out[4 * wr : 4 * wr + 4, :, :, columns] = both


class Edges:
    def __init__(self, place, middle, rows_out, columns_out, rows_in, columns_in, corner_in, send, recv):
        lat, lon = device_of(place)
        above, beside = (lat + 31) % 32, (lon + 3) % 4
        self.middle, self.rows_out, self.columns_out = middle, rows_out, columns_out
        self.rows_in, self.columns_in, self.corner_in = rows_in, columns_in, corner_in
        plan = (
            (rows_out, rows_in, (above, lon)),
            (columns_out, columns_in, (lat, beside)),
            (columns_out.at[pl.ds(0, 32)], corner_in, (above, beside)),
        )
        self.copies = [
            pltpu.make_async_remote_copy(
                src_ref=src,
                dst_ref=dst,
                send_sem=send.at[k],
                recv_sem=recv.at[k],
                device_id=other,
                device_id_type=MESH,
            )
            for k, (src, dst, other) in enumerate(plan)
        ]

    def start(self):
        middle = self.middle
        for r in range(2):
            self.rows_out[r] = middle[r, :, 0:16].reshape(48, D).astype(BF16)
        for part in range(6):
            cells = [divmod(part * 4 + i, LATENT) for i in range(4)]
            rows = jnp.concatenate([middle[r, q, 0:4] for r, q in cells], axis=0)
            self.columns_out[part * 16 : (part + 1) * 16] = rows.astype(BF16)
        for copy in self.copies:
            copy.start()

    def finish(self):
        middle = self.middle
        for copy in self.copies:
            copy.wait_recv()
        for r in range(2):
            middle[8 + r, :, 0:16] = self.rows_in[r].astype(F32).reshape(LATENT, 16, D)
        for part in range(6):
            rows = self.columns_in[part * 16 : (part + 1) * 16].astype(F32)
            for i in range(4):
                r, q = divmod(part * 4 + i, LATENT)
                middle[r, q, 16:20] = rows[i * 4 : (i + 1) * 4]
        for part in range(2):
            rows = self.corner_in[part * 16 : (part + 1) * 16].astype(F32)
            for i in range(4):
                r, q = divmod(part * 4 + i, LATENT)
                if r < 2:
                    middle[8 + r, q, 16:20] = rows[i * 4 : (i + 1) * 4]

    def drain(self):
        for copy in self.copies:
            copy.wait_send()


class Tiles:
    def __init__(self, place, latents, x, send, recv, own):
        lat, lon = device_of(place)

        def at(column):
            return pl.ds(pl.multiple_of(column * 16, 16), 16)

        self.own = pltpu.make_async_copy(latents.at[:, :, at(lon)], x.at[pl.ds(2 * lon, 2)], own)
        chip, core = lon // 2, lon % 2
        partners = ((1 - chip) * 2 + core, (1 - chip) * 2 + 1 - core, chip * 2 + 1 - core)
        self.out, self.arriving = [], []
        for k, other in enumerate(partners):
            for copies, row in ((self.out, lon), (self.arriving, other)):
                copies.append(
                    pltpu.make_async_remote_copy(
                        src_ref=latents.at[:, :, at(other)],
                        dst_ref=x.at[pl.ds(2 * row, 2)],
                        send_sem=send.at[k],
                        recv_sem=recv.at[k],
                        device_id=(lat, other),
                        device_id_type=MESH,
                    )
                )

    def start(self, here):
        if here:
            self.out[2].start()
            self.own.start()
        else:
            self.out[0].start()
            self.out[1].start()

    def finish(self):
        self.own.wait()
        for copy in self.arriving:
            copy.wait_recv()

    def drain(self):
        for copy in self.out:
            copy.wait_send()


WIDTHS = (384, 256, 512)
REDUCE_ORDERS = (("z", "x", "y"), ("x", "y", "z"), ("y", "z", "x"))


def kernel(factor, tokens, grads, kw_far, vw_far, ro_far, lq, gains, qkv, ow, label, *refs):
    out_far, grad_key, grad_value, grad_out = refs[:4]
    w, latents, x, rows_out, columns_out, rows_in, columns_in, corner_in = refs[4:12]
    packed, landing = refs[12:15], refs[15:45]
    g_send, g_recv, r_send, r_recv, t_send, t_recv, e_send, e_recv, near, out = refs[45:]
    leave = pltpu.make_async_copy(out, out_far, near.at[14])
    place = my_place()
    all_greeted = greet(place)
    y = place["y"]
    own = []
    for layer in range(2):
        for half in range(2):
            columns = pl.ds(128 * half, 128)
            tile = layer * 8 + half * 4
            mine = (y % 2, place["core"], place["z"], y // 2, place["x"])
            own.append((qkv.at[layer, :, :, columns], w.at[(pl.ds(tile, 3),) + mine]))
            own.append((ow.at[layer, :, columns], w.at[(tile + 3,) + mine]))
    own = [pltpu.make_async_copy(src, dst, near.at[i]) for i, (src, dst) in enumerate(own)]
    for copy in own:
        copy.start()
    layers = [
        [Gather(place, w, g_send, g_recv, 3 * layer + i, part) for i, part in enumerate(PARTS[layer])]
        for layer in range(2)
    ]
    sums = [
        Reduce(place, packed[i], landing[10 * i : 10 * i + 10], r_send.at[i], r_recv.at[i], REDUCE_ORDERS[i])
        for i in range(3)
    ]
    tiles = Tiles(place, latents, x, t_send, t_recv, near.at[8])

    def gathered(layer, s):
        def hook():
            for part in layers[layer]:
                part.step(s)

        return hook

    def reduced(s, *parts):
        def hook():
            for part in parts:
                sums[part].step(s)

        return hook

    def both(*hooks):
        def hook():
            for one in hooks:
                one()

        return hook

    def resampler(tok, grad, kw, vw, ro, kq, values, logits, weights, spread, d_att, att, d_logits, turned):
        pairs = ((kw_far, kw), (tokens, tok), (vw_far, vw), (grads, grad), (ro_far, ro))
        copies = [pltpu.make_async_copy(far, here, near.at[9 + i]) for i, (far, here) in enumerate(pairs)]
        for copy in copies:
            copy.start()
        all_greeted()
        for copy in own:
            copy.wait()
        gathered(0, 0)()
        spread_heads(spread)
        gathered(1, 0)()
        copies[0].wait()
        key_queries(kw, lq, kq)
        gathered(0, 1)()
        copies[1].wait()
        copies[2].wait()
        resample_project(tok, vw, kq, values, logits, {0: gathered(1, 1)})
        resample_softmax(logits, weights)
        copies[3].wait()
        copies[4].wait()
        resample_cotangents(grad, ro, d_att)
        chip = y % 2

        def first_half():
            resample_latents(1 - chip, att, ro, lq, latents)
            tiles.start(False)

        hooks = {0: gathered(0, 2), 3: first_half, 6: both(gathered(0, 3), gathered(1, 2))}
        resample_mix(chip, values, weights, logits, spread, d_att, att, d_logits, hooks)
        resample_latents(chip, att, ro, lq, latents)
        tiles.start(True)
        out_gradient(grad, att, turned, packed[2])
        reduced(0, 2)()
        token_gradients(tok, values, d_logits, turned, packed, {0: gathered(0, 4)})

    pl.run_scoped(
        resampler,
        pltpu.VMEM((2, LEV, 64, D), BF16),
        pltpu.VMEM((2, LATENT, 64, D), BF16),
        pltpu.VMEM((D, D), BF16),
        pltpu.VMEM((D, D), BF16),
        pltpu.VMEM((D, D), BF16),
        pltpu.VMEM((2, D, 128), BF16),
        pltpu.VMEM((2, LEV, 64, D), BF16),
        pltpu.VMEM((2, LEV, 64, 128), F32),
        pltpu.VMEM((2, LEV, 64, 128), BF16),
        pltpu.VMEM((4, 128, 768), BF16),
        pltpu.VMEM((2, LATENT, 64, D), BF16),
        pltpu.VMEM((2, LATENT, 64, D), BF16),
        pltpu.VMEM((2, LEV, 64, 128), BF16),
        pltpu.VMEM((256, GROUPS * 208), BF16),
    )
    reduced(0, 0, 1)()
    reduced(1, 2)()

    def backbone(middle, normed, mixed, bias):
        edges = Edges(place, middle, rows_out, columns_out, rows_in, columns_in, corner_in, e_send, e_recv)
        core = place["core"]
        label_mask(label, place, bias)
        reduced(1, 1)()
        tiles.finish()
        ready = both(gathered(0, 5), reduced(1, 0))
        hooks = {1: gathered(0, 6), 2: gathered(1, 3), 3: gathered(1, 4)}
        first_sublayer(core, x, gains[0:1, :], w, normed, mixed, middle, ready, hooks)
        edges.start()
        gathered(1, 5)()
        reduced(2, 0, 1)()
        edges.finish()
        reduced(2, 2)()
        hooks = {1: both(gathered(1, 6), reduced(3, 0, 1)), 2: reduced(3, 2)}
        second_sublayer(core, middle, gains[1:2, :], w, normed, mixed, bias, out, hooks)
        leave.start()
        reduced(4, 0, 1, 2)()
        edges.drain()

    pl.run_scoped(
        backbone,
        pltpu.VMEM((10, LATENT, 24, D), F32),
        pltpu.VMEM((384, D), BF16),
        pltpu.VMEM((384, D), BF16),
        pltpu.VMEM((4, 96, 96), F32),
    )
    finish_gradients(factor, [part.result() for part in sums], lq, grad_key, grad_value, grad_out)
    leave.wait()
    tiles.drain()
    for part in layers[0] + layers[1] + sums:
        part.drain()


def whole(factor, tokens, grads, kw, vw, ro, lq, gains, qkv, ow, label):
    vmem, far = pl.BlockSpec(memory_space=pltpu.VMEM), pl.BlockSpec(memory_space=pl.ANY)
    landings = []
    for order, width in zip(REDUCE_ORDERS, WIDTHS):
        landings += landing_shapes(order, width)
    dma = pltpu.SemaphoreType.DMA
    return pl.pallas_call(
        functools.partial(kernel, factor),
        out_shape=[jax.ShapeDtypeStruct((8, LATENT, 16, D), BF16)] + [jax.ShapeDtypeStruct((8, D), F32)] * 3,
        in_specs=[far] * 5 + [vmem, vmem, far, far, vmem],
        out_specs=[far] + [vmem] * 3,
        scratch_shapes=[
            pltpu.VMEM((16, 2, 2, 4, 2, 4, 32, 128), BF16),
            pltpu.VMEM((2, LATENT, 64, D), BF16),
            pltpu.VMEM((8, LATENT, 16, D), BF16),
            pltpu.VMEM((2, 48, D), BF16),
            pltpu.VMEM((96, D), BF16),
            pltpu.VMEM((2, 48, D), BF16),
            pltpu.VMEM((96, D), BF16),
            pltpu.VMEM((32, D), BF16),
        ]
        + [pltpu.VMEM((2, 4, 2, 4, 2, 16, width), BF16) for width in WIDTHS]
        + landings
        + [dma((6, 18)), dma((6, 18)), dma((3, 10)), dma((3, 10))]
        + [dma((3,)), dma((3,)), dma((3,)), dma((3,)), dma((15,)), pltpu.VMEM((8, LATENT, 16, D), BF16)],
        compiler_params=pltpu.CompilerParams(collective_id=0, has_side_effects=True, vmem_limit_bytes=63 * MIB),
    )(tokens, grads, kw, vw, ro, lq, gains, qkv, ow, label)


def hand_over_kernel(*refs):
    count = len(refs) // 2
    for i in range(count):
        refs[count + i][...] = refs[i][...]


def hand_over(results):
    return pl.pallas_call(
        hand_over_kernel,
        out_shape=[jax.ShapeDtypeStruct(r.shape, r.dtype) for r in results],
        in_specs=[pl.BlockSpec(memory_space=pltpu.VMEM)] * len(results),
        out_specs=[pl.BlockSpec(memory_space=pltpu.VMEM)] * len(results),
    )(*results)


def local(
    level_tokens,
    latent_query,
    key_weight,
    value_weight,
    resample_out,
    norm_gain,
    qkv_weight,
    out_weight,
    window_label,
    grad_latents,
):
    factor = (2 * 64 * lax.axis_size("lat") * lax.axis_size("lon")) ** (-0.5)
    results = whole(
        factor,
        level_tokens.swapaxes(1, 2),
        grad_latents.swapaxes(1, 2),
        key_weight,
        value_weight,
        resample_out,
        latent_query,
        norm_gain,
        qkv_weight.swapaxes(1, 2),
        out_weight,
        window_label,
    )
    out, grad_key, grad_value, grad_out = hand_over(results)
    return (out.swapaxes(1, 2), grad_key, grad_value, grad_out)


def solution(mesh):
    in_specs = (
        P(("lat", "lon"), None, None, None),
        P(),
        P(),
        P(),
        P(),
        P(),
        P(None, "lat", None, "lon"),
        P(None, "lat", "lon"),
        P("lat", "lon"),
        P(("lat", "lon"), None, None, None),
    )
    out_specs = (
        P("lat", "lon", None, None),
        P(("lat", "lon"), None),
        P(("lat", "lon"), None),
        P(("lat", "lon"), None),
    )
    return jax.shard_map(local, mesh=mesh, in_specs=in_specs, out_specs=out_specs, check_vma=False)
```
